32 devices in a mesh: dp: 2 (over core), ctx: 4 (over z), tp: 4 (over y, x).
Axes of the slice: x: 2, y: 2, z: 4, core: 2. Of those that a mesh axis runs over, the one named last changes fastest.
Arguments:
- query: bfloat16 [2048, 32, 128], P(('dp', 'ctx'), 'tp'), parts along dimension 0, may hold values from -30 to 30
- keys: bfloat16 [2048, 4, 128], P(('dp', 'ctx'), 'tp'), parts along dimension 0, may hold values from -6 to 6
- values: bfloat16 [2048, 4, 128], P(('dp', 'ctx'), 'tp'), parts along dimension 0, may hold values from -6 to 6
- output_gradient: bfloat16 [2048, 32, 128], P(('dp', 'ctx'), 'tp'), parts along dimension 0, may hold values from -6 to 6
- doc_lengths: int32 [16], P('dp'), parts along dimension 0, may hold values from 1 to 512, 1024 in all
- block_owner: int32 [8, 4], P('dp'), parts along dimension 0, may hold values from 0 to 3, each once within a row
Outputs:
- attended: bfloat16 [2048, 32, 128], P(('dp', 'ctx'), 'tp'), parts along dimension 0
- query_grad: bfloat16 [2048, 32, 128], P(('dp', 'ctx'), 'tp'), parts along dimension 0
- key_grad: bfloat16 [2048, 4, 128], P(('dp', 'ctx'), 'tp'), parts along dimension 0
- value_grad: bfloat16 [2048, 4, 128], P(('dp', 'ctx'), 'tp'), parts along dimension 0
The draws below stay inside these ranges and needn't reach their ends.
There are 2 independent parts, one for each index of `dp`. The reference program is written for one: setup_inputs(seed, part) draws one part's arguments, and reference() takes and returns one part's arrays. A program takes and returns all parts, laid end to end along the dimension named above; each array names one. Nothing has to cross between parts.
Inputs may be any that keep to these rules, and one draw needn't show every extreme that they name: `block_owner`: each row lists the owners of one loader shard's 4 blocks in order and names every owner once. `doc_lengths`: the lengths sum to 1024.
All inputs are finite; a program needn't handle non-finite values.
Results may differ from the reference program's by a relative error of at most 0.039.
Values may be sent and summed in bfloat16 or wider, within the bound.
No kernel may reach another device: no remote copies, remote signals or barrier semaphores. Data moves between devices by JAX's collectives and lax.ppermute only.
A program may use at most 64 MiB of HBM per device.

```python
import math
import jax
import jax.numpy as jnp
import numpy as np
from jax import lax

QUERY_HEADS = 32
KEY_VALUE_HEADS = 4
HEAD_SIZE = 128
TOKENS_PER_OWNER = 256
NDOCS = 8
PACKED_TOKENS = 1024
N_CTX = 4


def draw_query(key, part):
    drawn_values = jnp.clip(jax.random.normal(jax.random.fold_in(key, 32), (PACKED_TOKENS, QUERY_HEADS, HEAD_SIZE), jnp.float32), -6.0, 6.0)
    return drawn_values.astype(jnp.bfloat16)


def draw_keys(key, part):
    drawn_values = jnp.clip(jax.random.normal(jax.random.fold_in(key, 42), (PACKED_TOKENS, KEY_VALUE_HEADS, HEAD_SIZE), jnp.float32), -6.0, 6.0)
    return drawn_values.astype(jnp.bfloat16)


def shard_levels(stream_key, shape, cuts, smallest, high):
    gain, own = 1.0, jax.random.fold_in(stream_key, 6)
    for dim, parts in cuts:
        steps = jnp.exp(jax.random.uniform(jax.random.fold_in(own, dim), (parts,), jnp.float32, smallest / len(cuts), high / len(cuts)))
        gain = gain * jnp.repeat(steps, shape[dim] // parts).reshape([-1 if axis == dim else 1 for axis in range(len(shape))])
    return gain


def length_profile(number_of, total, reach, slope):
    portions = [(1 << 20) // math.isqrt(rank ** slope) + 1 for rank in range(2, number_of + 1)]
    rest, given = total - reach - (number_of - 1), [1] * (number_of - 1)
    while rest > 0:
        movable = [i for i in range(number_of - 1) if given[i] < reach]
        pool, remaining = sum([portions[i] for i in movable]), rest
        for i in movable:
            extra = min(reach - given[i], max(1, remaining * portions[i] // pool), rest)
            given[i] = given[i] + extra
            rest = rest - extra
    return np.array([reach] + given)


def uneven(rng, number_of, total, limit, skew):
    if number_of == 2:
        one = jax.random.randint(rng, (), max(1, total - limit), min(limit, total - 1) + 1)
        return jnp.stack([one, total - one])
    tallies = jnp.asarray(length_profile(number_of, total, limit, skew), jnp.int32)
    pairs = (number_of - 1) // 2
    giver, taker = tallies[1:1 + 2 * pairs:2], tallies[2:2 + 2 * pairs:2]
    room = jnp.minimum(giver - 1, limit - taker)
    passed = jax.random.randint(jax.random.fold_in(rng, 1), (pairs,), 0, 1 << 20) % (room + 1)
    tallies = tallies.at[1:1 + 2 * pairs:2].set(giver - passed).at[2:2 + 2 * pairs:2].set(taker + passed)
    return tallies[jax.random.permutation(jax.random.fold_in(rng, 2), number_of)]


def gaussian(own_key, shape, scale, reach, cuts=(), kind=jnp.bfloat16):
    values = scale * jax.random.normal(own_key, shape, jnp.float32)
    if cuts:
        values = values * shard_levels(own_key, shape, cuts, -0.22, 0.18)
    return jnp.clip(values, -reach, reach).astype(kind)


def setup_inputs(seed: int = 0, part: int = 0) -> dict:
    arg_keys = jax.random.split(jax.random.key(seed), 7)
    own_keys = jax.random.split(jax.random.fold_in(arg_keys[6], part), 7)
    query = draw_query(jax.random.fold_in(jax.random.fold_in(arg_keys[6], part), 71), part)
    keys = draw_keys(jax.random.fold_in(jax.random.fold_in(arg_keys[6], part), 71), part)
    values = gaussian(own_keys[2], (PACKED_TOKENS, KEY_VALUE_HEADS, HEAD_SIZE), 1.0, 6.0, ((0, 4), (1, 4)))
    output_gradient = gaussian(own_keys[3], (PACKED_TOKENS, QUERY_HEADS, HEAD_SIZE), 1.0, 6.0, ((0, 4), (1, 4)))
    doc_lengths = uneven(own_keys[4], NDOCS, PACKED_TOKENS, PACKED_TOKENS // 2, 2).astype(jnp.int32)
    block_owner = jax.vmap(lambda own: jax.random.permutation(own, N_CTX))(jax.random.split(own_keys[5], N_CTX)).reshape((N_CTX, N_CTX)).astype(jnp.int32)
    return {"query": query, "keys": keys, "values": values, "output_gradient": output_gradient, "doc_lengths": doc_lengths, "block_owner": block_owner}


def document_index(token_positions, doc_lengths):
    doc_ends = jnp.cumsum(doc_lengths).astype(jnp.int32)
    return jnp.sum((doc_ends[None, :] <= token_positions[:, None]).astype(jnp.int32), axis=1)


def owner_positions(block_owner, owner_id, local_rows):
    cycle_size = block_owner.shape[0]
    block_rows = local_rows // cycle_size
    slot_ids = jnp.arange(cycle_size, dtype=jnp.int32)
    matches = (block_owner == owner_id).astype(jnp.int32)
    slot_of = jnp.sum(matches * slot_ids[None, :], axis=1)
    starts = slot_ids * local_rows + slot_of * block_rows
    return (starts[:, None] + jnp.arange(block_rows, dtype=jnp.int32)[None, :]).reshape(-1)


def rounded(source):
    narrow = source.astype(jnp.bfloat16)
    narrow = lax.optimization_barrier(narrow)
    return narrow.astype(jnp.float32)


def reference(query, keys, values, output_gradient, doc_lengths, block_owner):
    heads_per_group = QUERY_HEADS // KEY_VALUE_HEADS
    softmax_scale = HEAD_SIZE ** -0.5
    owner_ids = jnp.arange(N_CTX, dtype=jnp.int32)
    token_positions = jax.vmap(lambda owner_id: owner_positions(block_owner, owner_id, TOKENS_PER_OWNER))(owner_ids).reshape(-1)
    documents = document_index(token_positions, doc_lengths)
    query_rows_all = jnp.take(query, token_positions, axis=0).astype(jnp.float32).reshape(PACKED_TOKENS, KEY_VALUE_HEADS, heads_per_group, HEAD_SIZE)
    key_rows = jnp.take(keys, token_positions, axis=0).astype(jnp.float32)
    value_rows = jnp.take(values, token_positions, axis=0).astype(jnp.float32)
    output_gradients = jnp.take(output_gradient, token_positions, axis=0).astype(jnp.float32).reshape(PACKED_TOKENS, KEY_VALUE_HEADS, heads_per_group, HEAD_SIZE)

    def visible(query_pos, query_doc):
        allowed = (query_doc[:, None] == documents[None, :]) & (token_positions[None, :] <= query_pos[:, None])
        return allowed[:, None, None, :]

    query_block_list = query_rows_all.reshape(N_CTX, TOKENS_PER_OWNER, KEY_VALUE_HEADS, heads_per_group, HEAD_SIZE)
    gradient_blocks = output_gradients.reshape(N_CTX, TOKENS_PER_OWNER, KEY_VALUE_HEADS, heads_per_group, HEAD_SIZE)
    pos_blocks = token_positions.reshape(N_CTX, TOKENS_PER_OWNER)
    doc_blocks = documents.reshape(N_CTX, TOKENS_PER_OWNER)

    def forward_block(inputs):
        q_block, query_pos, query_doc = inputs
        allowed = visible(query_pos, query_doc)
        scores = jnp.einsum("tgrd,ugd->tgru", q_block, key_rows) * softmax_scale
        scores = jnp.where(allowed, scores, -jnp.inf)
        row_max = jnp.max(scores, axis=-1)
        weights = jnp.where(allowed, jnp.exp(scores - row_max[..., None]), 0.0)
        row_sum = jnp.sum(weights, axis=-1)
        mixed_rows = jnp.einsum("tgru,ugd->tgrd", rounded(weights), value_rows)
        attended = (mixed_rows / row_sum[..., None]).astype(jnp.bfloat16)
        return attended, row_max + jnp.log(row_sum)

    attended, log_sums = lax.map(forward_block, (query_block_list, pos_blocks, doc_blocks))
    attended_token_rows = attended.reshape(PACKED_TOKENS, KEY_VALUE_HEADS, heads_per_group, HEAD_SIZE)
    row_delta_sum = jnp.sum(output_gradients * attended_token_rows.astype(jnp.float32), axis=-1)

    def backward_block(accums, inputs):
        key_acc, value_acc = accums
        q_block, g_block, query_pos, query_doc, lse_block, delta_block = inputs
        allowed = visible(query_pos, query_doc)
        scores = jnp.einsum("tgrd,ugd->tgru", q_block, key_rows) * softmax_scale
        probs = jnp.where(allowed, jnp.exp(scores - lse_block[..., None]), 0.0)
        value_acc = value_acc + jnp.einsum("tgru,tgrd->ugd", rounded(probs), g_block)
        products = jnp.einsum("tgrd,ugd->tgru", g_block, value_rows)
        slopes = rounded(probs * (products - delta_block[..., None]))
        query_part = (jnp.einsum("tgru,ugd->tgrd", slopes, key_rows) * softmax_scale).astype(jnp.bfloat16)
        key_acc = key_acc + jnp.einsum("tgru,tgrd->ugd", slopes, q_block) * softmax_scale
        return (key_acc, value_acc), query_part

    empty_gradient_blocks = jnp.zeros((PACKED_TOKENS, KEY_VALUE_HEADS, HEAD_SIZE), jnp.float32)
    delta_block_list = row_delta_sum.reshape(N_CTX, TOKENS_PER_OWNER, KEY_VALUE_HEADS, heads_per_group)
    (key_acc, value_acc), query_grads = lax.scan(backward_block, (empty_gradient_blocks, empty_gradient_blocks), (query_block_list, gradient_blocks, pos_blocks, doc_blocks, log_sums, delta_block_list))
    return (attended_token_rows.reshape(PACKED_TOKENS, QUERY_HEADS, HEAD_SIZE), query_grads.reshape(PACKED_TOKENS, QUERY_HEADS, HEAD_SIZE), key_acc.astype(jnp.bfloat16), value_acc.astype(jnp.bfloat16))
```

```python
import functools
import jax
import jax.numpy as jnp
from jax import lax
from jax.experimental import pallas as pl
from jax.experimental.pallas import tpu as pltpu
from jax.sharding import PartitionSpec as P

MASKED = -1e30
LOG2_E = 1.4426950408889634
VMEM_LIMIT = 48 * 1024 * 1024


def dot(a, b, contract):
    return lax.dot_general(a, b, ((contract[0], contract[1]), ((), ())), preferred_element_type=jnp.float32)


def attend_block(first_row, ends, q, g, k, v, reach, heads, scale):
    cols = q.shape[0]
    key_rows = k.shape[0]
    token = lax.broadcasted_iota(jnp.int32, (1, cols), 1) // heads
    query_pos = first_row + token
    doc_start = jnp.zeros((1, cols), jnp.int32)
    for end in ends:
        doc_start = jnp.maximum(doc_start, jnp.where(end <= query_pos, end, 0))
    low = doc_start - (first_row - reach)
    raw = dot(k, q, ((1,), (1,)))
    index = lax.broadcasted_iota(jnp.int32, (key_rows, cols), 0)
    allowed = index >= low
    allowed_late = jnp.logical_and(allowed[reach:], index[reach:] - reach <= token)
    raw = jnp.concatenate(
        [jnp.where(allowed[:reach], raw[:reach], MASKED), jnp.where(allowed_late, raw[reach:], MASKED)], axis=0
    )
    row_max = jnp.max(raw, axis=0, keepdims=True)
    weights = jnp.exp2((raw - row_max) * (scale * LOG2_E))
    inverse = 1.0 / jnp.sum(weights, axis=0, keepdims=True)
    attended_t = (dot(v, weights.astype(jnp.bfloat16), ((0,), (0,))) * inverse).astype(jnp.bfloat16)
    attended = attended_t.T
    g_t = g.T.astype(jnp.float32)
    delta = jnp.sum(g_t * attended_t.astype(jnp.float32), axis=0, keepdims=True)
    probs = weights * inverse
    products = dot(v, g, ((1,), (1,)))
    slopes = (probs * (products - delta)).astype(jnp.bfloat16)
    value_part = dot(probs.astype(jnp.bfloat16), g, ((1,), (0,)))
    key_part = dot(slopes, q, ((1,), (0,)))
    query_grad = (dot(k, slopes, ((0,), (0,))) * scale).astype(jnp.bfloat16).T
    return attended, query_grad, key_part, value_part


def work_kernel(layout, shifts, meta, *refs):
    n, reach_ranges, rows, heads, scale, ndocs, carried, final = layout
    block = rows // n
    reach = reach_ranges * rows
    q_ref, g_ref = refs[:2]
    refs = refs[2:]
    k_refs, v_refs = refs[: reach_ranges + 1], refs[reach_ranges + 1 : 2 * reach_ranges + 2]
    refs = refs[2 * reach_ranges + 2 :]
    if carried:
        acc_in, refs = refs[0], refs[1:]
    pay_refs, refs = refs[: len(shifts)], refs[len(shifts) :]
    if final:
        grad_refs, refs = refs[:n], refs[n:]
        k_win, v_win, acc = refs
    else:
        acc, k_win, v_win = refs
    step = pl.program_id(0)

    @pl.when(step == 0)
    def _():
        for i in range(reach_ranges + 1):
            k_win[pl.ds((reach_ranges - i) * rows, rows), :] = k_refs[i][...]
            v_win[pl.ds((reach_ranges - i) * rows, rows), :] = v_refs[i][...]
        acc[...] = acc_in[...] if carried else jnp.zeros_like(acc)

    own = meta[0]
    ends = [meta[1 + i] for i in range(ndocs)]
    table = 1 + ndocs
    shift = step + 1 if len(shifts) > 1 else shifts[0]
    if len(shifts) > 1:
        shift = jnp.int32(shifts[0])
        for i, value in enumerate(shifts):
            shift = jnp.where(step == i, value, shift)
    slot = meta[table + shift]
    start = pl.multiple_of(slot * block, block)
    keys_here = pl.ds(start, reach + block)
    width = q_ref.shape[1]
    attended, query_grad, key_part, value_part = attend_block(
        own * rows + slot * block, ends, q_ref[...], g_ref[...], k_win[keys_here, :], v_win[keys_here, :],
        reach, heads, scale,
    )
    acc[keys_here, :width] = acc[keys_here, :width] + key_part
    acc[keys_here, width:] = acc[keys_here, width:] + value_part
    for i in range(len(shifts)):

        @pl.when(step == i)
        def _():
            pay_refs[i][0] = attended
            pay_refs[i][1] = query_grad

    if final:

        @pl.when(step == len(shifts) - 1)
        def _():
            for to in range(n):
                for back in range(reach_ranges + 1):
                    at = meta[table + back * n + to] * block + (reach_ranges - back) * rows
                    part = acc[pl.ds(pl.multiple_of(at, block), block), :]
                    grad_refs[to][back, :, :width] = (part[:, :width] * scale).astype(grad_refs[to].dtype)
                    grad_refs[to][back, :, width:] = part[:, width:].astype(grad_refs[to].dtype)


def work(layout, shifts, meta, q, g, k_list, v_list, acc):
    n, reach_ranges, rows, heads, scale, ndocs, carried, final = layout
    width = q.shape[1]
    block = rows // n
    cols = block * heads
    table = 1 + ndocs
    window = (reach_ranges + 1) * rows

    def of_shift(step, meta):
        shift = jnp.int32(shifts[0])
        for i, value in enumerate(shifts):
            shift = jnp.where(step == i, value, shift)
        return (meta[table + shift], 0)

    def whole(shape):
        return pl.BlockSpec(shape, lambda step, meta: (0,) * len(shape))

    in_specs = [pl.BlockSpec((cols, width), of_shift)] * 2
    in_specs += [whole((rows, width))] * (2 * reach_ranges + 2)
    operands = [q, g, *k_list, *v_list]
    if carried:
        in_specs.append(whole((window, 2 * width)))
        operands.append(acc)
    out_shape = [jax.ShapeDtypeStruct((2, cols, width), jnp.bfloat16)] * len(shifts)
    scratch = [pltpu.VMEM((window, width), jnp.bfloat16)] * 2
    if final:
        grad_shape = (reach_ranges + 1, block, 2 * width)
        out_shape += [jax.ShapeDtypeStruct(grad_shape, jnp.bfloat16 if i else jnp.float32) for i in range(n)]
        scratch.append(pltpu.VMEM((window, 2 * width), jnp.float32))
    else:
        out_shape.append(jax.ShapeDtypeStruct((window, 2 * width), jnp.float32))
    return pl.pallas_call(
        functools.partial(work_kernel, layout, shifts),
        out_shape=out_shape,
        grid_spec=pltpu.PrefetchScalarGridSpec(
            num_scalar_prefetch=1,
            grid=(len(shifts),),
            in_specs=in_specs,
            out_specs=[whole(s.shape) for s in out_shape],
            scratch_shapes=scratch,
        ),
        compiler_params=pltpu.CompilerParams(vmem_limit_bytes=VMEM_LIMIT),
        name="attend_" + ("last" if final else "first"),
    )(meta, *operands)


def place_kernel(n, reach_ranges, meta, *refs):
    own = meta[0]
    pay_refs, grad_refs = refs[:n], refs[n : 2 * n]
    attended, query_grad, key_grad, value_grad, acc = refs[2 * n :]
    cols = pay_refs[0].shape[1]
    block = grad_refs[0].shape[1]
    width = key_grad.shape[1]
    for shift in range(n):
        source = lax.rem(own - shift + n, n)
        to = pl.ds(pl.multiple_of(source * cols, cols), cols)
        attended[to, :] = pay_refs[shift][0]
        query_grad[to, :] = pay_refs[shift][1]
    acc[...] = jnp.zeros_like(acc)
    for shift in range(n):
        for back in range(reach_ranges + 1):
            source = lax.rem(own - shift - back + 2 * n, n)
            to = pl.ds(pl.multiple_of(source * block, block), block)
            acc[to, :] = acc[to, :] + grad_refs[shift][back].astype(jnp.float32)
    key_grad[...] = acc[:, :width].astype(jnp.bfloat16)
    value_grad[...] = acc[:, width:].astype(jnp.bfloat16)


def place(n, reach_ranges, rows, heads, width, meta, payloads, grads):
    vmem = pl.BlockSpec(memory_space=pltpu.VMEM)
    big = jax.ShapeDtypeStruct((rows * heads, width), jnp.bfloat16)
    small = jax.ShapeDtypeStruct((rows, width), jnp.bfloat16)
    return pl.pallas_call(
        functools.partial(place_kernel, n, reach_ranges),
        out_shape=[big, big, small, small],
        in_specs=[pl.BlockSpec(memory_space=pltpu.SMEM)] + [vmem] * (2 * n),
        out_specs=[vmem] * 4,
        scratch_shapes=[pltpu.VMEM((rows, 2 * width), jnp.float32)],
        compiler_params=pltpu.CompilerParams(vmem_limit_bytes=VMEM_LIMIT),
        name="place",
    )(meta, *payloads, *grads)


def on_device(query, keys, values, output_gradient, doc_lengths, block_owner):
    n = lax.axis_size("ctx")
    own = lax.axis_index("ctx")
    rows, heads, width = query.shape
    scale = width ** (-0.5)
    ndocs = doc_lengths.shape[0]
    reach_ranges = n // 2

    def passed(array, by):
        return lax.ppermute(array, "ctx", [(i, (i + by) % n) for i in range(n)])

    k = keys.reshape(rows, width)
    v = values.reshape(rows, width)
    k_list = [k] + [passed(k, i) for i in range(1, reach_ranges + 1)]
    v_list = [v] + [passed(v, i) for i in range(1, reach_ranges + 1)]
    q = query.reshape(rows * heads, width)
    g = output_gradient.reshape(rows * heads, width)

    ranges = (own - jnp.arange(reach_ranges + 1)) % n
    targets = (own + jnp.arange(n)) % n
    slots = jnp.arange(n, dtype=jnp.int32)
    match = block_owner[ranges][:, None, :] == targets[None, :, None]
    table = jnp.sum(jnp.where(match, slots, 0), axis=2)
    meta = jnp.concatenate(
        [own.reshape(1).astype(jnp.int32), jnp.cumsum(doc_lengths).astype(jnp.int32), table.reshape(-1)]
    )

    first = [n // 2]
    rest = [i for i in range(1, n) if i != n // 2] + [0]
    layout = (n, reach_ranges, rows, heads, scale, ndocs)
    out = work(layout + (False, False), first, meta, q, g, k_list, v_list, None)
    payloads = {first[0]: passed(out[0], first[0])}
    out = work(layout + (True, True), rest, meta, q, g, k_list, v_list, out[1])
    for i, shift in enumerate(rest):
        payloads[shift] = passed(out[i], shift) if shift else out[i]
    grads = [passed(grad, i) if i else grad for i, grad in enumerate(out[len(rest) :])]
    attended, query_grad, key_grad, value_grad = place(
        n, reach_ranges, rows, heads, width, meta, [payloads[i] for i in range(n)], grads
    )
    return (
        attended.reshape(rows, heads, width),
        query_grad.reshape(rows, heads, width),
        key_grad.reshape(rows, 1, width),
        value_grad.reshape(rows, 1, width),
    )


def solution(mesh):
    rows = P(("dp", "ctx"), "tp", None)
    return jax.shard_map(
        on_device,
        mesh=mesh,
        in_specs=(rows, rows, rows, rows, P("dp"), P("dp", None)),
        out_specs=(rows, rows, rows, rows),
        check_vma=False,
    )
```

```python
import functools
import jax
import jax.numpy as jnp
from jax import lax
from jax.experimental import pallas as pl
from jax.experimental.pallas import tpu as pltpu
from jax.sharding import PartitionSpec as P

MASKED = -1e30
LOG2_E = 1.4426950408889634
VMEM_LIMIT = 32 * 1024 * 1024
EARLY = False


def dot(a, b, contract):
    return lax.dot_general(a, b, ((contract[0], contract[1]), ((), ())), preferred_element_type=jnp.float32)


def attend_block(first_row, ends, q, g, k, v, reach, heads, scale):
    cols = q.shape[0]
    key_rows = k.shape[0]
    token = lax.broadcasted_iota(jnp.int32, (1, cols), 1) // heads
    query_pos = first_row + token
    doc_start = jnp.zeros((1, cols), jnp.int32)
    for end in ends:
        doc_start = jnp.maximum(doc_start, jnp.where(end <= query_pos, end, 0))
    low = doc_start - (first_row - reach)
    raw = dot(k, q, ((1,), (1,)))
    index = lax.broadcasted_iota(jnp.int32, (key_rows, cols), 0)
    allowed = index >= low
    allowed_late = jnp.logical_and(allowed[reach:], index[reach:] - reach <= token)
    raw = jnp.concatenate(
        [jnp.where(allowed[:reach], raw[:reach], MASKED), jnp.where(allowed_late, raw[reach:], MASKED)], axis=0
    )
    row_max = jnp.max(raw, axis=0, keepdims=True)
    weights = jnp.exp2((raw - row_max) * (scale * LOG2_E))
    inverse = 1.0 / jnp.sum(weights, axis=0, keepdims=True)
    attended_t = (dot(v, weights.astype(jnp.bfloat16), ((0,), (0,))) * inverse).astype(jnp.bfloat16)
    attended = attended_t.T
    g_t = g.T.astype(jnp.float32)
    delta = jnp.sum(g_t * attended_t.astype(jnp.float32), axis=0, keepdims=True)
    probs = weights * inverse
    products = dot(v, g, ((1,), (1,)))
    slopes = (probs * (products - delta)).astype(jnp.bfloat16)
    value_part = dot(probs.astype(jnp.bfloat16), g, ((1,), (0,)))
    key_part = dot(slopes, q, ((1,), (0,))) * scale
    query_grad = (dot(k, slopes, ((0,), (0,))) * scale).astype(jnp.bfloat16).T
    return attended, query_grad, key_part, value_part


class Plan:
    def __init__(self, n, rows, heads, width, ndocs):
        self.n, self.rows, self.heads, self.width, self.ndocs = n, rows, heads, width, ndocs
        self.back = n // 2
        self.block = rows // n
        self.cols = self.block * heads
        self.reach = self.back * rows
        self.scale = width ** (-0.5)
        self.window_ranges = self.back + 3

    def ends(self, meta):
        return [meta[1 + i] for i in range(self.ndocs)]

    def slot(self, meta, loader, owner):
        return meta[1 + self.ndocs + loader * self.n + owner]

    def cost(self, blocks):
        return pl.CostEstimate(
            flops=14 * blocks * self.cols * (self.reach + self.block) * self.width * 8,
            bytes_accessed=blocks * self.cols * self.width * 16,
            transcendentals=blocks * self.cols * (self.reach + self.block),
        )


def fill_window(plan, refs, k_win, v_win):
    rows, width = plan.rows, plan.width
    k_win[pl.ds((plan.back + 1) * rows, rows), :] = refs[0][0]
    v_win[pl.ds((plan.back + 1) * rows, rows), :] = refs[0][1]
    for i in range(1, (len(refs) + 1) // 2):
        place = plan.back + 1 - i if i <= plan.back else plan.back + 2
        k_win[pl.ds(place * rows, rows), :] = refs[2 * i - 1][...]
        v_win[pl.ds(place * rows, rows), :] = refs[2 * i][...]
    if len(refs) > 2 * plan.back + 1:
        k_win[pl.ds(0, rows), :] = jnp.zeros((rows, width), k_win.dtype)
        v_win[pl.ds(0, rows), :] = jnp.zeros((rows, width), v_win.dtype)


def attend_at(plan, meta, loader, slot, q, g, k_win, v_win):
    start = (loader - meta[0] + 1) * plan.rows + slot * plan.block
    keys_here = pl.ds(pl.multiple_of(start, plan.block), plan.reach + plan.block)
    out = attend_block(
        loader * plan.rows + slot * plan.block, plan.ends(meta), q, g, k_win[keys_here, :], v_win[keys_here, :],
        plan.reach, plan.heads, plan.scale,
    )
    return keys_here, out


def pack_kernel(plan, meta, q_ref, g_ref, k_ref, v_ref, *refs):
    blocks, kv, sems, kv_sems = refs[: plan.n], refs[plan.n], refs[plan.n + 1], refs[plan.n + 2]
    own = meta[0]
    copies = [
        pltpu.make_async_copy(k_ref, kv.at[0], kv_sems.at[0]),
        pltpu.make_async_copy(v_ref, kv.at[1], kv_sems.at[1]),
    ]
    for shift, block in enumerate(blocks):
        slot = plan.slot(meta, own, lax.rem(own + shift, plan.n))
        at = pl.ds(pl.multiple_of(slot * plan.cols, plan.cols), plan.cols)
        copies.append(pltpu.make_async_copy(q_ref.at[at, :], block.at[0], sems.at[shift, 0]))
        copies.append(pltpu.make_async_copy(g_ref.at[at, :], block.at[1], sems.at[shift, 1]))
    for copy in copies:
        copy.start()
    for copy in copies:
        copy.wait()


def first_kernel(plan, shift, meta, qg, *refs):
    kv_refs, (pay_ref, grad_ref, k_win, v_win) = refs[:-4], refs[-4:]
    own = meta[0]
    slot = plan.slot(meta, own, lax.rem(own + shift, plan.n))
    fill_window(plan, kv_refs, k_win, v_win)
    _, (attended, query_grad, key_part, value_part) = attend_at(
        plan, meta, own, slot, qg[0], qg[1], k_win, v_win
    )
    pay_ref[0] = attended
    pay_ref[1] = query_grad
    grad_ref[:, : plan.width] = key_part
    grad_ref[:, plan.width :] = value_part


def last_kernel(plan, first_shift, items, meta, *refs):
    n, width, rows, block = plan.n, plan.width, plan.rows, plan.block
    qg_refs, refs = refs[: len(items)], refs[len(items) :]
    first_grad, refs = refs[0], refs[1:]
    kv_refs, refs = refs[: -(len(items) + 5)], refs[-(len(items) + 5) :]
    pay_refs, (send_ref, keep_ref, k_win, v_win, acc) = refs[: len(items)], refs[len(items) :]
    step = pl.program_id(0)
    own = meta[0]

    def valid(item):
        if item == "ahead":
            return own < n - 1
        if item == "behind":
            return jnp.logical_and(own >= 1, own <= plan.back)
        if EARLY and item == 1:
            return own >= plan.back
        if EARLY and item == n - 1:
            return own == 0
        return own >= 0

    @pl.when(step == 0)
    def _():
        fill_window(plan, kv_refs, k_win, v_win)
        acc[...] = jnp.zeros_like(acc)
        slot = plan.slot(meta, own, lax.rem(own + first_shift, n))
        keys_here = pl.ds(pl.multiple_of(rows + slot * block, block), plan.reach + block)
        acc[keys_here, :] = first_grad[...]

    for i, item in enumerate(items):

        @pl.when(jnp.logical_and(step == i, valid(item)))
        def _():
            loader = own + {"ahead": 1, "behind": -1}.get(item, 0)
            owner = own if item in ("ahead", "behind") else lax.rem(own + item, n)
            slot = plan.slot(meta, loader, owner)
            qg = qg_refs[i]
            keys_here, (attended, query_grad, key_part, value_part) = attend_at(
                plan, meta, loader, slot, qg[0], qg[1], k_win, v_win
            )
            acc[keys_here, :width] = acc[keys_here, :width] + key_part
            acc[keys_here, width:] = acc[keys_here, width:] + value_part
            pay_refs[i][0] = attended
            pay_refs[i][1] = query_grad

    @pl.when(step == len(items) - 1)
    def _():
        def of_range(key_range, carry):
            at = (lax.rem(key_range - own + plan.back + n, n) + 1) * rows
            for apart in range(n):
                slot = plan.slot(meta, key_range, own ^ apart)
                part = acc[pl.ds(pl.multiple_of(at + slot * block, block), block), :]
                to = keep_ref if apart % 2 == 0 else send_ref
                to[apart // 2, key_range] = part.astype(to.dtype)
            return carry

        lax.fori_loop(0, n, of_range, 0)


def spec_of(space):
    return pl.BlockSpec(memory_space=space)


def kernel_call(body, name, operands, spaces, out_shape, scratch, **more):
    return pl.pallas_call(
        body,
        out_shape=out_shape,
        in_specs=[spec_of(space) for space in spaces],
        compiler_params=pltpu.CompilerParams(vmem_limit_bytes=VMEM_LIMIT),
        scratch_shapes=scratch,
        name=name,
        **more,
    )(*operands)


def pack(plan, meta, q, g, k, v):
    out_shape = [jax.ShapeDtypeStruct((2, plan.cols, plan.width), jnp.bfloat16)] * plan.n
    out_shape.append(jax.ShapeDtypeStruct((2, plan.rows, plan.width), jnp.bfloat16))
    return kernel_call(
        functools.partial(pack_kernel, plan), "pack", (meta, q, g, k, v), [pltpu.SMEM] + [pl.ANY] * 4, out_shape,
        [pltpu.SemaphoreType.DMA((plan.n, 2)), pltpu.SemaphoreType.DMA((2,))],
        out_specs=[spec_of(pltpu.VMEM)] * len(out_shape),
    )


def attend_first(plan, shift, meta, qg, kv_list):
    window = pltpu.VMEM((plan.window_ranges * plan.rows, plan.width), jnp.bfloat16)
    out_shape = [
        jax.ShapeDtypeStruct((2, plan.cols, plan.width), jnp.bfloat16),
        jax.ShapeDtypeStruct((plan.reach + plan.block, 2 * plan.width), jnp.float32),
    ]
    operands = (meta, qg, *kv_list)
    return kernel_call(
        functools.partial(first_kernel, plan, shift), "attend_first", operands,
        [pltpu.SMEM] + [pltpu.VMEM] * (len(operands) - 1), out_shape, [window, window],
        out_specs=[spec_of(pltpu.VMEM)] * 2, cost_estimate=plan.cost(1),
    )


def attend_last(plan, first_shift, items, meta, qg_list, first_grad, kv_list):
    n = plan.n
    window = pltpu.VMEM((plan.window_ranges * plan.rows, plan.width), jnp.bfloat16)
    grads = (n // 2, n, plan.block, 2 * plan.width)
    out_shape = [jax.ShapeDtypeStruct((2, plan.cols, plan.width), jnp.bfloat16)] * len(items)
    out_shape += [jax.ShapeDtypeStruct(grads, jnp.bfloat16), jax.ShapeDtypeStruct(grads, jnp.float32)]
    operands = (meta, *qg_list, first_grad, *kv_list)
    return kernel_call(
        functools.partial(last_kernel, plan, first_shift, items), "attend_last", operands,
        [pltpu.SMEM] + [pltpu.VMEM] * (len(operands) - 1), out_shape,
        [window, window, pltpu.VMEM(((n + 1) * plan.rows, 2 * plan.width), jnp.float32)],
        out_specs=[spec_of(pltpu.VMEM)] * len(out_shape), cost_estimate=plan.cost(len(items)), grid=(len(items),),
    )


def place_kernel(plan, items, final, meta, *refs):
    n, cols, width, own = plan.n, plan.cols, plan.width, meta[0]
    pay_refs, refs = dict(zip(items, refs[: len(items)])), refs[len(items) :]
    if final:
        keep, arrived, _, _, attended, query_grad, key_grad, value_grad, sems = refs
    else:
        attended, query_grad, sems = refs

    def copies(i, item):
        if item == "ahead":
            source, here = own + 1, own < n - 1
        elif item == "behind":
            source, here = own - 1, jnp.logical_and(own >= 1, own <= plan.back)
        else:
            source = lax.rem(own - item + n, n)
            here = own >= 0
            if EARLY and item == 1:
                here = source >= plan.back
            if EARLY and item == n - 1:
                here = own == n - 1
        to = pl.ds(pl.multiple_of(source * cols, cols), cols)
        return here, [
            pltpu.make_async_copy(pay_refs[item].at[0], attended.at[to, :], sems.at[i, 0]),
            pltpu.make_async_copy(pay_refs[item].at[1], query_grad.at[to, :], sems.at[i, 1]),
        ]

    def each(act):
        for i, item in enumerate(items):
            here, pair = copies(i, item)

            @pl.when(here)
            def _():
                for copy in pair:
                    act(copy)

    each(lambda copy: copy.start())
    if final:
        total = keep[...] + arrived[...].astype(jnp.float32)
        key_grad[...] = total[:, :width].astype(jnp.bfloat16)
        value_grad[...] = total[:, width:].astype(jnp.bfloat16)
    each(lambda copy: copy.wait())


def place(plan, meta, payloads, grads=(), filled=()):
    items = tuple(payloads)
    big = jax.ShapeDtypeStruct((plan.rows * plan.heads, plan.width), jnp.bfloat16)
    small = jax.ShapeDtypeStruct((plan.rows, plan.width), jnp.bfloat16)
    final = len(filled) > 0
    at = 1 + len(items) + len(grads)
    return kernel_call(
        functools.partial(place_kernel, plan, items, final), "place_last" if final else "place_first",
        (meta, *payloads.values(), *grads, *filled),
        [pltpu.SMEM] + [pl.ANY] * len(items) + [pltpu.VMEM] * len(grads) + [pl.ANY] * len(filled),
        [big, big] + [small, small] * final, [pltpu.SemaphoreType.DMA((len(items), 2))],
        out_specs=[spec_of(pl.ANY)] * 2 + [spec_of(pltpu.VMEM)] * (2 * final),
        input_output_aliases={at: 0, at + 1: 1} if final else {},
        cost_estimate=plan.cost(len(items)),
    )


def on_device(query, keys, values, output_gradient, doc_lengths, block_owner):
    n = lax.axis_size("ctx")
    own = lax.axis_index("ctx")
    rows, heads, width = query.shape
    plan = Plan(n, rows, heads, width, doc_lengths.shape[0])

    def passed(array, by):
        return lax.ppermute(array, "ctx", [(i, (i + by) % n) for i in range(n)])

    k = keys.reshape(rows, width)
    v = values.reshape(rows, width)
    kv_list = []
    for i in range(1, plan.back + 1):
        kv_list += [passed(k, i), passed(v, i)]
    owners = jnp.arange(n, dtype=jnp.int32)
    match = block_owner[:, None, :] == owners[None, :, None]
    table = jnp.sum(jnp.where(match, owners, 0), axis=2)
    meta = jnp.concatenate(
        [own.reshape(1).astype(jnp.int32), jnp.cumsum(doc_lengths).astype(jnp.int32), table.reshape(-1)]
    )

    blocks = pack(plan, meta, query.reshape(rows * heads, width), output_gradient.reshape(rows * heads, width), k, v)
    kv_list = [blocks[n], *kv_list]
    first = n // 2
    items = tuple([i for i in range(1, n) if i != first] + [0])
    first_pay, first_grad = attend_first(plan, first, meta, blocks[first], kv_list)
    first_pay = passed(first_pay, first)
    out = attend_last(plan, first, items, meta, [blocks[i] for i in items], first_grad, kv_list)
    stay = {first: first_pay}
    late = {}
    for item, pay in zip(items, out):
        if item:
            late[item] = passed(pay, item)
        else:
            stay[item] = pay
    send, keep = out[len(items) :]
    bit = 1
    while True:
        arrived = lax.ppermute(send, "ctx", [(i, i ^ bit) for i in range(n)])
        bit *= 2
        if bit == n:
            break
        total = keep + arrived.astype(jnp.float32)
        send, keep = total[1::2].astype(jnp.bfloat16), total[0::2]
    grads = [keep.reshape(rows, 2 * width), arrived.reshape(rows, 2 * width)]
    attended, query_grad, key_grad, value_grad = place(plan, meta, late, grads, place(plan, meta, stay))
    return (
        attended.reshape(rows, heads, width),
        query_grad.reshape(rows, heads, width),
        key_grad.reshape(rows, 1, width),
        value_grad.reshape(rows, 1, width),
    )


def solution(mesh):
    rows = P(("dp", "ctx"), "tp", None)
    return jax.shard_map(
        on_device,
        mesh=mesh,
        in_specs=(rows, rows, rows, rows, P("dp"), P("dp", None)),
        out_specs=(rows, rows, rows, rows),
        check_vma=False,
    )
```

```python
import functools
import jax
import jax.numpy as jnp
from jax import lax
from jax.experimental import pallas as pl
from jax.experimental.pallas import tpu as pltpu
from jax.sharding import PartitionSpec as P

MASKED = -1e30
LOG2_E = 1.4426950408889634
VMEM_LIMIT = 32 * 1024 * 1024
EARLY = False


def dot(a, b, contract):
    return lax.dot_general(a, b, ((contract[0], contract[1]), ((), ())), preferred_element_type=jnp.float32)


def attend_block(first_row, ends, q, g, k, v, reach, heads, scale):
    cols = q.shape[0]
    key_rows = k.shape[0]
    token = lax.broadcasted_iota(jnp.int32, (1, cols), 1) // heads
    query_pos = first_row + token
    doc_start = jnp.zeros((1, cols), jnp.int32)
    for end in ends:
        doc_start = jnp.maximum(doc_start, jnp.where(end <= query_pos, end, 0))
    low = doc_start - (first_row - reach)
    raw = dot(k, q, ((1,), (1,)))
    index = lax.broadcasted_iota(jnp.int32, (key_rows, cols), 0)
    allowed = index >= low
    allowed_late = jnp.logical_and(allowed[reach:], index[reach:] - reach <= token)
    raw = jnp.concatenate(
        [jnp.where(allowed[:reach], raw[:reach], MASKED), jnp.where(allowed_late, raw[reach:], MASKED)], axis=0
    )
    row_max = jnp.max(raw, axis=0, keepdims=True)
    weights = jnp.exp2((raw - row_max) * (scale * LOG2_E))
    inverse = 1.0 / jnp.sum(weights, axis=0, keepdims=True)
    attended_t = (dot(v, weights.astype(jnp.bfloat16), ((0,), (0,))) * inverse).astype(jnp.bfloat16)
    attended = attended_t.T
    g_t = g.T.astype(jnp.float32)
    delta = jnp.sum(g_t * attended_t.astype(jnp.float32), axis=0, keepdims=True)
    probs = weights * inverse
    products = dot(v, g, ((1,), (1,)))
    slopes = (probs * (products - delta)).astype(jnp.bfloat16)
    value_part = dot(probs.astype(jnp.bfloat16), g, ((1,), (0,)))
    key_part = dot(slopes, q, ((1,), (0,))) * scale
    query_grad = (dot(k, slopes, ((0,), (0,))) * scale).astype(jnp.bfloat16).T
    return attended, query_grad, key_part, value_part


class Plan:
    def __init__(self, n, rows, heads, width, ndocs):
        self.n, self.rows, self.heads, self.width, self.ndocs = n, rows, heads, width, ndocs
        self.back = n // 2
        self.block = rows // n
        self.cols = self.block * heads
        self.reach = self.back * rows
        self.scale = width ** (-0.5)
        self.window_ranges = self.back + 3

    def ends(self, meta):
        return [meta[1 + i] for i in range(self.ndocs)]

    def slot(self, meta, loader, owner):
        return meta[1 + self.ndocs + loader * self.n + owner]

    def cost(self, blocks):
        return pl.CostEstimate(
            flops=14 * blocks * self.cols * (self.reach + self.block) * self.width * 8,
            bytes_accessed=blocks * self.cols * self.width * 16,
            transcendentals=blocks * self.cols * (self.reach + self.block),
        )


def fill_window(plan, refs, k_win, v_win):
    rows, width = plan.rows, plan.width
    k_win[pl.ds((plan.back + 1) * rows, rows), :] = refs[0][0]
    v_win[pl.ds((plan.back + 1) * rows, rows), :] = refs[0][1]
    for i in range(1, (len(refs) + 1) // 2):
        place = plan.back + 1 - i if i <= plan.back else plan.back + 2
        k_win[pl.ds(place * rows, rows), :] = refs[2 * i - 1][...]
        v_win[pl.ds(place * rows, rows), :] = refs[2 * i][...]
    if len(refs) > 2 * plan.back + 1:
        k_win[pl.ds(0, rows), :] = jnp.zeros((rows, width), k_win.dtype)
        v_win[pl.ds(0, rows), :] = jnp.zeros((rows, width), v_win.dtype)


def attend_at(plan, meta, loader, slot, q, g, k_win, v_win):
    start = (loader - meta[0] + 1) * plan.rows + slot * plan.block
    keys_here = pl.ds(pl.multiple_of(start, plan.block), plan.reach + plan.block)
    out = attend_block(
        loader * plan.rows + slot * plan.block, plan.ends(meta), q, g, k_win[keys_here, :], v_win[keys_here, :],
        plan.reach, plan.heads, plan.scale,
    )
    return keys_here, out


def pack_kernel(plan, meta, q_ref, g_ref, k_ref, v_ref, *refs):
    blocks, kv, sems, kv_sems = refs[: plan.n], refs[plan.n], refs[plan.n + 1], refs[plan.n + 2]
    own = meta[0]
    copies = [
        pltpu.make_async_copy(k_ref, kv.at[0], kv_sems.at[0]),
        pltpu.make_async_copy(v_ref, kv.at[1], kv_sems.at[1]),
    ]
    for shift, block in enumerate(blocks):
        slot = plan.slot(meta, own, lax.rem(own + shift, plan.n))
        at = pl.ds(pl.multiple_of(slot * plan.cols, plan.cols), plan.cols)
        copies.append(pltpu.make_async_copy(q_ref.at[at, :], block.at[0], sems.at[shift, 0]))
        copies.append(pltpu.make_async_copy(g_ref.at[at, :], block.at[1], sems.at[shift, 1]))
    for copy in copies:
        copy.start()
    for copy in copies:
        copy.wait()


def first_kernel(plan, shift, meta, qg, *refs):
    kv_refs, (pay_ref, grad_ref, k_win, v_win) = refs[:-4], refs[-4:]
    own = meta[0]
    slot = plan.slot(meta, own, lax.rem(own + shift, plan.n))
    fill_window(plan, kv_refs, k_win, v_win)
    _, (attended, query_grad, key_part, value_part) = attend_at(
        plan, meta, own, slot, qg[0], qg[1], k_win, v_win
    )
    pay_ref[0] = attended
    pay_ref[1] = query_grad
    grad_ref[:, : plan.width] = key_part
    grad_ref[:, plan.width :] = value_part


def last_kernel(plan, first_shift, items, meta, *refs):
    n, width, rows, block = plan.n, plan.width, plan.rows, plan.block
    qg_refs, refs = refs[: len(items)], refs[len(items) :]
    first_grad, refs = refs[0], refs[1:]
    kv_refs, refs = refs[: -(len(items) + 7)], refs[-(len(items) + 7) :]
    pay_refs, grad_refs, (k_win, v_win, acc) = refs[: len(items)], refs[len(items) : -3], refs[-3:]
    step = pl.program_id(0)
    own = meta[0]

    def valid(item):
        if item == "ahead":
            return own < n - 1
        if item == "behind":
            return jnp.logical_and(own >= 1, own <= plan.back)
        if EARLY and item == 1:
            return own >= plan.back
        if EARLY and item == n - 1:
            return own == 0
        return own >= 0

    @pl.when(step == 0)
    def _():
        fill_window(plan, kv_refs, k_win, v_win)
        acc[...] = jnp.zeros_like(acc)
        slot = plan.slot(meta, own, lax.rem(own + first_shift, n))
        keys_here = pl.ds(pl.multiple_of(rows + slot * block, block), plan.reach + block)
        acc[keys_here, :] = first_grad[...]

    for i, item in enumerate(items):

        @pl.when(jnp.logical_and(step == i, valid(item)))
        def _():
            loader = own + {"ahead": 1, "behind": -1}.get(item, 0)
            owner = own if item in ("ahead", "behind") else lax.rem(own + item, n)
            slot = plan.slot(meta, loader, owner)
            qg = qg_refs[i]
            keys_here, (attended, query_grad, key_part, value_part) = attend_at(
                plan, meta, loader, slot, qg[0], qg[1], k_win, v_win
            )
            acc[keys_here, :width] = acc[keys_here, :width] + key_part
            acc[keys_here, width:] = acc[keys_here, width:] + value_part
            pay_refs[i][0] = attended
            pay_refs[i][1] = query_grad

    @pl.when(step == len(items) - 1)
    def _():
        def of_range(key_range, carry):
            at = (lax.rem(key_range - own + plan.back + n, n) + 1) * rows
            for apart in range(n):
                slot = plan.slot(meta, key_range, own ^ apart)
                part = acc[pl.ds(pl.multiple_of(at + slot * block, block), block), :]
                to = grad_refs[apart % 4]
                to[apart // 4, key_range] = part.astype(to.dtype)
            return carry

        lax.fori_loop(0, n, of_range, 0)


def spec_of(space):
    return pl.BlockSpec(memory_space=space)


def kernel_call(body, name, operands, spaces, out_shape, scratch, **more):
    return pl.pallas_call(
        body,
        out_shape=out_shape,
        in_specs=[spec_of(space) for space in spaces],
        compiler_params=pltpu.CompilerParams(vmem_limit_bytes=VMEM_LIMIT),
        scratch_shapes=scratch,
        name=name,
        **more,
    )(*operands)


def pack(plan, meta, q, g, k, v):
    out_shape = [jax.ShapeDtypeStruct((2, plan.cols, plan.width), jnp.bfloat16)] * plan.n
    out_shape.append(jax.ShapeDtypeStruct((2, plan.rows, plan.width), jnp.bfloat16))
    return kernel_call(
        functools.partial(pack_kernel, plan), "pack", (meta, q, g, k, v), [pltpu.SMEM] + [pl.ANY] * 4, out_shape,
        [pltpu.SemaphoreType.DMA((plan.n, 2)), pltpu.SemaphoreType.DMA((2,))],
        out_specs=[spec_of(pltpu.VMEM)] * len(out_shape),
        cost_estimate=pl.CostEstimate(flops=0, bytes_accessed=1024, transcendentals=0),
    )


def attend_first(plan, shift, meta, qg, kv_list):
    window = pltpu.VMEM((plan.window_ranges * plan.rows, plan.width), jnp.bfloat16)
    out_shape = [
        jax.ShapeDtypeStruct((2, plan.cols, plan.width), jnp.bfloat16),
        jax.ShapeDtypeStruct((plan.reach + plan.block, 2 * plan.width), jnp.float32),
    ]
    operands = (meta, qg, *kv_list)
    return kernel_call(
        functools.partial(first_kernel, plan, shift), "attend_first", operands,
        [pltpu.SMEM] + [pltpu.VMEM] * (len(operands) - 1), out_shape, [window, window],
        out_specs=[spec_of(pltpu.VMEM)] * 2, cost_estimate=plan.cost(1),
    )


def attend_last(plan, first_shift, items, meta, qg_list, first_grad, kv_list):
    n = plan.n
    window = pltpu.VMEM((plan.window_ranges * plan.rows, plan.width), jnp.bfloat16)
    grads = (n // 4, n, plan.block, 2 * plan.width)
    out_shape = [jax.ShapeDtypeStruct((2, plan.cols, plan.width), jnp.bfloat16)] * len(items)
    out_shape += [jax.ShapeDtypeStruct(grads, jnp.bfloat16 if apart % 2 else jnp.float32) for apart in range(4)]
    operands = (meta, *qg_list, first_grad, *kv_list)
    return kernel_call(
        functools.partial(last_kernel, plan, first_shift, items), "attend_last", operands,
        [pltpu.SMEM] + [pltpu.VMEM] * (len(operands) - 1), out_shape,
        [window, window, pltpu.VMEM(((n + 1) * plan.rows, 2 * plan.width), jnp.float32)],
        out_specs=[spec_of(pltpu.VMEM)] * len(out_shape), cost_estimate=plan.cost(len(items)), grid=(len(items),),
    )


def place_kernel(plan, items, final, meta, *refs):
    n, cols, width, own = plan.n, plan.cols, plan.width, meta[0]
    pay_refs, refs = dict(zip(items, refs[: len(items)])), refs[len(items) :]
    if final:
        grads, (_, _, attended, query_grad, key_grad, value_grad, sems) = refs[:-7], refs[-7:]
    else:
        grads, (attended, query_grad, send, sems) = refs[:-4], refs[-4:]

    def copies(i, item):
        if item == "ahead":
            source, here = own + 1, own < n - 1
        elif item == "behind":
            source, here = own - 1, jnp.logical_and(own >= 1, own <= plan.back)
        else:
            source = lax.rem(own - item + n, n)
            here = own >= 0
            if EARLY and item == 1:
                here = source >= plan.back
            if EARLY and item == n - 1:
                here = own == n - 1
        to = pl.ds(pl.multiple_of(source * cols, cols), cols)
        return here, [
            pltpu.make_async_copy(pay_refs[item].at[0], attended.at[to, :], sems.at[i, 0]),
            pltpu.make_async_copy(pay_refs[item].at[1], query_grad.at[to, :], sems.at[i, 1]),
        ]

    def each(act):
        for i, item in enumerate(items):
            here, pair = copies(i, item)

            @pl.when(here)
            def _():
                for copy in pair:
                    act(copy)

    each(lambda copy: copy.start())
    total = sum(grad[...].astype(jnp.float32) for grad in grads)
    if not final:
        send[...] = total.astype(jnp.bfloat16)
    if final:
        key_grad[...] = total[:, :width].astype(jnp.bfloat16)
        value_grad[...] = total[:, width:].astype(jnp.bfloat16)
    each(lambda copy: copy.wait())


def place(plan, meta, payloads, grads=(), filled=()):
    items = tuple(payloads)
    big = jax.ShapeDtypeStruct((plan.rows * plan.heads, plan.width), jnp.bfloat16)
    small = jax.ShapeDtypeStruct((plan.rows, plan.width), jnp.bfloat16)
    final = len(filled) > 0
    at = 1 + len(items) + len(grads)
    return kernel_call(
        functools.partial(place_kernel, plan, items, final), "place_last" if final else "place_first",
        (meta, *payloads.values(), *grads, *filled),
        [pltpu.SMEM] + [pl.ANY] * len(items) + [pltpu.VMEM] * len(grads) + [pl.ANY] * len(filled),
        [big, big] + ([small, small] if final else [jax.ShapeDtypeStruct(grads[0].shape, jnp.bfloat16)]), [pltpu.SemaphoreType.DMA((len(items), 2))],
        out_specs=[spec_of(pl.ANY)] * 2 + [spec_of(pltpu.VMEM)] * (1 + final),
        input_output_aliases={at: 0, at + 1: 1} if final else {},
        cost_estimate=plan.cost(len(items)),
    )


def on_device(query, keys, values, output_gradient, doc_lengths, block_owner):
    n = lax.axis_size("ctx")
    own = lax.axis_index("ctx")
    rows, heads, width = query.shape
    plan = Plan(n, rows, heads, width, doc_lengths.shape[0])

    def passed(array, by):
        return lax.ppermute(array, "ctx", [(i, (i + by) % n) for i in range(n)])

    k = keys.reshape(rows, width)
    v = values.reshape(rows, width)
    kv_list = []
    for i in range(1, plan.back + 1):
        kv_list += [passed(k, i), passed(v, i)]
    owners = jnp.arange(n, dtype=jnp.int32)
    match = block_owner[:, None, :] == owners[None, :, None]
    table = jnp.sum(jnp.where(match, owners, 0), axis=2)
    meta = jnp.concatenate(
        [own.reshape(1).astype(jnp.int32), jnp.cumsum(doc_lengths).astype(jnp.int32), table.reshape(-1)]
    )

    blocks = pack(plan, meta, query.reshape(rows * heads, width), output_gradient.reshape(rows * heads, width), k, v)
    kv_list = [blocks[n], *kv_list]
    first = n // 2
    items = tuple([i for i in range(1, n) if i != first] + [0])
    first_pay, first_grad = attend_first(plan, first, meta, blocks[first], kv_list)
    first_pay = passed(first_pay, first)
    out = attend_last(plan, first, items, meta, [blocks[i] for i in items], first_grad, kv_list)
    stay = {first: first_pay}
    late = {}
    for item, pay in zip(items, out):
        if item:
            late[item] = passed(pay, item)
        else:
            stay[item] = pay
    def across(array, bit):
        return lax.ppermute(array, "ctx", [(i, i ^ bit) for i in range(n)])

    keep, to_keep, pass_on, to_pass_on = out[len(items) :]
    pass_on = (pass_on, across(to_pass_on, 1))
    terms = (keep, across(to_keep, 1))
    attended, query_grad, send = place(plan, meta, stay, pass_on)
    terms += (across(send, 2),)
    bit = 4
    while bit < n:
        total = sum(term.astype(jnp.float32) for term in terms)
        terms = (total[0::2], across(total[1::2].astype(jnp.bfloat16), bit))
        bit *= 2
    terms = [term.reshape(rows, 2 * width) for term in terms]
    attended, query_grad, key_grad, value_grad = place(plan, meta, late, terms, (attended, query_grad))
    return (
        attended.reshape(rows, heads, width),
        query_grad.reshape(rows, heads, width),
        key_grad.reshape(rows, 1, width),
        value_grad.reshape(rows, 1, width),
    )


def solution(mesh):
    rows = P(("dp", "ctx"), "tp", None)
    return jax.shard_map(
        on_device,
        mesh=mesh,
        in_specs=(rows, rows, rows, rows, P("dp"), P("dp", None)),
        out_specs=(rows, rows, rows, rows),
        check_vma=False,
    )
```

```python
import functools
import jax
import jax.numpy as jnp
from jax import lax
from jax.experimental import pallas as pl
from jax.experimental.pallas import tpu as pltpu
from jax.sharding import PartitionSpec as P

MASKED = -1e30
LOG2_E = 1.4426950408889634
VMEM_LIMIT = 32 * 1024 * 1024


def dot(a, b, contract):
    return lax.dot_general(a, b, ((contract[0], contract[1]), ((), ())), preferred_element_type=jnp.float32)


def attend_block(first_row, ends, q, g, k, v, reach, heads, scale):
    cols = q.shape[0]
    key_rows = k.shape[0]
    token = lax.broadcasted_iota(jnp.int32, (1, cols), 1) // heads
    query_pos = first_row + token
    doc_start = jnp.zeros((1, cols), jnp.int32)
    for end in ends:
        doc_start = jnp.maximum(doc_start, jnp.where(end <= query_pos, end, 0))
    low = doc_start - (first_row - reach)
    raw = dot(k, q, ((1,), (1,)))
    index = lax.broadcasted_iota(jnp.int32, (key_rows, cols), 0)
    allowed = index >= low
    allowed_late = jnp.logical_and(allowed[reach:], index[reach:] - reach <= token)
    raw = jnp.concatenate(
        [jnp.where(allowed[:reach], raw[:reach], MASKED), jnp.where(allowed_late, raw[reach:], MASKED)], axis=0
    )
    row_max = jnp.max(raw, axis=0, keepdims=True)
    weights = jnp.exp2((raw - row_max) * (scale * LOG2_E))
    inverse = 1.0 / jnp.sum(weights, axis=0, keepdims=True)
    attended_t = (dot(v, weights.astype(jnp.bfloat16), ((0,), (0,))) * inverse).astype(jnp.bfloat16)
    attended = attended_t.T
    g_t = g.T.astype(jnp.float32)
    delta = jnp.sum(g_t * attended_t.astype(jnp.float32), axis=0, keepdims=True)
    probs = weights * inverse
    products = dot(v, g, ((1,), (1,)))
    slopes = (probs * (products - delta)).astype(jnp.bfloat16)
    value_part = dot(probs.astype(jnp.bfloat16), g, ((1,), (0,)))
    key_part = dot(slopes, q, ((1,), (0,))) * scale
    query_grad = (dot(k, slopes, ((0,), (0,))) * scale).astype(jnp.bfloat16).T
    return attended, query_grad, key_part, value_part


class Plan:
    def __init__(self, n, rows, heads, width, ndocs):
        self.n, self.rows, self.heads, self.width, self.ndocs = n, rows, heads, width, ndocs
        self.back = n // 2
        self.block = rows // n
        self.cols = self.block * heads
        self.reach = self.back * rows
        self.scale = width ** (-0.5)
        self.window_ranges = self.back + 3

    def ends(self, meta):
        return [meta[1 + i] for i in range(self.ndocs)]

    def slot(self, meta, loader, owner):
        return meta[1 + self.ndocs + loader * self.n + owner]

    def cost(self, blocks):
        return pl.CostEstimate(
            flops=14 * blocks * self.cols * (self.reach + self.block) * self.width * 8,
            bytes_accessed=blocks * self.cols * self.width * 16,
            transcendentals=blocks * self.cols * (self.reach + self.block),
        )


def fill_window(plan, refs, k_win, v_win):
    rows = plan.rows
    for i, ref in enumerate(refs):
        place = plan.back + 1 - i if i <= plan.back else plan.back + 2
        k_win[pl.ds(place * rows, rows), :] = ref[pl.ds(0, rows), :]
        v_win[pl.ds(place * rows, rows), :] = ref[pl.ds(rows, rows), :]
    if len(refs) > plan.back + 1:
        k_win[pl.ds(0, rows), :] = jnp.zeros((rows, plan.width), k_win.dtype)
        v_win[pl.ds(0, rows), :] = jnp.zeros((rows, plan.width), v_win.dtype)


def attend_at(plan, meta, loader, slot, q, g, k_win, v_win):
    start = (loader - meta[0] + 1) * plan.rows + slot * plan.block
    keys_here = pl.ds(pl.multiple_of(start, plan.block), plan.reach + plan.block)
    out = attend_block(
        loader * plan.rows + slot * plan.block, plan.ends(meta), q, g, k_win[keys_here, :], v_win[keys_here, :],
        plan.reach, plan.heads, plan.scale,
    )
    return keys_here, out


def pack_kernel(plan, meta, q_ref, g_ref, *refs):
    blocks, sems = refs[: plan.n], refs[plan.n]
    own = meta[0]
    copies = []
    for shift, block in enumerate(blocks):
        slot = plan.slot(meta, own, lax.rem(own + shift, plan.n))
        at = pl.ds(pl.multiple_of(slot * plan.cols, plan.cols), plan.cols)
        copies.append(pltpu.make_async_copy(q_ref.at[at, :], block.at[0], sems.at[shift, 0]))
        copies.append(pltpu.make_async_copy(g_ref.at[at, :], block.at[1], sems.at[shift, 1]))
    for copy in copies:
        copy.start()
    for copy in copies:
        copy.wait()


def first_kernel(plan, shift, meta, qg, *refs):
    kv_refs, (pay_ref, grad_ref, k_win, v_win) = refs[:-4], refs[-4:]
    own = meta[0]
    slot = plan.slot(meta, own, lax.rem(own + shift, plan.n))
    fill_window(plan, kv_refs, k_win, v_win)
    _, (attended, query_grad, key_part, value_part) = attend_at(
        plan, meta, own, slot, qg[0], qg[1], k_win, v_win
    )
    pay_ref[0] = attended
    pay_ref[1] = query_grad
    grad_ref[:, : plan.width] = key_part
    grad_ref[:, plan.width :] = value_part


def last_kernel(plan, first_shift, items, meta, *refs):
    n, width, rows, block = plan.n, plan.width, plan.rows, plan.block
    qg_refs, refs = refs[: len(items)], refs[len(items) :]
    first_grad, refs = refs[0], refs[1:]
    kv_refs, refs = refs[: -(len(items) + 7)], refs[-(len(items) + 7) :]
    pay_refs, grad_refs, (k_win, v_win, acc) = refs[: len(items)], refs[len(items) : -3], refs[-3:]
    step = pl.program_id(0)
    own = meta[0]

    def valid(item):
        if item == "ahead":
            return own < n - 1
        if item == "behind":
            return jnp.logical_and(own >= 1, own <= plan.back)
        if item == 1:
            return own >= plan.back
        if item == n - 1:
            return own == 0
        return own >= 0

    @pl.when(step == 0)
    def _():
        fill_window(plan, kv_refs, k_win, v_win)
        acc[...] = jnp.zeros_like(acc)
        slot = plan.slot(meta, own, lax.rem(own + first_shift, n))
        keys_here = pl.ds(pl.multiple_of(rows + slot * block, block), plan.reach + block)
        acc[keys_here, :] = first_grad[...]

    for i, item in enumerate(items):

        @pl.when(jnp.logical_and(step == i, valid(item)))
        def _():
            loader = own + {"ahead": 1, "behind": -1}.get(item, 0)
            owner = own if item in ("ahead", "behind") else lax.rem(own + item, n)
            slot = plan.slot(meta, loader, owner)
            qg = qg_refs[i]
            keys_here, (attended, query_grad, key_part, value_part) = attend_at(
                plan, meta, loader, slot, qg[0], qg[1], k_win, v_win
            )
            acc[keys_here, :width] = acc[keys_here, :width] + key_part
            acc[keys_here, width:] = acc[keys_here, width:] + value_part
            pay_refs[i][0] = attended
            pay_refs[i][1] = query_grad

    @pl.when(step == len(items) - 1)
    def _():
        def of_range(key_range, carry):
            at = (lax.rem(key_range - own + plan.back + n, n) + 1) * rows
            for apart in range(n):
                slot = plan.slot(meta, key_range, own ^ apart)
                part = acc[pl.ds(pl.multiple_of(at + slot * block, block), block), :]
                to = grad_refs[apart % 4]
                to[apart // 4, key_range] = part.astype(to.dtype)
            return carry

        lax.fori_loop(0, n, of_range, 0)


def spec_of(space):
    return pl.BlockSpec(memory_space=space)


def kernel_call(body, name, operands, spaces, out_shape, scratch, **more):
    return pl.pallas_call(
        body,
        out_shape=out_shape,
        in_specs=[spec_of(space) for space in spaces],
        compiler_params=pltpu.CompilerParams(vmem_limit_bytes=VMEM_LIMIT),
        scratch_shapes=scratch,
        name=name,
        **more,
    )(*operands)


def pack(plan, meta, q, g):
    out_shape = [jax.ShapeDtypeStruct((2, plan.cols, plan.width), jnp.bfloat16)] * plan.n
    q, g = (pltpu.with_memory_space_constraint(x, pltpu.HBM) for x in (q, g))
    return kernel_call(
        functools.partial(pack_kernel, plan), "pack", (meta, q, g), [pltpu.SMEM] + [pl.ANY] * 2, out_shape,
        [pltpu.SemaphoreType.DMA((plan.n, 2))],
        out_specs=[spec_of(pltpu.VMEM)] * len(out_shape),
    )


def attend_first(plan, shift, meta, qg, kv_list):
    window = pltpu.VMEM((plan.window_ranges * plan.rows, plan.width), jnp.bfloat16)
    out_shape = [
        jax.ShapeDtypeStruct((2, plan.cols, plan.width), jnp.bfloat16),
        jax.ShapeDtypeStruct((plan.reach + plan.block, 2 * plan.width), jnp.float32),
    ]
    operands = (meta, qg, *kv_list)
    return kernel_call(
        functools.partial(first_kernel, plan, shift), "attend_first", operands,
        [pltpu.SMEM] + [pltpu.VMEM] * (len(operands) - 1), out_shape, [window, window],
        out_specs=[spec_of(pltpu.VMEM)] * 2, cost_estimate=plan.cost(1),
    )


def attend_last(plan, first_shift, items, meta, qg_list, first_grad, kv_list):
    n = plan.n
    window = pltpu.VMEM((plan.window_ranges * plan.rows, plan.width), jnp.bfloat16)
    grads = (n // 4, n, plan.block, 2 * plan.width)
    out_shape = [jax.ShapeDtypeStruct((2, plan.cols, plan.width), jnp.bfloat16)] * len(items)
    out_shape += [jax.ShapeDtypeStruct(grads, jnp.bfloat16 if apart % 2 else jnp.float32) for apart in range(4)]
    operands = (meta, *qg_list, first_grad, *kv_list)
    return kernel_call(
        functools.partial(last_kernel, plan, first_shift, items), "attend_last", operands,
        [pltpu.SMEM] + [pltpu.VMEM] * (len(operands) - 1), out_shape,
        [window, window, pltpu.VMEM(((n + 1) * plan.rows, 2 * plan.width), jnp.float32)],
        out_specs=[spec_of(pltpu.VMEM)] * len(out_shape), cost_estimate=plan.cost(len(items)), grid=(len(items),),
    )


def place_kernel(plan, items, final, meta, *refs):
    n, cols, width, own = plan.n, plan.cols, plan.width, meta[0]
    pay_refs, refs = dict(zip(items, refs[: len(items)])), refs[len(items) :]
    if final:
        grads, (_, _, attended, query_grad, key_grad, value_grad, sems) = refs[:-7], refs[-7:]
    else:
        grads, (attended, query_grad, send, sems) = refs[:-4], refs[-4:]

    def copies(i, item):
        if item == "ahead":
            source, here = own + 1, own < n - 1
        elif item == "behind":
            source, here = own - 1, jnp.logical_and(own >= 1, own <= plan.back)
        else:
            source = lax.rem(own - item + n, n)
            here = own >= 0
            if item == 1:
                here = source >= plan.back
            if item == n - 1:
                here = own == n - 1
        to = pl.ds(pl.multiple_of(source * cols, cols), cols)
        return here, [
            pltpu.make_async_copy(pay_refs[item].at[0], attended.at[to, :], sems.at[i, 0]),
            pltpu.make_async_copy(pay_refs[item].at[1], query_grad.at[to, :], sems.at[i, 1]),
        ]

    def each(act):
        for i, item in enumerate(items):
            here, pair = copies(i, item)

            @pl.when(here)
            def _():
                for copy in pair:
                    act(copy)

    each(lambda copy: copy.start())
    total = sum(grad[...].astype(jnp.float32) for grad in grads)
    if not final:
        send[...] = total.astype(jnp.bfloat16)
    if final:
        key_grad[...] = total[:, :width].astype(jnp.bfloat16)
        value_grad[...] = total[:, width:].astype(jnp.bfloat16)
    each(lambda copy: copy.wait())


def place(plan, meta, payloads, grads=(), filled=()):
    items = tuple(payloads)
    big = jax.ShapeDtypeStruct((plan.rows * plan.heads, plan.width), jnp.bfloat16)
    small = jax.ShapeDtypeStruct((plan.rows, plan.width), jnp.bfloat16)
    final = len(filled) > 0
    at = 1 + len(items) + len(grads)
    return kernel_call(
        functools.partial(place_kernel, plan, items, final), "place_last" if final else "place_first",
        (meta, *payloads.values(), *grads, *filled),
        [pltpu.SMEM] + [pl.ANY] * len(items) + [pltpu.VMEM] * len(grads) + [pl.ANY] * len(filled),
        [big, big] + ([small, small] if final else [jax.ShapeDtypeStruct(grads[0].shape, jnp.bfloat16)]), [pltpu.SemaphoreType.DMA((len(items), 2))],
        out_specs=[spec_of(pl.ANY)] * 2 + [spec_of(pltpu.VMEM)] * (1 + final),
        input_output_aliases={at: 0, at + 1: 1} if final else {},
        cost_estimate=plan.cost(len(items)),
    )


def on_device(query, keys, values, output_gradient, doc_lengths, block_owner):
    n = lax.axis_size("ctx")
    own = lax.axis_index("ctx")
    rows, heads, width = query.shape
    plan = Plan(n, rows, heads, width, doc_lengths.shape[0])

    def passed(array, by, sources=range(n)):
        return lax.ppermute(array, "ctx", [(i, (i + by) % n) for i in sources])

    kv = jnp.concatenate([keys.reshape(rows, width), values.reshape(rows, width)])
    kv_back = [passed(kv, i, range(n - i)) for i in range(1, plan.back + 1)]
    kv_ahead = passed(kv, -1, range(1, n))

    owners = jnp.arange(n, dtype=jnp.int32)
    match = block_owner[:, None, :] == owners[None, :, None]
    table = jnp.sum(jnp.where(match, owners, 0), axis=2)
    meta = jnp.concatenate(
        [own.reshape(1).astype(jnp.int32), jnp.cumsum(doc_lengths).astype(jnp.int32), table.reshape(-1)]
    )

    blocks = pack(plan, meta, query.reshape(rows * heads, width), output_gradient.reshape(rows * heads, width))
    from_ahead = passed(blocks[n - 1], -1, range(1, n))
    from_behind = passed(blocks[1], 1, range(plan.back))
    kv_list = [kv, *kv_back]
    first = n // 2
    first_pay, first_grad = attend_first(plan, first, meta, blocks[first], kv_list)
    first_pay = passed(first_pay, first)
    sent = [i for i in range(1, n) if i != first]
    items = (*sent, 0, "ahead", "behind")
    qg_list = [blocks[i] for i in sent] + [blocks[0], from_ahead, from_behind]
    out = attend_last(plan, first, items, meta, qg_list, first_grad, [*kv_list, kv_ahead])
    stay = {first: first_pay}
    late = {}
    for item, pay in zip(items, out):
        if item in sent:
            sources = range(plan.back, n) if item == 1 else range(1) if item == n - 1 else range(n)
            late[item] = passed(pay, item, sources)
        else:
            stay[item] = pay
    def across(array, bit):
        return lax.ppermute(array, "ctx", [(i, i ^ bit) for i in range(n)])

    keep, to_keep, pass_on, to_pass_on = out[len(items) :]
    pass_on = (pass_on, across(to_pass_on, 1))
    terms = (keep, across(to_keep, 1))
    attended, query_grad, send = place(plan, meta, stay, pass_on)
    terms += (across(send, 2),)
    bit = 4
    while bit < n:
        total = sum(term.astype(jnp.float32) for term in terms)
        terms = (total[0::2], across(total[1::2].astype(jnp.bfloat16), bit))
        bit *= 2
    terms = [term.reshape(rows, 2 * width) for term in terms]
    attended, query_grad, key_grad, value_grad = place(plan, meta, late, terms, (attended, query_grad))
    return (
        attended.reshape(rows, heads, width),
        query_grad.reshape(rows, heads, width),
        key_grad.reshape(rows, 1, width),
        value_grad.reshape(rows, 1, width),
    )


def solution(mesh):
    rows = P(("dp", "ctx"), "tp", None)
    return jax.shard_map(
        on_device,
        mesh=mesh,
        in_specs=(rows, rows, rows, rows, P("dp"), P("dp", None)),
        out_specs=(rows, rows, rows, rows),
        check_vma=False,
    )
```

```python
import functools
import jax
import jax.numpy as jnp
from jax import lax
from jax.experimental import pallas as pl
from jax.experimental.pallas import tpu as pltpu
from jax.sharding import PartitionSpec as P

MASKED = -1e30
LOG2_E = 1.4426950408889634
VMEM_LIMIT = 32 * 1024 * 1024


def dot(a, b, contract):
    return lax.dot_general(a, b, ((contract[0], contract[1]), ((), ())), preferred_element_type=jnp.float32)


def attend_block(first_row, ends, q, g, k, v, reach, heads, scale):
    cols = q.shape[0]
    key_rows = k.shape[0]
    token = lax.broadcasted_iota(jnp.int32, (1, cols), 1) // heads
    query_pos = first_row + token
    doc_start = jnp.zeros((1, cols), jnp.int32)
    for end in ends:
        doc_start = jnp.maximum(doc_start, jnp.where(end <= query_pos, end, 0))
    low = doc_start - (first_row - reach)
    raw = dot(k, q, ((1,), (1,)))
    index = lax.broadcasted_iota(jnp.int32, (key_rows, cols), 0)
    allowed = index >= low
    allowed_late = jnp.logical_and(allowed[reach:], index[reach:] - reach <= token)
    raw = jnp.concatenate(
        [jnp.where(allowed[:reach], raw[:reach], MASKED), jnp.where(allowed_late, raw[reach:], MASKED)], axis=0
    )
    row_max = jnp.max(raw, axis=0, keepdims=True)
    weights = jnp.exp2((raw - row_max) * (scale * LOG2_E))
    inverse = 1.0 / jnp.sum(weights, axis=0, keepdims=True)
    attended_t = (dot(v, weights.astype(jnp.bfloat16), ((0,), (0,))) * inverse).astype(jnp.bfloat16)
    attended = attended_t.T
    g_t = g.T.astype(jnp.float32)
    delta = jnp.sum(g_t * attended_t.astype(jnp.float32), axis=0, keepdims=True)
    probs = weights * inverse
    products = dot(v, g, ((1,), (1,)))
    slopes = (probs * (products - delta)).astype(jnp.bfloat16)
    value_part = dot(probs.astype(jnp.bfloat16), g, ((1,), (0,)))
    key_part = dot(slopes, q, ((1,), (0,))) * scale
    query_grad = (dot(k, slopes, ((0,), (0,))) * scale).astype(jnp.bfloat16).T
    return attended, query_grad, key_part, value_part


class Plan:
    def __init__(self, n, rows, heads, width, ndocs):
        self.n, self.rows, self.heads, self.width, self.ndocs = n, rows, heads, width, ndocs
        self.back = n // 2
        self.block = rows // n
        self.cols = self.block * heads
        self.reach = self.back * rows
        self.scale = width ** (-0.5)
        self.window_ranges = self.back + 3

    def ends(self, meta):
        return [meta[1 + i] for i in range(self.ndocs)]

    def slot(self, meta, loader, owner):
        return meta[1 + self.ndocs + loader * self.n + owner]

    def cost(self, blocks):
        return pl.CostEstimate(
            flops=14 * blocks * self.cols * (self.reach + self.block) * self.width * 8,
            bytes_accessed=blocks * self.cols * self.width * 16,
            transcendentals=blocks * self.cols * (self.reach + self.block),
        )


def fill_window(plan, refs, k_win, v_win):
    rows = plan.rows
    for i, ref in enumerate(refs):
        place = plan.back + 1 - i if i <= plan.back else plan.back + 2
        k_win[pl.ds(place * rows, rows), :] = ref[pl.ds(0, rows), :]
        v_win[pl.ds(place * rows, rows), :] = ref[pl.ds(rows, rows), :]
    if len(refs) > plan.back + 1:
        k_win[pl.ds(0, rows), :] = jnp.zeros((rows, plan.width), k_win.dtype)
        v_win[pl.ds(0, rows), :] = jnp.zeros((rows, plan.width), v_win.dtype)


def attend_at(plan, meta, loader, slot, q, g, k_win, v_win):
    start = (loader - meta[0] + 1) * plan.rows + slot * plan.block
    keys_here = pl.ds(pl.multiple_of(start, plan.block), plan.reach + plan.block)
    out = attend_block(
        loader * plan.rows + slot * plan.block, plan.ends(meta), q, g, k_win[keys_here, :], v_win[keys_here, :],
        plan.reach, plan.heads, plan.scale,
    )
    return keys_here, out


def pack_kernel(plan, meta, q_ref, g_ref, *refs):
    blocks, sems = refs[: plan.n], refs[plan.n]
    own = meta[0]
    copies = []
    for apart, block in enumerate(blocks):
        slot = plan.slot(meta, own, own ^ apart)
        at = pl.ds(pl.multiple_of(slot * plan.cols, plan.cols), plan.cols)
        copies.append(pltpu.make_async_copy(q_ref.at[at, :], block.at[0], sems.at[apart, 0]))
        copies.append(pltpu.make_async_copy(g_ref.at[at, :], block.at[1], sems.at[apart, 1]))
    for copy in copies:
        copy.start()
    for copy in copies:
        copy.wait()


def first_kernel(plan, apart, meta, qg, *refs):
    kv_refs, (pay_ref, grad_ref, k_win, v_win) = refs[:-4], refs[-4:]
    own = meta[0]
    slot = plan.slot(meta, own, own ^ apart)
    fill_window(plan, kv_refs, k_win, v_win)
    _, (attended, query_grad, key_part, value_part) = attend_at(
        plan, meta, own, slot, qg[0], qg[1], k_win, v_win
    )
    pay_ref[0] = attended
    pay_ref[1] = query_grad
    grad_ref[:, : plan.width] = key_part
    grad_ref[:, plan.width :] = value_part


def last_kernel(plan, first, items, meta, *refs):
    n, width, rows, block = plan.n, plan.width, plan.rows, plan.block
    qg_refs, refs = refs[: len(items)], refs[len(items) :]
    first_grad, refs = refs[0], refs[1:]
    kv_refs, refs = refs[: -(len(items) + 7)], refs[-(len(items) + 7) :]
    pay_refs, grad_refs, (k_win, v_win, acc) = refs[: len(items)], refs[len(items) : -3], refs[-3:]
    step = pl.program_id(0)
    own = meta[0]

    @pl.when(step == 0)
    def _():
        fill_window(plan, kv_refs, k_win, v_win)
        acc[...] = jnp.zeros_like(acc)
        slot = plan.slot(meta, own, own ^ first)
        keys_here = pl.ds(pl.multiple_of(rows + slot * block, block), plan.reach + block)
        acc[keys_here, :] = first_grad[...]

    for i, item in enumerate(items):

        @pl.when(step == i)
        def _():
            slot = plan.slot(meta, own, own ^ item)
            qg = qg_refs[i]
            keys_here, (attended, query_grad, key_part, value_part) = attend_at(
                plan, meta, own, slot, qg[0], qg[1], k_win, v_win
            )
            acc[keys_here, :width] = acc[keys_here, :width] + key_part
            acc[keys_here, width:] = acc[keys_here, width:] + value_part
            pay_refs[i][0] = attended
            pay_refs[i][1] = query_grad

    @pl.when(step == len(items) - 1)
    def _():
        def of_range(key_range, carry):
            at = (lax.rem(key_range - own + plan.back + n, n) + 1) * rows
            for apart in range(n):
                slot = plan.slot(meta, key_range, own ^ apart)
                part = acc[pl.ds(pl.multiple_of(at + slot * block, block), block), :]
                to = grad_refs[apart % 4]
                to[apart // 4, key_range] = part.astype(to.dtype)
            return carry

        lax.fori_loop(0, n, of_range, 0)


def spec_of(space):
    return pl.BlockSpec(memory_space=space)


def kernel_call(body, name, operands, spaces, out_shape, scratch, **more):
    return pl.pallas_call(
        body,
        out_shape=out_shape,
        in_specs=[spec_of(space) for space in spaces],
        compiler_params=pltpu.CompilerParams(vmem_limit_bytes=VMEM_LIMIT),
        scratch_shapes=scratch,
        name=name,
        **more,
    )(*operands)


def pack(plan, meta, q, g):
    out_shape = [jax.ShapeDtypeStruct((2, plan.cols, plan.width), jnp.bfloat16)] * plan.n
    q, g = (pltpu.with_memory_space_constraint(x, pltpu.HBM) for x in (q, g))
    return kernel_call(
        functools.partial(pack_kernel, plan), "pack", (meta, q, g), [pltpu.SMEM] + [pl.ANY] * 2, out_shape,
        [pltpu.SemaphoreType.DMA((plan.n, 2))],
        out_specs=[spec_of(pltpu.VMEM)] * len(out_shape),
    )


def attend_first(plan, apart, meta, qg, kv_list):
    window = pltpu.VMEM((plan.window_ranges * plan.rows, plan.width), jnp.bfloat16)
    out_shape = [
        jax.ShapeDtypeStruct((2, plan.cols, plan.width), jnp.bfloat16),
        jax.ShapeDtypeStruct((plan.reach + plan.block, 2 * plan.width), jnp.float32),
    ]
    operands = (meta, qg, *kv_list)
    return kernel_call(
        functools.partial(first_kernel, plan, apart), "attend_first", operands,
        [pltpu.SMEM] + [pltpu.VMEM] * (len(operands) - 1), out_shape, [window, window],
        out_specs=[spec_of(pltpu.VMEM)] * 2, cost_estimate=plan.cost(1),
    )


def attend_last(plan, first, items, meta, qg_list, first_grad, kv_list):
    n = plan.n
    window = pltpu.VMEM((plan.window_ranges * plan.rows, plan.width), jnp.bfloat16)
    grads = (n // 4, n, plan.block, 2 * plan.width)
    out_shape = [jax.ShapeDtypeStruct((2, plan.cols, plan.width), jnp.bfloat16)] * len(items)
    out_shape += [jax.ShapeDtypeStruct(grads, jnp.bfloat16 if apart % 2 else jnp.float32) for apart in range(4)]
    operands = (meta, *qg_list, first_grad, *kv_list)
    return kernel_call(
        functools.partial(last_kernel, plan, first, items), "attend_last", operands,
        [pltpu.SMEM] + [pltpu.VMEM] * (len(operands) - 1), out_shape,
        [window, window, pltpu.VMEM(((n + 1) * plan.rows, 2 * plan.width), jnp.float32)],
        out_specs=[spec_of(pltpu.VMEM)] * len(out_shape), cost_estimate=plan.cost(len(items)), grid=(len(items),),
    )


def place_kernel(plan, items, final, *refs):
    n, cols, width = plan.n, plan.cols, plan.width
    own = lax.axis_index("ctx")
    pay_refs, refs = refs[: len(items)], refs[len(items) :]
    if final:
        grads, (_, _, attended, query_grad, key_grad, value_grad, sums, sems, sum_sems) = refs[:-9], refs[-9:]
    else:
        grads, (attended, query_grad, send, sems) = refs[:-4], refs[-4:]
    copies = []
    for i, item in enumerate(items):
        to = pl.ds(pl.multiple_of((own ^ item) * cols, cols), cols)
        copies.append(pltpu.make_async_copy(pay_refs[i].at[0], attended.at[to, :], sems.at[i, 0]))
        copies.append(pltpu.make_async_copy(pay_refs[i].at[1], query_grad.at[to, :], sems.at[i, 1]))
    for copy in copies:
        copy.start()
    total = sum(grad[...].astype(jnp.float32) for grad in grads).astype(jnp.bfloat16)
    if final:
        sums[0] = total[:, :width]
        sums[1] = total[:, width:]
        for i, ref in enumerate((key_grad, value_grad)):
            copies.append(pltpu.make_async_copy(sums.at[i], ref, sum_sems.at[i]))
            copies[-1].start()
    else:
        send[...] = total
    for copy in copies:
        copy.wait()


def place(plan, payloads, grads, filled=()):
    items = tuple(payloads)
    big = jax.ShapeDtypeStruct((plan.rows * plan.heads, plan.width), jnp.bfloat16)
    small = jax.ShapeDtypeStruct((plan.rows, plan.width), jnp.bfloat16)
    final = len(filled) > 0
    at = len(items) + len(grads)
    scratch = [pltpu.SemaphoreType.DMA((len(items), 2))]
    if final:
        scratch = [pltpu.VMEM((2, plan.rows, plan.width), jnp.bfloat16), *scratch, pltpu.SemaphoreType.DMA((2,))]
    return kernel_call(
        functools.partial(place_kernel, plan, items, final), "place_last" if final else "place_first",
        (*payloads.values(), *grads, *filled),
        [pl.ANY] * len(items) + [pltpu.VMEM] * len(grads) + [pl.ANY] * len(filled),
        [big, big] + ([small, small] if final else [jax.ShapeDtypeStruct(grads[0].shape, jnp.bfloat16)]), scratch,
        out_specs=[spec_of(pl.ANY)] * 2 + [spec_of(pl.ANY)] * 2 if final else [spec_of(pl.ANY)] * 2 + [spec_of(pltpu.VMEM)],
        input_output_aliases={at: 0, at + 1: 1} if final else {},
        cost_estimate=plan.cost(len(items)),
    )


def on_device(query, keys, values, output_gradient, doc_lengths, block_owner):
    n = lax.axis_size("ctx")
    own = lax.axis_index("ctx")
    rows, heads, width = query.shape
    plan = Plan(n, rows, heads, width, doc_lengths.shape[0])

    def permuted(array, pairs):
        return lax.ppermute(array, "ctx", pairs)

    def across(array, bits):
        return permuted(array, [(i, i ^ bits) for i in range(n)])

    kv = jnp.concatenate([keys.reshape(rows, width), values.reshape(rows, width)])
    kv_list = [kv] + [permuted(kv, [(i, i + by) for i in range(n - by)]) for by in range(1, plan.back + 1)]

    owners = jnp.arange(n, dtype=jnp.int32)
    match = block_owner[:, None, :] == owners[None, :, None]
    table = jnp.sum(jnp.where(match, owners, 0), axis=2)
    meta = jnp.concatenate(
        [own.reshape(1).astype(jnp.int32), jnp.cumsum(doc_lengths).astype(jnp.int32), table.reshape(-1)]
    )

    blocks = pack(plan, meta, query.reshape(rows * heads, width), output_gradient.reshape(rows * heads, width))
    first = n // 2
    first_pay, first_grad = attend_first(plan, first, meta, blocks[first], kv_list)
    stay = {first: across(first_pay, first)}
    sent = [x for x in range(n - 1, 0, -1) if x != first]
    items = (*sent, 0)
    out = attend_last(plan, first, items, meta, [blocks[x] for x in items], first_grad, kv_list)
    late = {x: across(pay, x) for x, pay in zip(sent, out)}
    stay[0] = out[len(sent)]
    keep, to_keep, pass_on, to_pass_on = out[len(items) :]
    pass_on = (pass_on, across(to_pass_on, 1))
    terms = (keep, across(to_keep, 1))
    attended, query_grad, send = place(plan, stay, pass_on)
    terms += (across(send, 2),)
    bit = 4
    while bit < n:
        total = sum(term.astype(jnp.float32) for term in terms)
        terms = (total[0::2], across(total[1::2].astype(jnp.bfloat16), bit))
        bit *= 2
    terms = [term.reshape(rows, 2 * width) for term in terms]
    attended, query_grad, key_grad, value_grad = place(plan, late, terms, (attended, query_grad))
    return (
        attended.reshape(rows, heads, width),
        query_grad.reshape(rows, heads, width),
        key_grad.reshape(rows, 1, width),
        value_grad.reshape(rows, 1, width),
    )


def solution(mesh):
    rows = P(("dp", "ctx"), "tp", None)
    return jax.shard_map(
        on_device,
        mesh=mesh,
        in_specs=(rows, rows, rows, rows, P("dp"), P("dp", None)),
        out_specs=(rows, rows, rows, rows),
        check_vma=False,
    )
```

```python
import functools
import jax
import jax.numpy as jnp
from jax import lax
from jax.experimental import pallas as pl
from jax.experimental.pallas import tpu as pltpu
from jax.sharding import PartitionSpec as P

MASKED = -1e30
LOG2_E = 1.4426950408889634
VMEM_LIMIT = 32 * 1024 * 1024


def dot(a, b, contract):
    return lax.dot_general(a, b, ((contract[0], contract[1]), ((), ())), preferred_element_type=jnp.float32)


def attend_block(first_row, ends, q, g, k, v, reach, heads, scale):
    cols = q.shape[0]
    key_rows = k.shape[0]
    token = lax.broadcasted_iota(jnp.int32, (1, cols), 1) // heads
    query_pos = first_row + token
    doc_start = jnp.zeros((1, cols), jnp.int32)
    for end in ends:
        doc_start = jnp.maximum(doc_start, jnp.where(end <= query_pos, end, 0))
    low = doc_start - (first_row - reach)
    raw = dot(k, q, ((1,), (1,)))
    index = lax.broadcasted_iota(jnp.int32, (key_rows, cols), 0)
    allowed = index >= low
    allowed_late = jnp.logical_and(allowed[reach:], index[reach:] - reach <= token)
    raw = jnp.concatenate(
        [jnp.where(allowed[:reach], raw[:reach], MASKED), jnp.where(allowed_late, raw[reach:], MASKED)], axis=0
    )
    row_max = jnp.max(raw, axis=0, keepdims=True)
    weights = jnp.exp2((raw - row_max) * (scale * LOG2_E))
    inverse = 1.0 / jnp.sum(weights, axis=0, keepdims=True)
    attended_t = (dot(v, weights.astype(jnp.bfloat16), ((0,), (0,))) * inverse).astype(jnp.bfloat16)
    attended = attended_t.T
    g_t = g.T.astype(jnp.float32)
    delta = jnp.sum(g_t * attended_t.astype(jnp.float32), axis=0, keepdims=True)
    probs = weights * inverse
    products = dot(v, g, ((1,), (1,)))
    slopes = (probs * (products - delta)).astype(jnp.bfloat16)
    value_part = dot(probs.astype(jnp.bfloat16), g, ((1,), (0,)))
    key_part = dot(slopes, q, ((1,), (0,))) * scale
    query_grad = (dot(k, slopes, ((0,), (0,))) * scale).astype(jnp.bfloat16).T
    return attended, query_grad, key_part, value_part


class Plan:
    def __init__(self, n, rows, heads, width, ndocs):
        self.n, self.rows, self.heads, self.width, self.ndocs = n, rows, heads, width, ndocs
        self.back = n // 2
        self.block = rows // n
        self.cols = self.block * heads
        self.reach = self.back * rows
        self.scale = width ** (-0.5)
        self.window_ranges = self.back + 3
        self.grad_rows = 2 * (self.back + 1) * self.block

    def is_middle(self, own):
        return jnp.logical_or(own == self.back - 1, own == self.back)

    def first_range(self, own):
        return jnp.maximum(own - self.back, 0)

    def ends(self, meta):
        return [meta[1 + i] for i in range(self.ndocs)]

    def slot(self, meta, loader, owner):
        return meta[1 + self.ndocs + loader * self.n + owner]

    def cost(self, blocks):
        return pl.CostEstimate(
            flops=14 * blocks * self.cols * (self.reach + self.block) * self.width * 8,
            bytes_accessed=blocks * self.cols * self.width * 16,
            transcendentals=blocks * self.cols * (self.reach + self.block),
        )


def fill_window(plan, own, refs, k_win, v_win):
    rows = plan.rows
    empty = jnp.zeros((rows, plan.width), k_win.dtype)
    for place in (0, 1):
        k_win[pl.ds(place * rows, rows), :] = empty
        v_win[pl.ds(place * rows, rows), :] = empty
    for i, ref in enumerate(refs):
        place = plan.back + 1 - i
        if i == plan.back:
            place = jnp.where(own == plan.back - 1, plan.back + 2, place)
        to = pl.ds(pl.multiple_of(place * rows, rows), rows)
        k_win[to, :] = ref[pl.ds(0, rows), :]
        v_win[to, :] = ref[pl.ds(rows, rows), :]


def attend_at(plan, meta, loader, slot, q, g, k_win, v_win):
    start = (loader - meta[0] + 1) * plan.rows + slot * plan.block
    keys_here = pl.ds(pl.multiple_of(start, plan.block), plan.reach + plan.block)
    out = attend_block(
        loader * plan.rows + slot * plan.block, plan.ends(meta), q, g, k_win[keys_here, :], v_win[keys_here, :],
        plan.reach, plan.heads, plan.scale,
    )
    return keys_here, out


def pack_kernel(plan, meta, q_ref, g_ref, *refs):
    blocks, sems = refs[: plan.n], refs[plan.n]
    own = meta[0]
    copies = []
    for apart, block in enumerate(blocks):
        slot = plan.slot(meta, own, own ^ apart)
        at = pl.ds(pl.multiple_of(slot * plan.cols, plan.cols), plan.cols)
        copies.append(pltpu.make_async_copy(q_ref.at[at, :], block.at[0], sems.at[apart, 0]))
        copies.append(pltpu.make_async_copy(g_ref.at[at, :], block.at[1], sems.at[apart, 1]))
    for copy in copies:
        copy.start()
    for copy in copies:
        copy.wait()


def first_kernel(plan, apart, meta, qg, *refs):
    kv_refs, (pay_ref, grad_ref, k_win, v_win) = refs[:-4], refs[-4:]
    own = meta[0]
    slot = plan.slot(meta, own, own ^ apart)
    fill_window(plan, own, kv_refs, k_win, v_win)
    _, (attended, query_grad, key_part, value_part) = attend_at(
        plan, meta, own, slot, qg[0], qg[1], k_win, v_win
    )
    pay_ref[pl.ds(0, plan.cols), :] = attended
    pay_ref[pl.ds(plan.cols, plan.cols), :] = query_grad
    grad_ref[:, : plan.width] = key_part
    grad_ref[:, plan.width :] = value_part


def last_kernel(plan, first, items, meta, *refs):
    n, width, rows, block = plan.n, plan.width, plan.rows, plan.block
    qg_refs, (got_ref, first_grad), refs = refs[: len(items)], refs[len(items) : len(items) + 2], refs[len(items) + 2 :]
    outs = len(items) + n - 1 + 4
    kv_refs, refs = refs[:-outs], refs[-outs:]
    pay_refs, grad_refs, (k_win, v_win, acc, qg) = refs[: len(items)], refs[len(items) : -4], refs[-4:]
    grad_refs = [grad_refs[0], pay_refs[items.index(1)].at[pl.ds(2 * plan.cols, plan.grad_rows), :], *grad_refs[1:]]
    step = pl.program_id(0)
    own = meta[0]
    middle = plan.is_middle(own)

    @pl.when(step == 0)
    def _():
        fill_window(plan, own, kv_refs, k_win, v_win)
        acc[...] = jnp.zeros_like(acc)
        slot = plan.slot(meta, own, own ^ first)
        keys_here = pl.ds(pl.multiple_of(rows + slot * block, block), plan.reach + block)
        acc[keys_here, :] = first_grad[...]

    for i, item in enumerate(items):

        @pl.when(step == i)
        def _():
            loader, owner, source = own, own ^ item, qg_refs[i]
            if item == n - 1:
                loader, owner, source = jnp.where(middle, owner, own), jnp.where(middle, own, owner), qg

                @pl.when(middle)
                def _():
                    qg[...] = got_ref[...]

                @pl.when(jnp.logical_not(middle))
                def _():
                    qg[...] = qg_refs[i][...]

            slot = plan.slot(meta, loader, owner)
            keys_here, (attended, query_grad, key_part, value_part) = attend_at(
                plan, meta, loader, slot, source[0], source[1], k_win, v_win
            )
            acc[keys_here, :width] = acc[keys_here, :width] + key_part
            acc[keys_here, width:] = acc[keys_here, width:] + value_part
            pay_refs[i][pl.ds(0, plan.cols), :] = attended
            pay_refs[i][pl.ds(plan.cols, plan.cols), :] = query_grad

    @pl.when(step == len(items) - 1)
    def _():
        def of_range(i, carry):
            key_range = plan.first_range(own) + i
            at = (key_range - own + plan.back + 1) * rows
            for apart in range(n):
                slot = plan.slot(meta, key_range, own ^ apart)
                part = acc[pl.ds(pl.multiple_of(at + slot * block, block), block), :]
                part = part.astype(grad_refs[apart].dtype)
                to = pl.multiple_of(i * block, block)
                grad_refs[apart][pl.ds(to, block), :] = part[:, :width]
                to = pl.multiple_of(i * block + plan.grad_rows // 2, block)
                grad_refs[apart][pl.ds(to, block), :] = part[:, width:]
            return carry

        lax.fori_loop(0, plan.back + 1, of_range, 0)


def spec_of(space):
    return pl.BlockSpec(memory_space=space)


def kernel_call(body, name, operands, spaces, out_shape, scratch, **more):
    return pl.pallas_call(
        body,
        out_shape=out_shape,
        in_specs=[spec_of(space) for space in spaces],
        compiler_params=pltpu.CompilerParams(vmem_limit_bytes=VMEM_LIMIT),
        scratch_shapes=scratch,
        name=name,
        **more,
    )(*operands)


def pack(plan, meta, q, g):
    out_shape = [jax.ShapeDtypeStruct((2, plan.cols, plan.width), jnp.bfloat16)] * plan.n
    q, g = (pltpu.with_memory_space_constraint(x, pltpu.HBM) for x in (q, g))
    return kernel_call(
        functools.partial(pack_kernel, plan), "pack", (meta, q, g), [pltpu.SMEM] + [pl.ANY] * 2, out_shape,
        [pltpu.SemaphoreType.DMA((plan.n, 2))],
        out_specs=[spec_of(pltpu.VMEM)] * len(out_shape),
    )


def attend_first(plan, apart, meta, qg, kv_list):
    window = pltpu.VMEM((plan.window_ranges * plan.rows, plan.width), jnp.bfloat16)
    out_shape = [
        jax.ShapeDtypeStruct((2 * plan.cols, plan.width), jnp.bfloat16),
        jax.ShapeDtypeStruct((plan.reach + plan.block, 2 * plan.width), jnp.float32),
    ]
    operands = (meta, qg, *kv_list)
    return kernel_call(
        functools.partial(first_kernel, plan, apart), "attend_first", operands,
        [pltpu.SMEM] + [pltpu.VMEM] * (len(operands) - 1), out_shape, [window, window],
        out_specs=[spec_of(pltpu.VMEM)] * 2, cost_estimate=plan.cost(1),
    )


def attend_last(plan, first, items, meta, qg_list, got, first_grad, kv_list):
    n = plan.n
    rows = plan.window_ranges * plan.rows
    window = pltpu.VMEM((rows, plan.width), jnp.bfloat16)
    sum_rows = (2 * plan.back + 2) * plan.rows
    block = (2, plan.cols, plan.width)
    pay_rows = [2 * plan.cols + (plan.grad_rows if x == 1 else 0) for x in items]
    out_shape = [jax.ShapeDtypeStruct((size, plan.width), jnp.bfloat16) for size in pay_rows]
    grads = (plan.grad_rows, plan.width)
    out_shape += [jax.ShapeDtypeStruct(grads, jnp.bfloat16 if i else jnp.float32) for i in range(n - 1)]
    operands = (meta, *qg_list, got, first_grad, *kv_list)
    return kernel_call(
        functools.partial(last_kernel, plan, first, items), "attend_last", operands,
        [pltpu.SMEM] + [pltpu.VMEM] * (len(operands) - 1), out_shape,
        [window, window, pltpu.VMEM((sum_rows, 2 * plan.width), jnp.float32), pltpu.VMEM(block, jnp.bfloat16)],
        out_specs=[spec_of(pltpu.VMEM)] * len(out_shape), cost_estimate=plan.cost(len(items)), grid=(len(items),),
    )


def place_kernel(plan, late, *refs):
    n, cols, width = plan.n, plan.cols, plan.width
    own = lax.axis_index("ctx")
    middle = plan.is_middle(own)

    def copies(i, x, pay, attended, query_grad, sems):
        to = pl.ds(pl.multiple_of((own ^ x) * cols, cols), cols)
        return [
            pltpu.make_async_copy(pay.at[pl.ds(0, cols), :], attended.at[to, :], sems.at[i, 0]),
            pltpu.make_async_copy(pay.at[pl.ds(cols, cols), :], query_grad.at[to, :], sems.at[i, 1]),
        ]

    if late:
        pay_refs, grad_refs, refs = refs[: len(late)], refs[len(late) : len(late) + n - 1], refs[len(late) + n - 1 :]
        grad_refs = [grad_refs[0], pay_refs[late.index(1)].at[pl.ds(2 * cols, plan.grad_rows), :], *grad_refs[1:]]
        _, _, attended, query_grad, key_grad, value_grad, acc, sums, sems, sum_sems = refs
        items = late
    else:
        items = (n // 2, 0, n - 1)
        pay_refs, (attended, query_grad, sems) = refs[:3], refs[3:]

    def each(act):
        for i, item in enumerate(items):
            here = middle if not late else jnp.logical_not(middle)

            def run():
                for copy in copies(i, item, pay_refs[i], attended, query_grad, sems):
                    act(copy)

            if item == n - 1:
                pl.when(here)(run)
            else:
                run()

    each(lambda copy: copy.start())
    if late:
        acc[...] = jnp.zeros_like(acc)
        for x in range(n):
            for i in range(plan.back + 1):
                at = (plan.first_range(own ^ x) + i) * plan.block
                to = pl.ds(pl.multiple_of(at, plan.block), plan.block)
                for part in range(2):
                    term = grad_refs[x][pl.ds(i * plan.block + part * plan.grad_rows // 2, plan.block), :]
                    acc[part, to, :] = acc[part, to, :] + term.astype(jnp.float32)
        for i, ref in enumerate((key_grad, value_grad)):
            sums[i] = acc[i].astype(jnp.bfloat16)
            pltpu.make_async_copy(sums.at[i], ref, sum_sems.at[i]).start()
        for i, ref in enumerate((key_grad, value_grad)):
            pltpu.make_async_copy(sums.at[i], ref, sum_sems.at[i]).wait()
    each(lambda copy: copy.wait())


def place(plan, payloads, late=(), grads=(), filled=()):
    big = jax.ShapeDtypeStruct((plan.rows * plan.heads, plan.width), jnp.bfloat16)
    small = jax.ShapeDtypeStruct((plan.rows, plan.width), jnp.bfloat16)
    out_shape, scratch = [big, big], [pltpu.SemaphoreType.DMA((len(payloads), 2))]
    if late:
        out_shape += [small, small]
        scratch = [
            pltpu.VMEM((2, plan.rows, plan.width), jnp.float32),
            pltpu.VMEM((2, plan.rows, plan.width), jnp.bfloat16),
            *scratch,
            pltpu.SemaphoreType.DMA((2,)),
        ]
    at = len(payloads) + len(grads)
    return kernel_call(
        functools.partial(place_kernel, plan, late), "place_last" if late else "place_first",
        (*payloads, *grads, *filled),
        [pltpu.VMEM] * (len(payloads) + len(grads)) + [pl.ANY] * len(filled),
        out_shape, scratch,
        out_specs=[spec_of(pl.ANY)] * len(out_shape),
        input_output_aliases={at: 0, at + 1: 1} if late else {},
        cost_estimate=plan.cost(len(payloads)),
    )


def on_device(query, keys, values, output_gradient, doc_lengths, block_owner):
    n = lax.axis_size("ctx")
    own = lax.axis_index("ctx")
    rows, heads, width = query.shape
    plan = Plan(n, rows, heads, width, doc_lengths.shape[0])

    def permuted(array, pairs):
        return lax.ppermute(array, "ctx", pairs)

    def across(array, bits):
        return permuted(array, [(i, i ^ bits) for i in range(n)])

    kv = jnp.concatenate([keys.reshape(rows, width), values.reshape(rows, width)])
    kv_list = [kv]
    for by in range(1, plan.back + 1):
        pairs = [(i, i + by) for i in range(n - by)]
        kv_list.append(permuted(kv, pairs + [(n // 2, n // 2 - 1)] if by == plan.back else pairs))

    owners = jnp.arange(n, dtype=jnp.int32)
    match = block_owner[:, None, :] == owners[None, :, None]
    table = jnp.sum(jnp.where(match, owners, 0), axis=2)
    meta = jnp.concatenate(
        [own.reshape(1).astype(jnp.int32), jnp.cumsum(doc_lengths).astype(jnp.int32), table.reshape(-1)]
    )

    blocks = pack(plan, meta, query.reshape(rows * heads, width), output_gradient.reshape(rows * heads, width))
    middle = (n // 2 - 1, n // 2)
    got = permuted(blocks[n - 1], [middle, middle[::-1]])
    first = n // 2
    first_pay, first_grad = attend_first(plan, first, meta, blocks[first], kv_list)
    first_pay = across(first_pay, first)
    sent = tuple(x for x in range(n - 1, 0, -1) if x != first)
    items = (*sent, 0)
    out = attend_last(plan, first, items, meta, [blocks[x] for x in items], got, first_grad, kv_list)
    pays, grads = out[: len(items)], out[len(items) :]
    late = [permuted(pays[0], [(i, i ^ (n - 1)) for i in range(n) if i not in middle])]
    late += [across(pay, x) for x, pay in zip(sent[1:], pays[1:])]
    grads = [across(grad, i + 1) if i else grad for i, grad in enumerate(grads)]
    filled = place(plan, [first_pay, pays[-1], pays[0]])
    attended, query_grad, key_grad, value_grad = place(plan, late, sent, grads, filled)
    return (
        attended.reshape(rows, heads, width),
        query_grad.reshape(rows, heads, width),
        key_grad.reshape(rows, 1, width),
        value_grad.reshape(rows, 1, width),
    )


def solution(mesh):
    rows = P(("dp", "ctx"), "tp", None)
    return jax.shard_map(
        on_device,
        mesh=mesh,
        in_specs=(rows, rows, rows, rows, P("dp"), P("dp", None)),
        out_specs=(rows, rows, rows, rows),
        check_vma=False,
    )
```

```python
import functools
import jax
import jax.numpy as jnp
from jax import lax
from jax.experimental import pallas as pl
from jax.experimental.pallas import tpu as pltpu
from jax.sharding import PartitionSpec as P

MASKED = -1e30
LOG2_E = 1.4426950408889634
VMEM_LIMIT = 32 * 1024 * 1024


def dot(a, b, contract):
    return lax.dot_general(a, b, ((contract[0], contract[1]), ((), ())), preferred_element_type=jnp.float32)


def attend_block(first_row, ends, q, g, k, v, reach, heads, scale):
    cols = q.shape[0]
    key_rows = k.shape[0]
    token = lax.broadcasted_iota(jnp.int32, (1, cols), 1) // heads
    query_pos = first_row + token
    doc_start = jnp.zeros((1, cols), jnp.int32)
    for end in ends:
        doc_start = jnp.maximum(doc_start, jnp.where(end <= query_pos, end, 0))
    low = doc_start - (first_row - reach)
    raw = dot(k, q, ((1,), (1,)))
    index = lax.broadcasted_iota(jnp.int32, (key_rows, cols), 0)
    allowed = index >= low
    allowed_late = jnp.logical_and(allowed[reach:], index[reach:] - reach <= token)
    raw = jnp.concatenate(
        [jnp.where(allowed[:reach], raw[:reach], MASKED), jnp.where(allowed_late, raw[reach:], MASKED)], axis=0
    )
    row_max = jnp.max(raw, axis=0, keepdims=True)
    weights = jnp.exp2((raw - row_max) * (scale * LOG2_E))
    inverse = 1.0 / jnp.sum(weights, axis=0, keepdims=True)
    attended_t = (dot(v, weights.astype(jnp.bfloat16), ((0,), (0,))) * inverse).astype(jnp.bfloat16)
    attended = attended_t.T
    g_t = g.T.astype(jnp.float32)
    delta = jnp.sum(g_t * attended_t.astype(jnp.float32), axis=0, keepdims=True)
    probs = weights * inverse
    products = dot(v, g, ((1,), (1,)))
    slopes = (probs * (products - delta)).astype(jnp.bfloat16)
    value_part = dot(probs.astype(jnp.bfloat16), g, ((1,), (0,)))
    key_part = dot(slopes, q, ((1,), (0,))) * scale
    query_grad = (dot(k, slopes, ((0,), (0,))) * scale).astype(jnp.bfloat16).T
    return attended, query_grad, key_part, value_part


class Plan:
    def __init__(self, n, rows, heads, width, ndocs):
        self.n, self.rows, self.heads, self.width, self.ndocs = n, rows, heads, width, ndocs
        self.back = n // 2
        self.block = rows // n
        self.cols = self.block * heads
        self.reach = self.back * rows
        self.scale = width ** (-0.5)
        self.window_ranges = self.back + 3
        self.grad_rows = 2 * (self.back + 1) * self.block

    def is_middle(self, own):
        return jnp.logical_or(own == self.back - 1, own == self.back)

    def first_range(self, own):
        return jnp.maximum(own - self.back, 0)

    def ends(self, meta):
        return [meta[1 + i] for i in range(self.ndocs)]

    def slot(self, meta, loader, owner):
        return meta[1 + self.ndocs + loader * self.n + owner]

    def cost(self, blocks):
        return pl.CostEstimate(
            flops=14 * blocks * self.cols * (self.reach + self.block) * self.width * 8,
            bytes_accessed=blocks * self.cols * self.width * 16,
            transcendentals=blocks * self.cols * (self.reach + self.block),
        )


def fill_window(plan, own, refs, k_win, v_win):
    rows = plan.rows
    empty = jnp.zeros((rows, plan.width), k_win.dtype)
    for place in (0, 1):
        k_win[pl.ds(place * rows, rows), :] = empty
        v_win[pl.ds(place * rows, rows), :] = empty
    k_win[pl.ds((plan.back + 1) * rows, rows), :] = refs[0][pl.ds(0, rows), :]
    v_win[pl.ds((plan.back + 1) * rows, rows), :] = refs[0][pl.ds(rows, rows), :]
    for i in range(1, plan.back + 1):
        place = plan.back + 1 - i
        if i == plan.back:
            place = jnp.where(own == plan.back - 1, plan.back + 2, place)
        to = pl.ds(pl.multiple_of(place * rows, rows), rows)
        k_win[to, :] = refs[2 * i - 1][...]
        v_win[to, :] = refs[2 * i][...]


def attend_at(plan, meta, loader, slot, q, g, k_win, v_win):
    start = (loader - meta[0] + 1) * plan.rows + slot * plan.block
    keys_here = pl.ds(pl.multiple_of(start, plan.block), plan.reach + plan.block)
    out = attend_block(
        loader * plan.rows + slot * plan.block, plan.ends(meta), q, g, k_win[keys_here, :], v_win[keys_here, :],
        plan.reach, plan.heads, plan.scale,
    )
    return keys_here, out


def pack_kernel(plan, meta, q_ref, g_ref, k_ref, v_ref, *refs):
    blocks, (kv, sems, kv_sems) = refs[: plan.n], refs[plan.n :]
    own = meta[0]
    copies = []
    for apart, block in enumerate(blocks):
        slot = plan.slot(meta, own, own ^ apart)
        at = pl.ds(pl.multiple_of(slot * plan.cols, plan.cols), plan.cols)
        copies.append(pltpu.make_async_copy(q_ref.at[at, :], block.at[0], sems.at[apart, 0]))
        copies.append(pltpu.make_async_copy(g_ref.at[at, :], block.at[1], sems.at[apart, 1]))
    for i, ref in enumerate((k_ref, v_ref)):
        to = kv.at[pl.ds(i * plan.rows, plan.rows), :]
        copies.append(pltpu.make_async_copy(ref, to, kv_sems.at[i]))
    for copy in copies:
        copy.start()
    for copy in copies:
        copy.wait()


def first_kernel(plan, apart, meta, qg, *refs):
    kv_refs, (pay_ref, grad_ref, k_win, v_win) = refs[:-4], refs[-4:]
    own = meta[0]
    slot = plan.slot(meta, own, own ^ apart)
    fill_window(plan, own, kv_refs, k_win, v_win)
    _, (attended, query_grad, key_part, value_part) = attend_at(
        plan, meta, own, slot, qg[0], qg[1], k_win, v_win
    )
    put_rows(plan, pay_ref, attended, query_grad)
    grad_ref[:, : plan.width] = key_part
    grad_ref[:, plan.width :] = value_part


def add_parts(plan, acc, keys_here, key_part, value_part):
    acc[keys_here, : plan.width] = acc[keys_here, : plan.width] + key_part
    acc[keys_here, plan.width :] = acc[keys_here, plan.width :] + value_part


def put_rows(plan, pay_ref, attended, query_grad):
    pay_ref[pl.ds(0, plan.cols), :] = attended
    pay_ref[pl.ds(plan.cols, plan.cols), :] = query_grad


def next_kernel(plan, first, items, meta, *refs):
    qg_refs, first_grad, refs = refs[: len(items)], refs[len(items)], refs[len(items) + 1 :]
    outs = len(items) + 3
    kv_refs, pay_refs, (acc, k_win, v_win) = refs[:-outs], refs[-outs:-3], refs[-3:]
    step = pl.program_id(0)
    own = meta[0]

    @pl.when(step == 0)
    def _():
        fill_window(plan, own, kv_refs, k_win, v_win)
        acc[...] = jnp.zeros_like(acc)
        slot = plan.slot(meta, own, own ^ first)
        start = pl.multiple_of(plan.rows + slot * plan.block, plan.block)
        acc[pl.ds(start, plan.reach + plan.block), :] = first_grad[...]

    for i, item in enumerate(items):

        @pl.when(step == i)
        def _():
            slot = plan.slot(meta, own, own ^ item)
            keys_here, (attended, query_grad, *parts) = attend_at(
                plan, meta, own, slot, qg_refs[i][0], qg_refs[i][1], k_win, v_win
            )
            add_parts(plan, acc, keys_here, *parts)
            put_rows(plan, pay_refs[i], attended, query_grad)


def last_kernel(plan, meta, *refs):
    n, width, block, rows = plan.n, plan.width, plan.block, plan.rows
    qg_ref, got_ref, near_ref, acc_ref, refs = *refs[:4], refs[4:]
    outs = 2 + n - 1 + 4
    kv_refs, (pay_ref, near_pay_ref, *grad_refs), (k_win, v_win, acc, qg) = refs[:-outs], refs[-outs:-4], refs[-4:]
    own = meta[0]
    middle = plan.is_middle(own)

    @pl.when(middle)
    def _():
        qg[...] = got_ref[...]

    @pl.when(jnp.logical_not(middle))
    def _():
        qg[...] = qg_ref[...]

    fill_window(plan, own, kv_refs, k_win, v_win)
    size = acc_ref.shape[0]
    acc[pl.ds(0, size), :] = acc_ref[...]
    acc[pl.ds(size, acc.shape[0] - size), :] = jnp.zeros((acc.shape[0] - size, 2 * width), jnp.float32)
    loader, owner = jnp.where(middle, own ^ (n - 1), own), jnp.where(middle, own, own ^ (n - 1))
    keys_here, (attended, query_grad, *parts) = attend_at(
        plan, meta, loader, plan.slot(meta, loader, owner), qg[0], qg[1], k_win, v_win
    )
    add_parts(plan, acc, keys_here, *parts)
    put_rows(plan, pay_ref, attended, query_grad)

    near_pay_ref[pl.ds(0, 2 * plan.cols), :] = near_ref[...]
    grad_refs = [grad_refs[0], near_pay_ref.at[pl.ds(2 * plan.cols, plan.grad_rows), :], *grad_refs[1:]]

    def of_range(i, carry):
        key_range = plan.first_range(own) + i
        at = (key_range - own + plan.back + 1) * rows
        for apart in range(n):
            slot = plan.slot(meta, key_range, own ^ apart)
            part = acc[pl.ds(pl.multiple_of(at + slot * block, block), block), :].astype(grad_refs[apart].dtype)
            to = pl.multiple_of(i * block, block)
            grad_refs[apart][pl.ds(to, block), :] = part[:, :width]
            to = pl.multiple_of(i * block + plan.grad_rows // 2, block)
            grad_refs[apart][pl.ds(to, block), :] = part[:, width:]
        return carry

    lax.fori_loop(0, plan.back + 1, of_range, 0)


def spec_of(space):
    return pl.BlockSpec(memory_space=space)


def kernel_call(body, name, operands, spaces, out_shape, scratch, **more):
    return pl.pallas_call(
        body,
        out_shape=out_shape,
        in_specs=[spec_of(space) for space in spaces],
        compiler_params=pltpu.CompilerParams(vmem_limit_bytes=VMEM_LIMIT),
        scratch_shapes=scratch,
        name=name,
        **more,
    )(*operands)


def pack(plan, meta, *operands):
    out_shape = [jax.ShapeDtypeStruct((2, plan.cols, plan.width), jnp.bfloat16)] * plan.n
    out_shape.append(jax.ShapeDtypeStruct((2 * plan.rows, plan.width), jnp.bfloat16))
    operands = [pltpu.with_memory_space_constraint(x, pltpu.HBM) for x in operands]
    return kernel_call(
        functools.partial(pack_kernel, plan), "pack", (meta, *operands), [pltpu.SMEM] + [pl.ANY] * 4, out_shape,
        [pltpu.SemaphoreType.DMA((plan.n, 2)), pltpu.SemaphoreType.DMA((2,))],
        out_specs=[spec_of(pltpu.VMEM)] * len(out_shape),
    )


def attend_first(plan, apart, meta, qg, kv_list):
    window = pltpu.VMEM((plan.window_ranges * plan.rows, plan.width), jnp.bfloat16)
    out_shape = [
        jax.ShapeDtypeStruct((2 * plan.cols, plan.width), jnp.bfloat16),
        jax.ShapeDtypeStruct((plan.reach + plan.block, 2 * plan.width), jnp.float32),
    ]
    operands = (meta, qg, *kv_list)
    return kernel_call(
        functools.partial(first_kernel, plan, apart), "attend_first", operands,
        [pltpu.SMEM] + [pltpu.VMEM] * (len(operands) - 1), out_shape, [window, window],
        out_specs=[spec_of(pltpu.VMEM)] * 2, cost_estimate=plan.cost(1),
    )


def attend_next(plan, first, items, meta, qg_list, first_grad, kv_list):
    rows = plan.window_ranges * plan.rows
    window = pltpu.VMEM((rows, plan.width), jnp.bfloat16)
    out_shape = [jax.ShapeDtypeStruct((2 * plan.cols, plan.width), jnp.bfloat16)] * len(items)
    out_shape.append(jax.ShapeDtypeStruct((rows, 2 * plan.width), jnp.float32))
    operands = (meta, *qg_list, first_grad, *kv_list)
    return kernel_call(
        functools.partial(next_kernel, plan, first, items), "attend_next", operands,
        [pltpu.SMEM] + [pltpu.VMEM] * (len(operands) - 1), out_shape, [window, window],
        out_specs=[spec_of(pltpu.VMEM)] * len(out_shape), cost_estimate=plan.cost(len(items)), grid=(len(items),),
    )


def attend_last(plan, meta, qg, got, near_pay, sums, kv_list):
    n = plan.n
    window = pltpu.VMEM((plan.window_ranges * plan.rows, plan.width), jnp.bfloat16)
    sum_rows = (2 * plan.back + 2) * plan.rows
    out_shape = [
        jax.ShapeDtypeStruct((size, plan.width), jnp.bfloat16) for size in (2 * plan.cols, 2 * plan.cols + plan.grad_rows)
    ]
    grads = (plan.grad_rows, plan.width)
    out_shape += [jax.ShapeDtypeStruct(grads, jnp.bfloat16 if i else jnp.float32) for i in range(n - 1)]
    operands = (meta, qg, got, near_pay, sums, *kv_list)
    return kernel_call(
        functools.partial(last_kernel, plan), "attend_last", operands,
        [pltpu.SMEM] + [pltpu.VMEM] * (len(operands) - 1), out_shape,
        [window, window, pltpu.VMEM((sum_rows, 2 * plan.width), jnp.float32), pltpu.VMEM(qg.shape, jnp.bfloat16)],
        out_specs=[spec_of(pltpu.VMEM)] * len(out_shape), cost_estimate=plan.cost(1),
    )


def place_kernel(plan, late, *refs):
    n, cols, width = plan.n, plan.cols, plan.width
    own = lax.axis_index("ctx")
    middle = plan.is_middle(own)

    def copies(i, x, pay, attended, query_grad, sems):
        to = pl.ds(pl.multiple_of((own ^ x) * cols, cols), cols)
        return [
            pltpu.make_async_copy(pay.at[pl.ds(0, cols), :], attended.at[to, :], sems.at[i, 0]),
            pltpu.make_async_copy(pay.at[pl.ds(cols, cols), :], query_grad.at[to, :], sems.at[i, 1]),
        ]

    if late:
        pay_refs, grad_refs, refs = refs[: len(late)], refs[len(late) : len(late) + n - 1], refs[len(late) + n - 1 :]
        grad_refs = [grad_refs[0], pay_refs[late.index(1)].at[pl.ds(2 * cols, plan.grad_rows), :], *grad_refs[1:]]
        _, _, attended, query_grad, key_grad, value_grad, acc, sums, sems, sum_sems = refs
        items = late
    else:
        items = (n // 2, 0, n - 1)
        pay_refs, (attended, query_grad, sems) = refs[:3], refs[3:]

    def each(act):
        for i, item in enumerate(items):
            here = middle if not late else jnp.logical_not(middle)

            def run():
                for copy in copies(i, item, pay_refs[i], attended, query_grad, sems):
                    act(copy)

            if item == n - 1:
                pl.when(here)(run)
            else:
                run()

    each(lambda copy: copy.start())
    if late:
        acc[...] = jnp.zeros_like(acc)
        for x in range(n):
            for i in range(plan.back + 1):
                at = (plan.first_range(own ^ x) + i) * plan.block
                to = pl.ds(pl.multiple_of(at, plan.block), plan.block)
                for part in range(2):
                    term = grad_refs[x][pl.ds(i * plan.block + part * plan.grad_rows // 2, plan.block), :]
                    acc[part, to, :] = acc[part, to, :] + term.astype(jnp.float32)
        for i, ref in enumerate((key_grad, value_grad)):
            sums[i] = acc[i].astype(jnp.bfloat16)
            pltpu.make_async_copy(sums.at[i], ref, sum_sems.at[i]).start()
        for i, ref in enumerate((key_grad, value_grad)):
            pltpu.make_async_copy(sums.at[i], ref, sum_sems.at[i]).wait()
    each(lambda copy: copy.wait())


def place(plan, payloads, late=(), grads=(), filled=()):
    big = jax.ShapeDtypeStruct((plan.rows * plan.heads, plan.width), jnp.bfloat16)
    small = jax.ShapeDtypeStruct((plan.rows, plan.width), jnp.bfloat16)
    out_shape, scratch = [big, big], [pltpu.SemaphoreType.DMA((len(payloads), 2))]
    if late:
        out_shape += [small, small]
        scratch = [
            pltpu.VMEM((2, plan.rows, plan.width), jnp.float32),
            pltpu.VMEM((2, plan.rows, plan.width), jnp.bfloat16),
            *scratch,
            pltpu.SemaphoreType.DMA((2,)),
        ]
    at = len(payloads) + len(grads)
    return kernel_call(
        functools.partial(place_kernel, plan, late), "place_last" if late else "place_first",
        (*payloads, *grads, *filled),
        [pltpu.VMEM] * (len(payloads) + len(grads)) + [pl.ANY] * len(filled),
        out_shape, scratch,
        out_specs=[spec_of(pl.ANY)] * len(out_shape),
        input_output_aliases={at: 0, at + 1: 1} if late else {},
        cost_estimate=plan.cost(len(payloads)),
    )


def on_device(query, keys, values, output_gradient, doc_lengths, block_owner):
    n = lax.axis_size("ctx")
    own = lax.axis_index("ctx")
    rows, heads, width = query.shape
    plan = Plan(n, rows, heads, width, doc_lengths.shape[0])

    def permuted(array, pairs):
        return lax.ppermute(array, "ctx", pairs)

    def across(array, bits):
        return permuted(array, [(i, i ^ bits) for i in range(n)])

    k = keys.reshape(rows, width)
    v = values.reshape(rows, width)
    kv_list = []
    for by in range(1, plan.back + 1):
        pairs = [(i, i + by) for i in range(n - by)]
        if by == plan.back:
            pairs.append((n // 2, n // 2 - 1))
        kv_list += [permuted(k, pairs), permuted(v, pairs)]

    owners = jnp.arange(n, dtype=jnp.int32)
    match = block_owner[:, None, :] == owners[None, :, None]
    table = jnp.sum(jnp.where(match, owners, 0), axis=2)
    meta = jnp.concatenate(
        [own.reshape(1).astype(jnp.int32), jnp.cumsum(doc_lengths).astype(jnp.int32), table.reshape(-1)]
    )

    q, g = (x.reshape(rows * heads, width) for x in (query, output_gradient))
    *blocks, kv = pack(plan, meta, q, g, k, v)
    kv_list = [kv, *kv_list]
    middle = (n // 2 - 1, n // 2)
    got = permuted(blocks[n - 1], [middle, middle[::-1]])
    first = n // 2
    first_pay, first_grad = attend_first(plan, first, meta, blocks[first], kv_list)
    first_pay = across(first_pay, first)
    items = tuple(x for x in range(n - 1) if x != first)
    *pays, sums = attend_next(plan, first, items, meta, [blocks[x] for x in items], first_grad, kv_list)
    pays = dict(zip(items, pays))
    last_pay, pays[1], *grads = attend_last(plan, meta, blocks[n - 1], got, pays[1], sums, kv_list)
    late = [permuted(last_pay, [(i, i ^ (n - 1)) for i in range(n) if i not in middle])]
    sent = (n - 1, *items[1:])
    late += [across(pays[x], x) for x in sent[1:]]
    grads = [across(grad, i + 1) if i else grad for i, grad in enumerate(grads)]
    filled = place(plan, [first_pay, pays[0], last_pay])
    attended, query_grad, key_grad, value_grad = place(plan, late, sent, grads, filled)
    return (
        attended.reshape(rows, heads, width),
        query_grad.reshape(rows, heads, width),
        key_grad.reshape(rows, 1, width),
        value_grad.reshape(rows, 1, width),
    )


def solution(mesh):
    rows = P(("dp", "ctx"), "tp", None)
    return jax.shard_map(
        on_device,
        mesh=mesh,
        in_specs=(rows, rows, rows, rows, P("dp"), P("dp", None)),
        out_specs=(rows, rows, rows, rows),
        check_vma=False,
    )
```

```python
import functools
import jax
import jax.numpy as jnp
from jax import lax
from jax.experimental import pallas as pl
from jax.experimental.pallas import tpu as pltpu
from jax.sharding import PartitionSpec as P

MASKED = -1e30
LOG2_E = 1.4426950408889634
VMEM_LIMIT = 32 * 1024 * 1024


def dot(a, b, contract):
    return lax.dot_general(a, b, ((contract[0], contract[1]), ((), ())), preferred_element_type=jnp.float32)


def attend_block(first_row, ends, q, g, k, v, reach, heads, scale):
    cols = q.shape[0]
    key_rows = k.shape[0]
    token = lax.broadcasted_iota(jnp.int32, (1, cols), 1) // heads
    query_pos = first_row + token
    doc_start = jnp.zeros((1, cols), jnp.int32)
    for end in ends:
        doc_start = jnp.maximum(doc_start, jnp.where(end <= query_pos, end, 0))
    low = doc_start - (first_row - reach)
    raw = dot(k, q, ((1,), (1,)))
    index = lax.broadcasted_iota(jnp.int32, (key_rows, cols), 0)
    allowed = index >= low
    allowed_late = jnp.logical_and(allowed[reach:], index[reach:] - reach <= token)
    raw = jnp.concatenate(
        [jnp.where(allowed[:reach], raw[:reach], MASKED), jnp.where(allowed_late, raw[reach:], MASKED)], axis=0
    )
    row_max = jnp.max(raw, axis=0, keepdims=True)
    weights = jnp.exp2((raw - row_max) * (scale * LOG2_E))
    inverse = 1.0 / jnp.sum(weights, axis=0, keepdims=True)
    attended_t = (dot(v, weights.astype(jnp.bfloat16), ((0,), (0,))) * inverse).astype(jnp.bfloat16)
    attended = attended_t.T
    g_t = g.T.astype(jnp.float32)
    delta = jnp.sum(g_t * attended_t.astype(jnp.float32), axis=0, keepdims=True)
    probs = weights * inverse
    products = dot(v, g, ((1,), (1,)))
    slopes = (probs * (products - delta)).astype(jnp.bfloat16)
    value_part = dot(probs.astype(jnp.bfloat16), g, ((1,), (0,)))
    key_part = dot(slopes, q, ((1,), (0,))) * scale
    query_grad = (dot(k, slopes, ((0,), (0,))) * scale).astype(jnp.bfloat16).T
    return attended, query_grad, key_part, value_part


class Plan:
    def __init__(self, n, rows, heads, width, ndocs):
        self.n, self.rows, self.heads, self.width, self.ndocs = n, rows, heads, width, ndocs
        self.back = n // 2
        self.block = rows // n
        self.cols = self.block * heads
        self.reach = self.back * rows
        self.scale = width ** (-0.5)
        self.window_ranges = self.back + 1

    def ends(self, meta):
        return [meta[1 + i] for i in range(self.ndocs)]

    def slot(self, meta, loader, owner):
        return meta[1 + self.ndocs + loader * self.n + owner]

    def cost(self, blocks):
        return pl.CostEstimate(
            flops=14 * blocks * self.cols * (self.reach + self.block) * self.width * 8,
            bytes_accessed=blocks * self.cols * self.width * 16,
            transcendentals=blocks * self.cols * (self.reach + self.block),
        )


def fill_window(plan, refs, k_win, v_win):
    rows = plan.rows
    k_win[pl.ds(plan.back * rows, rows), :] = refs[0][pl.ds(0, rows), :]
    v_win[pl.ds(plan.back * rows, rows), :] = refs[0][pl.ds(rows, rows), :]
    for i in range(1, plan.back + 1):
        to = pl.ds((plan.back - i) * rows, rows)
        k_win[to, :] = refs[2 * i - 1][...]
        v_win[to, :] = refs[2 * i][...]


def attend_at(plan, meta, loader, slot, q, g, k_win, v_win):
    start = (loader - meta[0]) * plan.rows + slot * plan.block
    keys_here = pl.ds(pl.multiple_of(start, plan.block), plan.reach + plan.block)
    out = attend_block(
        loader * plan.rows + slot * plan.block, plan.ends(meta), q, g, k_win[keys_here, :], v_win[keys_here, :],
        plan.reach, plan.heads, plan.scale,
    )
    return keys_here, out


def pack_kernel(plan, meta, q_ref, g_ref, k_ref, v_ref, *refs):
    blocks, (kv, sems, kv_sems) = refs[: plan.n], refs[plan.n :]
    own = meta[0]
    copies = []
    for apart, block in enumerate(blocks):
        slot = plan.slot(meta, own, own ^ apart)
        at = pl.ds(pl.multiple_of(slot * plan.cols, plan.cols), plan.cols)
        copies.append(pltpu.make_async_copy(q_ref.at[at, :], block.at[0], sems.at[apart, 0]))
        copies.append(pltpu.make_async_copy(g_ref.at[at, :], block.at[1], sems.at[apart, 1]))
    for i, ref in enumerate((k_ref, v_ref)):
        to = kv.at[pl.ds(i * plan.rows, plan.rows), :]
        copies.append(pltpu.make_async_copy(ref, to, kv_sems.at[i]))
    for copy in copies:
        copy.start()
    for copy in copies:
        copy.wait()


def first_kernel(plan, apart, meta, qg, *refs):
    kv_refs, (pay_ref, grad_ref, k_win, v_win) = refs[:-4], refs[-4:]
    own = meta[0]
    slot = plan.slot(meta, own, own ^ apart)
    fill_window(plan, kv_refs, k_win, v_win)
    _, (attended, query_grad, key_part, value_part) = attend_at(
        plan, meta, own, slot, qg[0], qg[1], k_win, v_win
    )
    pay_ref[0] = attended
    pay_ref[1] = query_grad
    grad_ref[:, : plan.width] = key_part
    grad_ref[:, plan.width :] = value_part


def last_kernel(plan, first, items, meta, *refs):
    n, width, rows, block = plan.n, plan.width, plan.rows, plan.block
    qg_refs, refs = refs[: len(items)], refs[len(items) :]
    first_grad, refs = refs[0], refs[1:]
    kv_refs, refs = refs[: -(len(items) + 7)], refs[-(len(items) + 7) :]
    pay_refs, grad_refs, (k_win, v_win, acc) = refs[: len(items)], refs[len(items) : -3], refs[-3:]
    step = pl.program_id(0)
    own = meta[0]

    @pl.when(step == 0)
    def _():
        fill_window(plan, kv_refs, k_win, v_win)
        acc[...] = jnp.zeros_like(acc)
        slot = plan.slot(meta, own, own ^ first)
        keys_here = pl.ds(pl.multiple_of(slot * block, block), plan.reach + block)
        acc[keys_here, :] = first_grad[...]

    for i, item in enumerate(items):

        @pl.when(step == i)
        def _():
            slot = plan.slot(meta, own, own ^ item)
            qg = qg_refs[i]
            keys_here, (attended, query_grad, key_part, value_part) = attend_at(
                plan, meta, own, slot, qg[0], qg[1], k_win, v_win
            )
            acc[keys_here, :width] = acc[keys_here, :width] + key_part
            acc[keys_here, width:] = acc[keys_here, width:] + value_part
            pay_refs[i][0] = attended
            pay_refs[i][1] = query_grad

    @pl.when(step == len(items) - 1)
    def _():
        def of_range(key_range, carry):
            at = lax.rem(key_range - own + plan.back + n, n) * rows
            for apart in range(n):
                slot = plan.slot(meta, key_range, own ^ apart)
                part = acc[pl.ds(pl.multiple_of(at + slot * block, block), block), :]
                to = grad_refs[apart % 4]
                to[apart // 4, key_range] = part.astype(to.dtype)
            return carry

        lax.fori_loop(0, n, of_range, 0)


def spec_of(space):
    return pl.BlockSpec(memory_space=space)


def kernel_call(body, name, operands, spaces, out_shape, scratch, **more):
    return pl.pallas_call(
        body,
        out_shape=out_shape,
        in_specs=[spec_of(space) for space in spaces],
        compiler_params=pltpu.CompilerParams(vmem_limit_bytes=VMEM_LIMIT),
        scratch_shapes=scratch,
        name=name,
        **more,
    )(*operands)


def pack(plan, meta, *operands):
    out_shape = [jax.ShapeDtypeStruct((2, plan.cols, plan.width), jnp.bfloat16)] * plan.n
    out_shape.append(jax.ShapeDtypeStruct((2 * plan.rows, plan.width), jnp.bfloat16))
    operands = [pltpu.with_memory_space_constraint(x, pltpu.HBM) for x in operands]
    return kernel_call(
        functools.partial(pack_kernel, plan), "pack", (meta, *operands), [pltpu.SMEM] + [pl.ANY] * 4, out_shape,
        [pltpu.SemaphoreType.DMA((plan.n, 2)), pltpu.SemaphoreType.DMA((2,))],
        out_specs=[spec_of(pltpu.VMEM)] * len(out_shape),
    )


def attend_first(plan, apart, meta, qg, kv_list):
    window = pltpu.VMEM((plan.window_ranges * plan.rows, plan.width), jnp.bfloat16)
    out_shape = [
        jax.ShapeDtypeStruct((2, plan.cols, plan.width), jnp.bfloat16),
        jax.ShapeDtypeStruct((plan.reach + plan.block, 2 * plan.width), jnp.float32),
    ]
    operands = (meta, qg, *kv_list)
    return kernel_call(
        functools.partial(first_kernel, plan, apart), "attend_first", operands,
        [pltpu.SMEM] + [pltpu.VMEM] * (len(operands) - 1), out_shape, [window, window],
        out_specs=[spec_of(pltpu.VMEM)] * 2, cost_estimate=plan.cost(1),
    )


def attend_last(plan, first, items, meta, qg_list, first_grad, kv_list):
    n = plan.n
    window = pltpu.VMEM((plan.window_ranges * plan.rows, plan.width), jnp.bfloat16)
    grads = (n // 4, n, plan.block, 2 * plan.width)
    out_shape = [jax.ShapeDtypeStruct((2, plan.cols, plan.width), jnp.bfloat16)] * len(items)
    out_shape += [jax.ShapeDtypeStruct(grads, jnp.bfloat16 if apart % 2 else jnp.float32) for apart in range(4)]
    operands = (meta, *qg_list, first_grad, *kv_list)
    return kernel_call(
        functools.partial(last_kernel, plan, first, items), "attend_last", operands,
        [pltpu.SMEM] + [pltpu.VMEM] * (len(operands) - 1), out_shape,
        [window, window, pltpu.VMEM((n * plan.rows, 2 * plan.width), jnp.float32)],
        out_specs=[spec_of(pltpu.VMEM)] * len(out_shape), cost_estimate=plan.cost(len(items)), grid=(len(items),),
    )


def place_kernel(plan, items, final, *refs):
    n, cols, width = plan.n, plan.cols, plan.width
    own = lax.axis_index("ctx")
    pay_refs, refs = refs[: len(items)], refs[len(items) :]
    if final:
        grads, (_, _, attended, query_grad, key_grad, value_grad, sums, sems, sum_sems) = refs[:-9], refs[-9:]
    else:
        grads, (attended, query_grad, send, sems) = refs[:-4], refs[-4:]
    copies = []
    for i, item in enumerate(items):
        to = pl.ds(pl.multiple_of((own ^ item) * cols, cols), cols)
        copies.append(pltpu.make_async_copy(pay_refs[i].at[0], attended.at[to, :], sems.at[i, 0]))
        copies.append(pltpu.make_async_copy(pay_refs[i].at[1], query_grad.at[to, :], sems.at[i, 1]))
    for copy in copies:
        copy.start()
    total = sum(grad[...].astype(jnp.float32) for grad in grads).astype(jnp.bfloat16)
    if final:
        sums[0] = total[:, :width]
        sums[1] = total[:, width:]
        for i, ref in enumerate((key_grad, value_grad)):
            copies.append(pltpu.make_async_copy(sums.at[i], ref, sum_sems.at[i]))
            copies[-1].start()
    else:
        send[...] = total
    for copy in copies:
        copy.wait()


def place(plan, payloads, grads, filled=()):
    items = tuple(payloads)
    big = jax.ShapeDtypeStruct((plan.rows * plan.heads, plan.width), jnp.bfloat16)
    small = jax.ShapeDtypeStruct((plan.rows, plan.width), jnp.bfloat16)
    final = len(filled) > 0
    at = len(items) + len(grads)
    scratch = [pltpu.SemaphoreType.DMA((len(items), 2))]
    if final:
        scratch = [pltpu.VMEM((2, plan.rows, plan.width), jnp.bfloat16), *scratch, pltpu.SemaphoreType.DMA((2,))]
    return kernel_call(
        functools.partial(place_kernel, plan, items, final), "place_last" if final else "place_first",
        (*payloads.values(), *grads, *filled),
        [pl.ANY] * len(items) + [pltpu.VMEM] * len(grads) + [pl.ANY] * len(filled),
        [big, big] + ([small, small] if final else [jax.ShapeDtypeStruct(grads[0].shape, jnp.bfloat16)]), scratch,
        out_specs=[spec_of(pl.ANY)] * 2 + ([spec_of(pl.ANY)] * 2 if final else [spec_of(pltpu.VMEM)]),
        input_output_aliases={at: 0, at + 1: 1} if final else {},
        cost_estimate=plan.cost(len(items)),
    )


def on_device(query, keys, values, output_gradient, doc_lengths, block_owner):
    n = lax.axis_size("ctx")
    own = lax.axis_index("ctx")
    rows, heads, width = query.shape
    plan = Plan(n, rows, heads, width, doc_lengths.shape[0])

    def permuted(array, pairs):
        return lax.ppermute(array, "ctx", pairs)

    def across(array, bits):
        return permuted(array, [(i, i ^ bits) for i in range(n)])

    k = keys.reshape(rows, width)
    v = values.reshape(rows, width)
    kv_list = []
    for by in range(1, plan.back + 1):
        pairs = [(i, (i + by) % n) for i in range(n)]
        kv_list += [permuted(k, pairs), permuted(v, pairs)]

    owners = jnp.arange(n, dtype=jnp.int32)
    match = block_owner[:, None, :] == owners[None, :, None]
    table = jnp.sum(jnp.where(match, owners, 0), axis=2)
    meta = jnp.concatenate(
        [own.reshape(1).astype(jnp.int32), jnp.cumsum(doc_lengths).astype(jnp.int32), table.reshape(-1)]
    )

    q, g = (x.reshape(rows * heads, width) for x in (query, output_gradient))
    *blocks, kv = pack(plan, meta, q, g, k, v)
    kv_list = [kv, *kv_list]
    first = n // 2
    first_pay, first_grad = attend_first(plan, first, meta, blocks[first], kv_list)
    stay = {first: across(first_pay, first)}
    sent = [x for x in range(n - 1, 0, -1) if x != first]
    items = (*sent, 0)
    out = attend_last(plan, first, items, meta, [blocks[x] for x in items], first_grad, kv_list)
    late = {x: across(pay, x) for x, pay in zip(sent, out)}
    stay[0] = out[len(sent)]
    keep, to_keep, pass_on, to_pass_on = out[len(items) :]
    attended, query_grad, send = place(plan, stay, (pass_on, across(to_pass_on, 1)))
    terms = (keep, across(to_keep, 1), across(send, 2))
    bit = 4
    while bit < n:
        total = sum(term.astype(jnp.float32) for term in terms)
        terms = (total[0::2], across(total[1::2].astype(jnp.bfloat16), bit))
        bit *= 2
    terms = [term.reshape(rows, 2 * width) for term in terms]
    attended, query_grad, key_grad, value_grad = place(plan, late, terms, (attended, query_grad))
    return (
        attended.reshape(rows, heads, width),
        query_grad.reshape(rows, heads, width),
        key_grad.reshape(rows, 1, width),
        value_grad.reshape(rows, 1, width),
    )


def solution(mesh):
    rows = P(("dp", "ctx"), "tp", None)
    return jax.shard_map(
        on_device,
        mesh=mesh,
        in_specs=(rows, rows, rows, rows, P("dp"), P("dp", None)),
        out_specs=(rows, rows, rows, rows),
        check_vma=False,
    )
```

```python
import functools
import jax
import jax.numpy as jnp
from jax import lax
from jax.experimental import pallas as pl
from jax.experimental.pallas import tpu as pltpu
from jax.sharding import PartitionSpec as P

MASKED = -1e30
LOG2_E = 1.4426950408889634
VMEM_LIMIT = 32 * 1024 * 1024


def dot(a, b, contract):
    return lax.dot_general(a, b, ((contract[0], contract[1]), ((), ())), preferred_element_type=jnp.float32)


def attend_block(first_row, ends, q, g, k, v, reach, heads, scale):
    cols = q.shape[0]
    key_rows = k.shape[0]
    token = lax.broadcasted_iota(jnp.int32, (1, cols), 1) // heads
    query_pos = first_row + token
    doc_start = jnp.zeros((1, cols), jnp.int32)
    for end in ends:
        doc_start = jnp.maximum(doc_start, jnp.where(end <= query_pos, end, 0))
    low = doc_start - (first_row - reach)
    raw = dot(k, q, ((1,), (1,)))
    index = lax.broadcasted_iota(jnp.int32, (key_rows, cols), 0)
    allowed = index >= low
    allowed_late = jnp.logical_and(allowed[reach:], index[reach:] - reach <= token)
    raw = jnp.concatenate(
        [jnp.where(allowed[:reach], raw[:reach], MASKED), jnp.where(allowed_late, raw[reach:], MASKED)], axis=0
    )
    row_max = jnp.max(raw, axis=0, keepdims=True)
    weights = jnp.exp2((raw - row_max) * (scale * LOG2_E))
    inverse = 1.0 / jnp.sum(weights, axis=0, keepdims=True)
    attended_t = (dot(v, weights.astype(jnp.bfloat16), ((0,), (0,))) * inverse).astype(jnp.bfloat16)
    attended = attended_t.T
    g_t = g.T.astype(jnp.float32)
    delta = jnp.sum(g_t * attended_t.astype(jnp.float32), axis=0, keepdims=True)
    probs = weights * inverse
    products = dot(v, g, ((1,), (1,)))
    slopes = (probs * (products - delta)).astype(jnp.bfloat16)
    value_part = dot(probs.astype(jnp.bfloat16), g, ((1,), (0,)))
    key_part = dot(slopes, q, ((1,), (0,))) * scale
    query_grad = (dot(k, slopes, ((0,), (0,))) * scale).astype(jnp.bfloat16).T
    return attended, query_grad, key_part, value_part


class Plan:
    def __init__(self, n, rows, heads, width, ndocs):
        self.n, self.rows, self.heads, self.width, self.ndocs = n, rows, heads, width, ndocs
        self.back = n // 2
        self.block = rows // n
        self.cols = self.block * heads
        self.reach = self.back * rows
        self.scale = width ** (-0.5)
        self.window_ranges = self.back + 1

    def ends(self, meta):
        return [meta[1 + i] for i in range(self.ndocs)]

    def slot(self, meta, loader, owner):
        return meta[1 + self.ndocs + loader * self.n + owner]

    def cost(self, blocks):
        return pl.CostEstimate(
            flops=14 * blocks * self.cols * (self.reach + self.block) * self.width * 8,
            bytes_accessed=blocks * self.cols * self.width * 16,
            transcendentals=blocks * self.cols * (self.reach + self.block),
        )


def fill_window(plan, refs, k_win, v_win):
    rows = plan.rows
    k_win[pl.ds(plan.back * rows, rows), :] = refs[0][pl.ds(0, rows), :]
    v_win[pl.ds(plan.back * rows, rows), :] = refs[0][pl.ds(rows, rows), :]
    for i in range(1, plan.back + 1):
        to = pl.ds((plan.back - i) * rows, rows)
        k_win[to, :] = refs[2 * i - 1][...]
        v_win[to, :] = refs[2 * i][...]


def attend_at(plan, meta, loader, slot, q, g, k_win, v_win):
    start = (loader - meta[0]) * plan.rows + slot * plan.block
    keys_here = pl.ds(pl.multiple_of(start, plan.block), plan.reach + plan.block)
    out = attend_block(
        loader * plan.rows + slot * plan.block, plan.ends(meta), q, g, k_win[keys_here, :], v_win[keys_here, :],
        plan.reach, plan.heads, plan.scale,
    )
    return keys_here, out


def pack_kernel(plan, meta, q_ref, g_ref, k_ref, v_ref, *refs):
    blocks, (kv, sems, kv_sems) = refs[: plan.n], refs[plan.n :]
    own = meta[0]
    copies = []
    for apart, block in enumerate(blocks):
        slot = plan.slot(meta, own, own ^ apart)
        at = pl.ds(pl.multiple_of(slot * plan.cols, plan.cols), plan.cols)
        copies.append(pltpu.make_async_copy(q_ref.at[at, :], block.at[0], sems.at[apart, 0]))
        copies.append(pltpu.make_async_copy(g_ref.at[at, :], block.at[1], sems.at[apart, 1]))
    for i, ref in enumerate((k_ref, v_ref)):
        to = kv.at[pl.ds(i * plan.rows, plan.rows), :]
        copies.append(pltpu.make_async_copy(ref, to, kv_sems.at[i]))
    for copy in copies:
        copy.start()
    for copy in copies:
        copy.wait()


def first_kernel(plan, apart, meta, qg, *refs):
    kv_refs, (pay_ref, grad_ref, k_win, v_win) = refs[:-4], refs[-4:]
    own = meta[0]
    slot = plan.slot(meta, own, own ^ apart)
    fill_window(plan, kv_refs, k_win, v_win)
    _, (attended, query_grad, key_part, value_part) = attend_at(
        plan, meta, own, slot, qg[0], qg[1], k_win, v_win
    )
    pay_ref[0] = attended
    pay_ref[1] = query_grad
    grad_ref[:, : plan.width] = key_part
    grad_ref[:, plan.width :] = value_part


def last_kernel(plan, first, items, meta, *refs):
    n, width, rows, block = plan.n, plan.width, plan.rows, plan.block
    qg_refs, refs = refs[: len(items)], refs[len(items) :]
    first_grad, refs = refs[0], refs[1:]
    kv_refs, refs = refs[: -(len(items) + 7)], refs[-(len(items) + 7) :]
    pay_refs, grad_refs, (k_win, v_win, acc) = refs[: len(items)], refs[len(items) : -3], refs[-3:]
    step = pl.program_id(0)
    own = meta[0]

    @pl.when(step == 0)
    def _():
        fill_window(plan, kv_refs, k_win, v_win)
        acc[...] = jnp.zeros_like(acc)
        slot = plan.slot(meta, own, own ^ first)
        keys_here = pl.ds(pl.multiple_of(slot * block, block), plan.reach + block)
        acc[keys_here, :] = first_grad[...]

    for i, item in enumerate(items):

        @pl.when(step == i)
        def _():
            slot = plan.slot(meta, own, own ^ item)
            qg = qg_refs[i]
            keys_here, (attended, query_grad, key_part, value_part) = attend_at(
                plan, meta, own, slot, qg[0], qg[1], k_win, v_win
            )
            acc[keys_here, :width] = acc[keys_here, :width] + key_part
            acc[keys_here, width:] = acc[keys_here, width:] + value_part
            pay_refs[i][0] = attended
            pay_refs[i][1] = query_grad

    @pl.when(step == len(items) - 1)
    def _():
        def put_part(key_range, entry, part):
            @pl.when(key_range < n // 2)
            def _():
                grad_refs[2][entry, key_range] = part.astype(jnp.bfloat16)

            @pl.when(key_range >= n // 2)
            def _():
                grad_refs[3][entry, key_range - n // 2] = part.astype(jnp.bfloat16)

        def of_range(key_range, carry):
            at = lax.rem(key_range - own + plan.back + n, n) * rows
            for apart in range(n):
                slot = plan.slot(meta, key_range, own ^ apart)
                part = acc[pl.ds(pl.multiple_of(at + slot * block, block), block), :]
                if apart % 2 == 0:
                    to = grad_refs[apart % 4 // 2]
                    to[apart // 4, key_range] = part
                else:
                    put_part(key_range, apart // 2, part)
            return carry

        lax.fori_loop(0, n, of_range, 0)


def spec_of(space):
    return pl.BlockSpec(memory_space=space)


def kernel_call(body, name, operands, spaces, out_shape, scratch, **more):
    return pl.pallas_call(
        body,
        out_shape=out_shape,
        in_specs=[spec_of(space) for space in spaces],
        compiler_params=pltpu.CompilerParams(vmem_limit_bytes=VMEM_LIMIT),
        scratch_shapes=scratch,
        name=name,
        **more,
    )(*operands)


def pack(plan, meta, *operands):
    out_shape = [jax.ShapeDtypeStruct((2, plan.cols, plan.width), jnp.bfloat16)] * plan.n
    out_shape.append(jax.ShapeDtypeStruct((2 * plan.rows, plan.width), jnp.bfloat16))
    operands = [pltpu.with_memory_space_constraint(x, pltpu.HBM) for x in operands]
    return kernel_call(
        functools.partial(pack_kernel, plan), "pack", (meta, *operands), [pltpu.SMEM] + [pl.ANY] * 4, out_shape,
        [pltpu.SemaphoreType.DMA((plan.n, 2)), pltpu.SemaphoreType.DMA((2,))],
        out_specs=[spec_of(pltpu.VMEM)] * len(out_shape),
    )


def attend_first(plan, apart, meta, qg, kv_list):
    window = pltpu.VMEM((plan.window_ranges * plan.rows, plan.width), jnp.bfloat16)
    out_shape = [
        jax.ShapeDtypeStruct((2, plan.cols, plan.width), jnp.bfloat16),
        jax.ShapeDtypeStruct((plan.reach + plan.block, 2 * plan.width), jnp.float32),
    ]
    operands = (meta, qg, *kv_list)
    return kernel_call(
        functools.partial(first_kernel, plan, apart), "attend_first", operands,
        [pltpu.SMEM] + [pltpu.VMEM] * (len(operands) - 1), out_shape, [window, window],
        out_specs=[spec_of(pltpu.VMEM)] * 2, cost_estimate=plan.cost(1),
    )


def attend_last(plan, first, items, meta, qg_list, first_grad, kv_list):
    n = plan.n
    window = pltpu.VMEM((plan.window_ranges * plan.rows, plan.width), jnp.bfloat16)
    keep = jax.ShapeDtypeStruct((n // 4, n, plan.block, 2 * plan.width), jnp.float32)
    send = jax.ShapeDtypeStruct((n // 2, n // 2, plan.block, 2 * plan.width), jnp.bfloat16)
    out_shape = [jax.ShapeDtypeStruct((2, plan.cols, plan.width), jnp.bfloat16)] * len(items)
    out_shape += [keep, keep, send, send]
    operands = (meta, *qg_list, first_grad, *kv_list)
    return kernel_call(
        functools.partial(last_kernel, plan, first, items), "attend_last", operands,
        [pltpu.SMEM] + [pltpu.VMEM] * (len(operands) - 1), out_shape,
        [window, window, pltpu.VMEM((n * plan.rows, 2 * plan.width), jnp.float32)],
        out_specs=[spec_of(pltpu.VMEM)] * len(out_shape), cost_estimate=plan.cost(len(items)), grid=(len(items),),
    )


def place_kernel(plan, items, final, *refs):
    n, cols, width = plan.n, plan.cols, plan.width
    own = lax.axis_index("ctx")
    pay_refs, refs = refs[: len(items)], refs[len(items) :]
    if final:
        grads, (_, _, attended, query_grad, key_grad, value_grad, sums, sems, sum_sems) = refs[:-9], refs[-9:]
    else:
        grads, (attended, query_grad, send, kept, sems) = refs[:-5], refs[-5:]
    copies = []
    for i, item in enumerate(items):
        to = pl.ds(pl.multiple_of((own ^ item) * cols, cols), cols)
        copies.append(pltpu.make_async_copy(pay_refs[i].at[0], attended.at[to, :], sems.at[i, 0]))
        copies.append(pltpu.make_async_copy(pay_refs[i].at[1], query_grad.at[to, :], sems.at[i, 1]))
    for copy in copies:
        copy.start()
    if final:
        total = sum(grad[...].astype(jnp.float32) for grad in grads).astype(jnp.bfloat16)
        sums[0] = total[:, :width]
        sums[1] = total[:, width:]
        for i, ref in enumerate((key_grad, value_grad)):
            copies.append(pltpu.make_async_copy(sums.at[i], ref, sum_sems.at[i]))
            copies[-1].start()
    else:
        pass_on, keep, *arrived = grads
        for entry in range(n // 2):
            for half, ref in enumerate(arrived):
                ranges = pl.ds(half * (n // 2), n // 2)
                total = (keep, pass_on)[entry % 2][entry // 2, ranges] + ref[entry].astype(jnp.float32)
                if entry % 2:
                    send[entry // 2, ranges] = total.astype(jnp.bfloat16)
                else:
                    kept[entry // 2, ranges] = total
    for copy in copies:
        copy.wait()


def place(plan, payloads, grads, filled=()):
    items = tuple(payloads)
    big = jax.ShapeDtypeStruct((plan.rows * plan.heads, plan.width), jnp.bfloat16)
    small = jax.ShapeDtypeStruct((plan.rows, plan.width), jnp.bfloat16)
    final = len(filled) > 0
    at = len(items) + len(grads)
    scratch = [pltpu.SemaphoreType.DMA((len(items), 2))]
    if final:
        scratch = [pltpu.VMEM((2, plan.rows, plan.width), jnp.bfloat16), *scratch, pltpu.SemaphoreType.DMA((2,))]
    return kernel_call(
        functools.partial(place_kernel, plan, items, final), "place_last" if final else "place_first",
        (*payloads.values(), *grads, *filled),
        [pl.ANY] * len(items) + [pltpu.VMEM] * len(grads) + [pl.ANY] * len(filled),
        [big, big] + ([small, small] if final else [jax.ShapeDtypeStruct(grads[0].shape, t) for t in (jnp.bfloat16, jnp.float32)]), scratch,
        out_specs=[spec_of(pl.ANY)] * 2 + [spec_of(pl.ANY if final else pltpu.VMEM)] * 2,
        input_output_aliases={at: 0, at + 1: 1} if final else {},
        cost_estimate=plan.cost(len(items)),
    )


def on_device(query, keys, values, output_gradient, doc_lengths, block_owner):
    n = lax.axis_size("ctx")
    own = lax.axis_index("ctx")
    rows, heads, width = query.shape
    plan = Plan(n, rows, heads, width, doc_lengths.shape[0])

    def permuted(array, pairs):
        return lax.ppermute(array, "ctx", pairs)

    def across(array, bits):
        return permuted(array, [(i, i ^ bits) for i in range(n)])

    k = keys.reshape(rows, width)
    v = values.reshape(rows, width)
    kv_list = []
    for by in range(1, plan.back + 1):
        pairs = [(i, (i + by) % n) for i in range(n)]
        kv_list += [permuted(k, pairs), permuted(v, pairs)]

    owners = jnp.arange(n, dtype=jnp.int32)
    match = block_owner[:, None, :] == owners[None, :, None]
    table = jnp.sum(jnp.where(match, owners, 0), axis=2)
    meta = jnp.concatenate(
        [own.reshape(1).astype(jnp.int32), jnp.cumsum(doc_lengths).astype(jnp.int32), table.reshape(-1)]
    )

    q, g = (x.reshape(rows * heads, width) for x in (query, output_gradient))
    *blocks, kv = pack(plan, meta, q, g, k, v)
    kv_list = [kv, *kv_list]
    first = n // 2
    first_pay, first_grad = attend_first(plan, first, meta, blocks[first], kv_list)
    stay = {first: across(first_pay, first)}
    sent = [x for x in range(1, n) if x != first]
    items = (*sent, 0)
    out = attend_last(plan, first, items, meta, [blocks[x] for x in items], first_grad, kv_list)
    late = {x: across(pay, x) for x, pay in zip(sent, out)}
    stay[0] = out[len(sent)]
    keep, pass_on, lower, upper = out[len(items) :]
    upper = permuted(upper, [(i, i ^ 1) for i in range(n // 2, n)])
    attended, query_grad, send, keep = place(plan, stay, (pass_on, keep, across(lower, 1), upper))
    terms = (keep, across(send, 2))
    bit = 4
    while bit < n:
        total = sum(term.astype(jnp.float32) for term in terms)
        terms = (total[0::2], across(total[1::2].astype(jnp.bfloat16), bit))
        bit *= 2
    terms = [term.reshape(rows, 2 * width) for term in terms]
    attended, query_grad, key_grad, value_grad = place(plan, late, terms, (attended, query_grad))
    return (
        attended.reshape(rows, heads, width),
        query_grad.reshape(rows, heads, width),
        key_grad.reshape(rows, 1, width),
        value_grad.reshape(rows, 1, width),
    )


def solution(mesh):
    rows = P(("dp", "ctx"), "tp", None)
    return jax.shard_map(
        on_device,
        mesh=mesh,
        in_specs=(rows, rows, rows, rows, P("dp"), P("dp", None)),
        out_specs=(rows, rows, rows, rows),
        check_vma=False,
    )
```

```python
import functools
import jax
import jax.numpy as jnp
from jax import lax
from jax.experimental import pallas as pl
from jax.experimental.pallas import tpu as pltpu
from jax.sharding import PartitionSpec as P

MASKED = -1e30
LOG2_E = 1.4426950408889634
VMEM_LIMIT = 32 * 1024 * 1024


def dot(a, b, contract):
    return lax.dot_general(a, b, ((contract[0], contract[1]), ((), ())), preferred_element_type=jnp.float32)


def attend_block(first_row, ends, q, g, k, v, reach, heads, scale):
    cols = q.shape[0]
    key_rows = k.shape[0]
    token = lax.broadcasted_iota(jnp.int32, (1, cols), 1) // heads
    query_pos = first_row + token
    doc_start = jnp.zeros((1, cols), jnp.int32)
    for end in ends:
        doc_start = jnp.maximum(doc_start, jnp.where(end <= query_pos, end, 0))
    low = doc_start - (first_row - reach)
    raw = dot(k, q, ((1,), (1,)))
    index = lax.broadcasted_iota(jnp.int32, (key_rows, cols), 0)
    allowed = index >= low
    allowed_late = jnp.logical_and(allowed[reach:], index[reach:] - reach <= token)
    raw = jnp.concatenate(
        [jnp.where(allowed[:reach], raw[:reach], MASKED), jnp.where(allowed_late, raw[reach:], MASKED)], axis=0
    )
    row_max = jnp.max(raw, axis=0, keepdims=True)
    weights = jnp.exp2((raw - row_max) * (scale * LOG2_E))
    inverse = 1.0 / jnp.sum(weights, axis=0, keepdims=True)
    attended_t = (dot(v, weights.astype(jnp.bfloat16), ((0,), (0,))) * inverse).astype(jnp.bfloat16)
    attended = attended_t.T
    g_t = g.T.astype(jnp.float32)
    delta = jnp.sum(g_t * attended_t.astype(jnp.float32), axis=0, keepdims=True)
    probs = weights * inverse
    products = dot(v, g, ((1,), (1,)))
    slopes = (probs * (products - delta)).astype(jnp.bfloat16)
    value_part = dot(probs.astype(jnp.bfloat16), g, ((1,), (0,)))
    key_part = dot(slopes, q, ((1,), (0,))) * scale
    query_grad = (dot(k, slopes, ((0,), (0,))) * scale).astype(jnp.bfloat16).T
    return attended, query_grad, key_part, value_part


class Plan:
    def __init__(self, n, rows, heads, width, ndocs):
        self.n, self.rows, self.heads, self.width, self.ndocs = n, rows, heads, width, ndocs
        self.back = n // 2
        self.block = rows // n
        self.cols = self.block * heads
        self.reach = self.back * rows
        self.scale = width ** (-0.5)
        self.lower = self.back + 1
        self.window_ranges = self.back + 2

    def ends(self, meta):
        return [meta[1 + i] for i in range(self.ndocs)]

    def slot(self, meta, loader, owner):
        return meta[1 + self.ndocs + loader * self.n + owner]

    def cost(self, blocks):
        return pl.CostEstimate(
            flops=14 * blocks * self.cols * (self.reach + self.block) * self.width * 8,
            bytes_accessed=blocks * self.cols * self.width * 16,
            transcendentals=blocks * self.cols * (self.reach + self.block),
        )


def fill_window(plan, own, refs, k_win, v_win):
    rows = plan.rows
    k_win[pl.ds(0, rows), :] = jnp.zeros((rows, plan.width), k_win.dtype)
    v_win[pl.ds(0, rows), :] = jnp.zeros((rows, plan.width), v_win.dtype)
    k_win[pl.ds(plan.back * rows, rows), :] = refs[0][pl.ds(0, rows), :]
    v_win[pl.ds(plan.back * rows, rows), :] = refs[0][pl.ds(rows, rows), :]
    for i in range(1, plan.back + 1):
        place = plan.back - i if i < plan.back else jnp.where(own == plan.back - 1, plan.back + 1, 0)
        to = pl.ds(pl.multiple_of(place * rows, rows), rows)
        k_win[to, :] = refs[2 * i - 1][...]
        v_win[to, :] = refs[2 * i][...]


def attend_at(plan, meta, loader, slot, q, g, k_win, v_win):
    start = (loader - meta[0]) * plan.rows + slot * plan.block
    keys_here = pl.ds(pl.multiple_of(start, plan.block), plan.reach + plan.block)
    out = attend_block(
        loader * plan.rows + slot * plan.block, plan.ends(meta), q, g, k_win[keys_here, :], v_win[keys_here, :],
        plan.reach, plan.heads, plan.scale,
    )
    return keys_here, out


def pack_kernel(plan, meta, q_ref, g_ref, k_ref, v_ref, *refs):
    blocks, (kv, sems, kv_sems) = refs[: plan.n], refs[plan.n :]
    own = meta[0]
    copies = []
    for apart, block in enumerate(blocks):
        slot = plan.slot(meta, own, own ^ apart)
        at = pl.ds(pl.multiple_of(slot * plan.cols, plan.cols), plan.cols)
        copies.append(pltpu.make_async_copy(q_ref.at[at, :], block.at[0], sems.at[apart, 0]))
        copies.append(pltpu.make_async_copy(g_ref.at[at, :], block.at[1], sems.at[apart, 1]))
    for i, ref in enumerate((k_ref, v_ref)):
        to = kv.at[pl.ds(i * plan.rows, plan.rows), :]
        copies.append(pltpu.make_async_copy(ref, to, kv_sems.at[i]))
    for copy in copies:
        copy.start()
    for copy in copies:
        copy.wait()


def first_kernel(plan, apart, meta, qg, *refs):
    kv_refs, (pay_ref, grad_ref, k_win, v_win) = refs[:-4], refs[-4:]
    own = meta[0]
    slot = plan.slot(meta, own, own ^ apart)
    fill_window(plan, own, kv_refs, k_win, v_win)
    _, (attended, query_grad, key_part, value_part) = attend_at(
        plan, meta, own, slot, qg[0], qg[1], k_win, v_win
    )
    pay_ref[0] = attended
    pay_ref[1] = query_grad
    grad_ref[:, : plan.width] = key_part
    grad_ref[:, plan.width :] = value_part


def add_parts(plan, acc, keys_here, key_part, value_part):
    acc[keys_here, : plan.width] = acc[keys_here, : plan.width] + key_part
    acc[keys_here, plan.width :] = acc[keys_here, plan.width :] + value_part


def put_rows(plan, pay_ref, attended, query_grad):
    pay_ref[0] = attended
    pay_ref[1] = query_grad


def next_kernel(plan, first, items, meta, *refs):
    n = plan.n
    qg_refs, first_grad, refs = refs[: len(items)], refs[len(items)], refs[len(items) + 1 :]
    outs = len(items) + 3
    kv_refs, pay_refs, (acc, k_win, v_win) = refs[:-outs], refs[-outs:-3], refs[-3:]
    step = pl.program_id(0)
    own = meta[0]

    @pl.when(step == 0)
    def _():
        fill_window(plan, own, kv_refs, k_win, v_win)
        acc[...] = jnp.zeros_like(acc)
        slot = plan.slot(meta, own, own ^ first)
        start = pl.multiple_of(slot * plan.block, plan.block)
        acc[pl.ds(start, plan.reach + plan.block), :] = first_grad[...]

    for i, item in enumerate(items):
        here = step == i
        if item == n - 1:
            here = jnp.logical_and(here, own != plan.back)

        @pl.when(here)
        def _():
            slot = plan.slot(meta, own, own ^ item)
            keys_here, (attended, query_grad, *parts) = attend_at(
                plan, meta, own, slot, qg_refs[i][0], qg_refs[i][1], k_win, v_win
            )
            add_parts(plan, acc, keys_here, *parts)
            put_rows(plan, pay_refs[i], attended, query_grad)


def last_kernel(plan, meta, got_ref, acc_ref, *refs):
    n, block, rows = plan.n, plan.block, plan.rows
    kv_refs, (pay_ref, *grad_refs), (k_win, v_win, acc) = refs[:-8], refs[-8:-3], refs[-3:]
    own = meta[0]
    acc[...] = acc_ref[...]

    @pl.when(own == plan.back - 1)
    def _():
        fill_window(plan, own, kv_refs, k_win, v_win)
        keys_here, (attended, query_grad, *parts) = attend_at(
            plan, meta, own + 1, plan.slot(meta, own + 1, own), got_ref[0], got_ref[1], k_win, v_win
        )
        add_parts(plan, acc, keys_here, *parts)
        put_rows(plan, pay_ref, attended, query_grad)

    def put_part(key_range, entry, part):
        @pl.when(key_range < plan.lower)
        def _():
            grad_refs[2][entry, key_range] = part.astype(jnp.bfloat16)

        @pl.when(key_range >= plan.lower)
        def _():
            grad_refs[3][entry, key_range - plan.lower] = part.astype(jnp.bfloat16)

    def of_range(key_range, carry):
        at = lax.rem(key_range - own + plan.back + n, n) * rows
        for apart in range(n):
            slot = plan.slot(meta, key_range, own ^ apart)
            part = acc[pl.ds(pl.multiple_of(at + slot * block, block), block), :]
            if apart % 2 == 0:
                to = grad_refs[apart % 4 // 2]
                to[apart // 4, key_range] = part
            else:
                put_part(key_range, apart // 2, part)
        return carry

    lax.fori_loop(0, n, of_range, 0)


def spec_of(space):
    return pl.BlockSpec(memory_space=space)


def kernel_call(body, name, operands, spaces, out_shape, scratch, **more):
    return pl.pallas_call(
        body,
        out_shape=out_shape,
        in_specs=[spec_of(space) for space in spaces],
        compiler_params=pltpu.CompilerParams(vmem_limit_bytes=VMEM_LIMIT),
        scratch_shapes=scratch,
        name=name,
        **more,
    )(*operands)


def pack(plan, meta, *operands):
    out_shape = [jax.ShapeDtypeStruct((2, plan.cols, plan.width), jnp.bfloat16)] * plan.n
    out_shape.append(jax.ShapeDtypeStruct((2 * plan.rows, plan.width), jnp.bfloat16))
    operands = [pltpu.with_memory_space_constraint(x, pltpu.HBM) for x in operands]
    return kernel_call(
        functools.partial(pack_kernel, plan), "pack", (meta, *operands), [pltpu.SMEM] + [pl.ANY] * 4, out_shape,
        [pltpu.SemaphoreType.DMA((plan.n, 2)), pltpu.SemaphoreType.DMA((2,))],
        out_specs=[spec_of(pltpu.VMEM)] * len(out_shape),
    )


def attend_first(plan, apart, meta, qg, kv_list):
    window = pltpu.VMEM((plan.window_ranges * plan.rows, plan.width), jnp.bfloat16)
    out_shape = [
        jax.ShapeDtypeStruct((2, plan.cols, plan.width), jnp.bfloat16),
        jax.ShapeDtypeStruct((plan.reach + plan.block, 2 * plan.width), jnp.float32),
    ]
    operands = (meta, qg, *kv_list)
    return kernel_call(
        functools.partial(first_kernel, plan, apart), "attend_first", operands,
        [pltpu.SMEM] + [pltpu.VMEM] * (len(operands) - 1), out_shape, [window, window],
        out_specs=[spec_of(pltpu.VMEM)] * 2, cost_estimate=plan.cost(1),
    )


def attend_next(plan, first, items, meta, qg_list, first_grad, kv_list):
    window = pltpu.VMEM((plan.window_ranges * plan.rows, plan.width), jnp.bfloat16)
    out_shape = [jax.ShapeDtypeStruct((2, plan.cols, plan.width), jnp.bfloat16)] * len(items)
    out_shape.append(jax.ShapeDtypeStruct((plan.n * plan.rows, 2 * plan.width), jnp.float32))
    operands = (meta, *qg_list, first_grad, *kv_list)
    return kernel_call(
        functools.partial(next_kernel, plan, first, items), "attend_next", operands,
        [pltpu.SMEM] + [pltpu.VMEM] * (len(operands) - 1), out_shape, [window, window],
        out_specs=[spec_of(pltpu.VMEM)] * len(out_shape), cost_estimate=plan.cost(len(items)), grid=(len(items),),
    )


def attend_last(plan, meta, got, sums, kv_list):
    n = plan.n
    window = pltpu.VMEM((plan.window_ranges * plan.rows, plan.width), jnp.bfloat16)
    part = (plan.block, 2 * plan.width)
    keep = jax.ShapeDtypeStruct((n // 4, n, *part), jnp.float32)
    lower = jax.ShapeDtypeStruct((n // 2, plan.lower, *part), jnp.bfloat16)
    upper = jax.ShapeDtypeStruct((n // 2, n - plan.lower, *part), jnp.bfloat16)
    out_shape = [jax.ShapeDtypeStruct((2, plan.cols, plan.width), jnp.bfloat16), keep, keep, lower, upper]
    operands = (meta, got, sums, *kv_list)
    return kernel_call(
        functools.partial(last_kernel, plan), "attend_last", operands,
        [pltpu.SMEM] + [pltpu.VMEM] * (len(operands) - 1), out_shape,
        [window, window, pltpu.VMEM(sums.shape, jnp.float32)],
        out_specs=[spec_of(pltpu.VMEM)] * len(out_shape), cost_estimate=plan.cost(1),
    )


def place_kernel(plan, items, final, *refs):
    n, cols, width = plan.n, plan.cols, plan.width
    own = lax.axis_index("ctx")
    pay_refs, refs = refs[: len(items)], refs[len(items) :]
    if final:
        grads, (_, _, attended, query_grad, key_grad, value_grad, sums, sems, sum_sems) = refs[:-9], refs[-9:]
    else:
        grads, (attended, query_grad, send, kept, sems) = refs[:-5], refs[-5:]
    copies = []
    for i, item in enumerate(items):
        to = pl.ds(pl.multiple_of((own ^ (n - 1 if item == "got" else item)) * cols, cols), cols)
        pair = [
            pltpu.make_async_copy(pay_refs[i].at[0], attended.at[to, :], sems.at[i, 0]),
            pltpu.make_async_copy(pay_refs[i].at[1], query_grad.at[to, :], sems.at[i, 1]),
        ]
        if item in ("got", n - 1):
            copies += [(copy, (own == plan.back - 1) == (item == "got")) for copy in pair]
        else:
            copies += [(copy, None) for copy in pair]

    def each(act):
        for copy, here in copies:
            if here is None:
                act(copy)
            else:
                pl.when(here)(functools.partial(act, copy))

    each(lambda copy: copy.start())
    if final:
        total = sum(grad[...].astype(jnp.float32) for grad in grads).astype(jnp.bfloat16)
        sums[0] = total[:, :width]
        sums[1] = total[:, width:]
        for i, ref in enumerate((key_grad, value_grad)):
            copies.append((pltpu.make_async_copy(sums.at[i], ref, sum_sems.at[i]), None))
            copies[-1][0].start()
    else:
        pass_on, keep, *arrived = grads
        for entry in range(n // 2):
            for half, ref in enumerate(arrived):
                ranges = pl.ds(plan.lower, n - plan.lower) if half else pl.ds(0, plan.lower)
                total = (keep, pass_on)[entry % 2][entry // 2, ranges] + ref[entry].astype(jnp.float32)
                if entry % 2:
                    send[entry // 2, ranges] = total.astype(jnp.bfloat16)
                else:
                    kept[entry // 2, ranges] = total
    each(lambda copy: copy.wait())


def place(plan, payloads, grads, filled=()):
    items = tuple(payloads)
    big = jax.ShapeDtypeStruct((plan.rows * plan.heads, plan.width), jnp.bfloat16)
    small = jax.ShapeDtypeStruct((plan.rows, plan.width), jnp.bfloat16)
    final = len(filled) > 0
    at = len(items) + len(grads)
    scratch = [pltpu.SemaphoreType.DMA((len(items), 2))]
    if final:
        scratch = [pltpu.VMEM((2, plan.rows, plan.width), jnp.bfloat16), *scratch, pltpu.SemaphoreType.DMA((2,))]
    return kernel_call(
        functools.partial(place_kernel, plan, items, final), "place_last" if final else "place_first",
        (*payloads.values(), *grads, *filled),
        [pl.ANY] * len(items) + [pltpu.VMEM] * len(grads) + [pl.ANY] * len(filled),
        [big, big] + ([small, small] if final else [jax.ShapeDtypeStruct(grads[0].shape, t) for t in (jnp.bfloat16, jnp.float32)]), scratch,
        out_specs=[spec_of(pl.ANY)] * 2 + [spec_of(pl.ANY if final else pltpu.VMEM)] * 2,
        input_output_aliases={at: 0, at + 1: 1} if final else {},
        cost_estimate=plan.cost(len(items)),
    )


def on_device(query, keys, values, output_gradient, doc_lengths, block_owner):
    n = lax.axis_size("ctx")
    own = lax.axis_index("ctx")
    rows, heads, width = query.shape
    plan = Plan(n, rows, heads, width, doc_lengths.shape[0])

    def permuted(array, pairs):
        return lax.ppermute(array, "ctx", pairs)

    def across(array, bits):
        return permuted(array, [(i, i ^ bits) for i in range(n)])

    k = keys.reshape(rows, width)
    v = values.reshape(rows, width)
    kv_list = []
    for by in range(1, plan.back + 1):
        pairs = [(i, (i + by) % n) for i in range(n)]
        if by == plan.back:
            pairs = [(i, i + by if i < by else (i - by - 1) % by) for i in range(n)]
        kv_list += [permuted(k, pairs), permuted(v, pairs)]

    owners = jnp.arange(n, dtype=jnp.int32)
    match = block_owner[:, None, :] == owners[None, :, None]
    table = jnp.sum(jnp.where(match, owners, 0), axis=2)
    meta = jnp.concatenate(
        [own.reshape(1).astype(jnp.int32), jnp.cumsum(doc_lengths).astype(jnp.int32), table.reshape(-1)]
    )

    q, g = (x.reshape(rows * heads, width) for x in (query, output_gradient))
    *blocks, kv = pack(plan, meta, q, g, k, v)
    kv_list = [kv, *kv_list]
    got = permuted(blocks[n - 1], [(plan.back, plan.back - 1)])
    first = n // 2
    first_pay, first_grad = attend_first(plan, first, meta, blocks[first], kv_list)
    stay = {first: across(first_pay, first)}
    items = tuple(x for x in range(n - 1, -1, -1) if x != first)
    *pays, sums = attend_next(plan, first, items, meta, [blocks[x] for x in items], first_grad, kv_list)
    stay["got"], *out = attend_last(plan, meta, got, sums, kv_list)
    stay[0] = pays[-1]
    late = {n - 1: permuted(pays[0], [(i, i ^ (n - 1)) for i in range(n) if i != plan.back])}
    late.update({x: across(pay, x) for x, pay in zip(items[1:-1], pays[1:-1])})
    keep, pass_on, lower, upper = out
    upper = permuted(upper, [(i, i ^ 1) for i in range(plan.back, n)])
    attended, query_grad, send, keep = place(plan, stay, (pass_on, keep, across(lower, 1), upper))
    terms = (keep, across(send, 2))
    bit = 4
    while bit < n:
        total = sum(term.astype(jnp.float32) for term in terms)
        terms = (total[0::2], across(total[1::2].astype(jnp.bfloat16), bit))
        bit *= 2
    terms = [term.reshape(rows, 2 * width) for term in terms]
    attended, query_grad, key_grad, value_grad = place(plan, late, terms, (attended, query_grad))
    return (
        attended.reshape(rows, heads, width),
        query_grad.reshape(rows, heads, width),
        key_grad.reshape(rows, 1, width),
        value_grad.reshape(rows, 1, width),
    )


def solution(mesh):
    rows = P(("dp", "ctx"), "tp", None)
    return jax.shard_map(
        on_device,
        mesh=mesh,
        in_specs=(rows, rows, rows, rows, P("dp"), P("dp", None)),
        out_specs=(rows, rows, rows, rows),
        check_vma=False,
    )
```

```python
import functools
import jax
import jax.numpy as jnp
from jax import lax
from jax.experimental import pallas as pl
from jax.experimental.pallas import tpu as pltpu
from jax.sharding import PartitionSpec as P

MASKED = -1e30
LOG2_E = 1.4426950408889634
VMEM_LIMIT = 32 * 1024 * 1024


def dot(a, b, contract):
    return lax.dot_general(a, b, ((contract[0], contract[1]), ((), ())), preferred_element_type=jnp.float32)


def attend_block(first_row, ends, q, g, k, v, reach, heads, scale):
    cols = q.shape[0]
    key_rows = k.shape[0]
    token = lax.broadcasted_iota(jnp.int32, (1, cols), 1) // heads
    query_pos = first_row + token
    doc_start = jnp.zeros((1, cols), jnp.int32)
    for end in ends:
        doc_start = jnp.maximum(doc_start, jnp.where(end <= query_pos, end, 0))
    low = doc_start - (first_row - reach)
    raw = dot(k, q, ((1,), (1,)))
    index = lax.broadcasted_iota(jnp.int32, (key_rows, cols), 0)
    allowed = index >= low
    allowed_late = jnp.logical_and(allowed[reach:], index[reach:] - reach <= token)
    raw = jnp.concatenate(
        [jnp.where(allowed[:reach], raw[:reach], MASKED), jnp.where(allowed_late, raw[reach:], MASKED)], axis=0
    )
    row_max = jnp.max(raw, axis=0, keepdims=True)
    weights = jnp.exp2((raw - row_max) * (scale * LOG2_E))
    inverse = 1.0 / jnp.sum(weights, axis=0, keepdims=True)
    attended_t = (dot(v, weights.astype(jnp.bfloat16), ((0,), (0,))) * inverse).astype(jnp.bfloat16)
    attended = attended_t.T
    g_t = g.T.astype(jnp.float32)
    delta = jnp.sum(g_t * attended_t.astype(jnp.float32), axis=0, keepdims=True)
    probs = weights * inverse
    products = dot(v, g, ((1,), (1,)))
    slopes = (probs * (products - delta)).astype(jnp.bfloat16)
    value_part = dot(probs.astype(jnp.bfloat16), g, ((1,), (0,)))
    key_part = dot(slopes, q, ((1,), (0,))) * scale
    query_grad = (dot(k, slopes, ((0,), (0,))) * scale).astype(jnp.bfloat16).T
    return attended, query_grad, key_part, value_part


class Plan:
    def __init__(self, n, rows, heads, width, ndocs):
        self.n, self.rows, self.heads, self.width, self.ndocs = n, rows, heads, width, ndocs
        self.back = n // 2
        self.block = rows // n
        self.cols = self.block * heads
        self.reach = self.back * rows
        self.scale = width ** (-0.5)
        self.lower = self.back + 1
        self.window_ranges = self.back + 2

    def ends(self, meta):
        return [meta[1 + i] for i in range(self.ndocs)]

    def slot(self, meta, loader, owner):
        return meta[1 + self.ndocs + loader * self.n + owner]

    def cost(self, blocks):
        return pl.CostEstimate(
            flops=14 * blocks * self.cols * (self.reach + self.block) * self.width * 8,
            bytes_accessed=blocks * self.cols * self.width * 16,
            transcendentals=blocks * self.cols * (self.reach + self.block),
        )


def fill_window(plan, own, refs, k_win, v_win):
    rows = plan.rows
    k_win[pl.ds(0, rows), :] = jnp.zeros((rows, plan.width), k_win.dtype)
    v_win[pl.ds(0, rows), :] = jnp.zeros((rows, plan.width), v_win.dtype)
    k_win[pl.ds(plan.back * rows, rows), :] = refs[0][pl.ds(0, rows), :]
    v_win[pl.ds(plan.back * rows, rows), :] = refs[0][pl.ds(rows, rows), :]
    for i in range(1, plan.back + 1):
        place = plan.back - i if i < plan.back else jnp.where(own == plan.back - 1, plan.back + 1, 0)
        to = pl.ds(pl.multiple_of(place * rows, rows), rows)
        k_win[to, :] = refs[2 * i - 1][...]
        v_win[to, :] = refs[2 * i][...]


def attend_at(plan, meta, loader, slot, q, g, k_win, v_win):
    start = (loader - meta[0]) * plan.rows + slot * plan.block
    keys_here = pl.ds(pl.multiple_of(start, plan.block), plan.reach + plan.block)
    out = attend_block(
        loader * plan.rows + slot * plan.block, plan.ends(meta), q, g, k_win[keys_here, :], v_win[keys_here, :],
        plan.reach, plan.heads, plan.scale,
    )
    return keys_here, out


def pack_kernel(plan, ends_ref, owners_ref, q_ref, g_ref, k_ref, v_ref, *refs):
    n = plan.n
    blocks, (kv, meta, sems, kv_sems) = refs[:n], refs[n:]
    own = lax.axis_index("ctx")
    copies = []
    for i, ref in enumerate((k_ref, v_ref)):
        to = kv.at[pl.ds(i * plan.rows, plan.rows), :]
        copies.append(pltpu.make_async_copy(ref, to, kv_sems.at[i]))
        copies[-1].start()

    def slots_of(loader):
        for slot in range(n):
            meta[1 + plan.ndocs + loader * n + owners_ref[loader, slot]] = slot

    slots_of(own)
    for apart in range(n - 1, -1, -1):
        slot = plan.slot(meta, own, own ^ apart)
        at = pl.ds(pl.multiple_of(slot * plan.cols, plan.cols), plan.cols)
        copies.append(pltpu.make_async_copy(q_ref.at[at, :], blocks[apart].at[0], sems.at[apart, 0]))
        copies.append(pltpu.make_async_copy(g_ref.at[at, :], blocks[apart].at[1], sems.at[apart, 1]))
        copies[-2].start()
        copies[-1].start()
    meta[0] = own
    end = jnp.int32(0)
    for i in range(plan.ndocs):
        end = end + ends_ref[i]
        meta[1 + i] = end
    for loader in range(n):
        slots_of(loader)
    for copy in copies:
        copy.wait()


def first_kernel(plan, apart, meta, qg, *refs):
    kv_refs, (pay_ref, grad_ref, k_win, v_win) = refs[:-4], refs[-4:]
    own = meta[0]
    slot = plan.slot(meta, own, own ^ apart)
    fill_window(plan, own, kv_refs, k_win, v_win)
    _, (attended, query_grad, key_part, value_part) = attend_at(
        plan, meta, own, slot, qg[0], qg[1], k_win, v_win
    )
    pay_ref[0] = attended
    pay_ref[1] = query_grad
    grad_ref[:, : plan.width] = key_part
    grad_ref[:, plan.width :] = value_part


def add_parts(plan, acc, keys_here, key_part, value_part):
    acc[keys_here, : plan.width] = acc[keys_here, : plan.width] + key_part
    acc[keys_here, plan.width :] = acc[keys_here, plan.width :] + value_part


def put_rows(plan, pay_ref, attended, query_grad):
    pay_ref[0] = attended
    pay_ref[1] = query_grad


def next_kernel(plan, first, items, meta, *refs):
    n = plan.n
    qg_refs, first_grad, refs = refs[: len(items)], refs[len(items)], refs[len(items) + 1 :]
    outs = len(items) + 3
    kv_refs, pay_refs, (acc, k_win, v_win) = refs[:-outs], refs[-outs:-3], refs[-3:]
    step = pl.program_id(0)
    own = meta[0]

    @pl.when(step == 0)
    def _():
        fill_window(plan, own, kv_refs, k_win, v_win)
        acc[...] = jnp.zeros_like(acc)
        slot = plan.slot(meta, own, own ^ first)
        start = pl.multiple_of(slot * plan.block, plan.block)
        acc[pl.ds(start, plan.reach + plan.block), :] = first_grad[...]

    for i, item in enumerate(items):
        here = step == i
        if item == n - 1:
            here = jnp.logical_and(here, own != plan.back)

        @pl.when(here)
        def _():
            slot = plan.slot(meta, own, own ^ item)
            keys_here, (attended, query_grad, *parts) = attend_at(
                plan, meta, own, slot, qg_refs[i][0], qg_refs[i][1], k_win, v_win
            )
            add_parts(plan, acc, keys_here, *parts)
            put_rows(plan, pay_refs[i], attended, query_grad)


def last_kernel(plan, meta, got_ref, acc_ref, *refs):
    n, block, rows = plan.n, plan.block, plan.rows
    kv_refs, (pay_ref, *grad_refs), (k_win, v_win, acc) = refs[:-8], refs[-8:-3], refs[-3:]
    own = meta[0]
    acc[...] = acc_ref[...]

    @pl.when(own == plan.back - 1)
    def _():
        fill_window(plan, own, kv_refs, k_win, v_win)
        keys_here, (attended, query_grad, *parts) = attend_at(
            plan, meta, own + 1, plan.slot(meta, own + 1, own), got_ref[0], got_ref[1], k_win, v_win
        )
        add_parts(plan, acc, keys_here, *parts)
        put_rows(plan, pay_ref, attended, query_grad)

    def put_part(key_range, entry, part):
        @pl.when(key_range < plan.lower)
        def _():
            grad_refs[2][entry, key_range] = part.astype(jnp.bfloat16)

        @pl.when(key_range >= plan.lower)
        def _():
            grad_refs[3][entry, key_range - plan.lower] = part.astype(jnp.bfloat16)

    def of_range(key_range, carry):
        at = lax.rem(key_range - own + plan.back + n, n) * rows
        for apart in range(n):
            slot = plan.slot(meta, key_range, own ^ apart)
            part = acc[pl.ds(pl.multiple_of(at + slot * block, block), block), :]
            if apart % 2 == 0:
                to = grad_refs[apart % 4 // 2]
                to[apart // 4, key_range] = part
            else:
                put_part(key_range, apart // 2, part)
        return carry

    lax.fori_loop(0, n, of_range, 0)


def spec_of(space):
    return pl.BlockSpec(memory_space=space)


def kernel_call(body, name, operands, spaces, out_shape, scratch, **more):
    return pl.pallas_call(
        body,
        out_shape=out_shape,
        in_specs=[spec_of(space) for space in spaces],
        compiler_params=pltpu.CompilerParams(vmem_limit_bytes=VMEM_LIMIT),
        scratch_shapes=scratch,
        name=name,
        **more,
    )(*operands)


def pack(plan, doc_lengths, block_owner, *operands):
    n = plan.n
    out_shape = [jax.ShapeDtypeStruct((2, plan.cols, plan.width), jnp.bfloat16)] * n
    out_shape.append(jax.ShapeDtypeStruct((2 * plan.rows, plan.width), jnp.bfloat16))
    out_shape.append(jax.ShapeDtypeStruct((1 + plan.ndocs + n * n,), jnp.int32))
    operands = [pltpu.with_memory_space_constraint(x, pltpu.HBM) for x in operands]
    return kernel_call(
        functools.partial(pack_kernel, plan), "pack", (doc_lengths, block_owner, *operands),
        [pltpu.SMEM] * 2 + [pl.ANY] * 4, out_shape,
        [pltpu.SemaphoreType.DMA((n, 2)), pltpu.SemaphoreType.DMA((2,))],
        out_specs=[spec_of(pltpu.VMEM)] * (n + 1) + [spec_of(pltpu.SMEM)],
    )


def attend_first(plan, apart, meta, qg, kv_list):
    window = pltpu.VMEM((plan.window_ranges * plan.rows, plan.width), jnp.bfloat16)
    out_shape = [
        jax.ShapeDtypeStruct((2, plan.cols, plan.width), jnp.bfloat16),
        jax.ShapeDtypeStruct((plan.reach + plan.block, 2 * plan.width), jnp.float32),
    ]
    operands = (meta, qg, *kv_list)
    return kernel_call(
        functools.partial(first_kernel, plan, apart), "attend_first", operands,
        [pltpu.SMEM] + [pltpu.VMEM] * (len(operands) - 1), out_shape, [window, window],
        out_specs=[spec_of(pltpu.VMEM)] * 2, cost_estimate=plan.cost(1),
    )


def attend_next(plan, first, items, meta, qg_list, first_grad, kv_list):
    window = pltpu.VMEM((plan.window_ranges * plan.rows, plan.width), jnp.bfloat16)
    out_shape = [jax.ShapeDtypeStruct((2, plan.cols, plan.width), jnp.bfloat16)] * len(items)
    out_shape.append(jax.ShapeDtypeStruct((plan.n * plan.rows, 2 * plan.width), jnp.float32))
    operands = (meta, *qg_list, first_grad, *kv_list)
    return kernel_call(
        functools.partial(next_kernel, plan, first, items), "attend_next", operands,
        [pltpu.SMEM] + [pltpu.VMEM] * (len(operands) - 1), out_shape, [window, window],
        out_specs=[spec_of(pltpu.VMEM)] * len(out_shape), cost_estimate=plan.cost(len(items)), grid=(len(items),),
    )


def attend_last(plan, meta, got, sums, kv_list):
    n = plan.n
    window = pltpu.VMEM((plan.window_ranges * plan.rows, plan.width), jnp.bfloat16)
    part = (plan.block, 2 * plan.width)
    keep = jax.ShapeDtypeStruct((n // 4, n, *part), jnp.float32)
    lower = jax.ShapeDtypeStruct((n // 2, plan.lower, *part), jnp.bfloat16)
    upper = jax.ShapeDtypeStruct((n // 2, n - plan.lower, *part), jnp.bfloat16)
    out_shape = [jax.ShapeDtypeStruct((2, plan.cols, plan.width), jnp.bfloat16), keep, keep, lower, upper]
    operands = (meta, got, sums, *kv_list)
    return kernel_call(
        functools.partial(last_kernel, plan), "attend_last", operands,
        [pltpu.SMEM] + [pltpu.VMEM] * (len(operands) - 1), out_shape,
        [window, window, pltpu.VMEM(sums.shape, jnp.float32)],
        out_specs=[spec_of(pltpu.VMEM)] * len(out_shape), cost_estimate=plan.cost(1),
    )


def place_kernel(plan, items, final, *refs):
    n, cols, width = plan.n, plan.cols, plan.width
    own = lax.axis_index("ctx")
    pay_refs, refs = refs[: len(items)], refs[len(items) :]
    if final:
        grads, (_, _, attended, query_grad, key_grad, value_grad, sums, sems, sum_sems) = refs[:-9], refs[-9:]
    else:
        grads, (attended, query_grad, send, kept, sems) = refs[:-5], refs[-5:]
    copies = []
    for i, item in enumerate(items):
        to = pl.ds(pl.multiple_of((own ^ (n - 1 if item == "got" else item)) * cols, cols), cols)
        pair = [
            pltpu.make_async_copy(pay_refs[i].at[0], attended.at[to, :], sems.at[i, 0]),
            pltpu.make_async_copy(pay_refs[i].at[1], query_grad.at[to, :], sems.at[i, 1]),
        ]
        if item in ("got", n - 1):
            copies += [(copy, (own == plan.back - 1) == (item == "got")) for copy in pair]
        else:
            copies += [(copy, None) for copy in pair]

    def each(act):
        for copy, here in copies:
            if here is None:
                act(copy)
            else:
                pl.when(here)(functools.partial(act, copy))

    each(lambda copy: copy.start())
    if final:
        total = sum(grad[...].astype(jnp.float32) for grad in grads).astype(jnp.bfloat16)
        sums[0] = total[:, :width]
        sums[1] = total[:, width:]
        for i, ref in enumerate((key_grad, value_grad)):
            copies.append((pltpu.make_async_copy(sums.at[i], ref, sum_sems.at[i]), None))
            copies[-1][0].start()
    else:
        pass_on, keep, *arrived = grads
        for entry in range(n // 2):
            for half, ref in enumerate(arrived):
                ranges = pl.ds(plan.lower, n - plan.lower) if half else pl.ds(0, plan.lower)
                total = (keep, pass_on)[entry % 2][entry // 2, ranges] + ref[entry].astype(jnp.float32)
                if entry % 2:
                    send[entry // 2, ranges] = total.astype(jnp.bfloat16)
                else:
                    kept[entry // 2, ranges] = total
    each(lambda copy: copy.wait())


def place(plan, payloads, grads, filled=()):
    items = tuple(payloads)
    big = jax.ShapeDtypeStruct((plan.rows * plan.heads, plan.width), jnp.bfloat16)
    small = jax.ShapeDtypeStruct((plan.rows, plan.width), jnp.bfloat16)
    final = len(filled) > 0
    at = len(items) + len(grads)
    scratch = [pltpu.SemaphoreType.DMA((len(items), 2))]
    if final:
        scratch = [pltpu.VMEM((2, plan.rows, plan.width), jnp.bfloat16), *scratch, pltpu.SemaphoreType.DMA((2,))]
    return kernel_call(
        functools.partial(place_kernel, plan, items, final), "place_last" if final else "place_first",
        (*payloads.values(), *grads, *filled),
        [pl.ANY] * len(items) + [pltpu.VMEM] * len(grads) + [pl.ANY] * len(filled),
        [big, big] + ([small, small] if final else [jax.ShapeDtypeStruct(grads[0].shape, t) for t in (jnp.bfloat16, jnp.float32)]), scratch,
        out_specs=[spec_of(pl.ANY)] * 2 + [spec_of(pl.ANY if final else pltpu.VMEM)] * 2,
        input_output_aliases={at: 0, at + 1: 1} if final else {},
        cost_estimate=plan.cost(len(items)),
    )


def on_device(query, keys, values, output_gradient, doc_lengths, block_owner):
    n = lax.axis_size("ctx")
    own = lax.axis_index("ctx")
    rows, heads, width = query.shape
    plan = Plan(n, rows, heads, width, doc_lengths.shape[0])

    def permuted(array, pairs):
        return lax.ppermute(array, "ctx", pairs)

    def across(array, bits):
        return permuted(array, [(i, i ^ bits) for i in range(n)])

    k = keys.reshape(rows, width)
    v = values.reshape(rows, width)
    kv_list = []
    for by in range(1, plan.back + 1):
        pairs = [(i, (i + by) % n) for i in range(n)]
        if by == plan.back:
            pairs = [(i, i + by if i < by else (i - by - 1) % by) for i in range(n)]
        kv_list += [permuted(k, pairs), permuted(v, pairs)]

    q, g = (x.reshape(rows * heads, width) for x in (query, output_gradient))
    *blocks, kv, meta = pack(plan, doc_lengths, block_owner, q, g, k, v)
    kv_list = [kv, *kv_list]
    got = permuted(blocks[n - 1], [(plan.back, plan.back - 1)])
    first = n // 2
    first_pay, first_grad = attend_first(plan, first, meta, blocks[first], kv_list)
    stay = {first: across(first_pay, first)}
    items = tuple(x for x in range(n - 1, -1, -1) if x != first)
    *pays, sums = attend_next(plan, first, items, meta, [blocks[x] for x in items], first_grad, kv_list)
    stay["got"], *out = attend_last(plan, meta, got, sums, kv_list)
    stay[0] = pays[-1]
    late = {n - 1: permuted(pays[0], [(i, i ^ (n - 1)) for i in range(n) if i != plan.back])}
    late.update({x: across(pay, x) for x, pay in zip(items[1:-1], pays[1:-1])})
    keep, pass_on, lower, upper = out
    upper = permuted(upper, [(i, i ^ 1) for i in range(plan.back, n)])
    attended, query_grad, send, keep = place(plan, stay, (pass_on, keep, across(lower, 1), upper))
    terms = (keep, across(send, 2))
    bit = 4
    while bit < n:
        total = sum(term.astype(jnp.float32) for term in terms)
        terms = (total[0::2], across(total[1::2].astype(jnp.bfloat16), bit))
        bit *= 2
    terms = [term.reshape(rows, 2 * width) for term in terms]
    attended, query_grad, key_grad, value_grad = place(plan, late, terms, (attended, query_grad))
    return (
        attended.reshape(rows, heads, width),
        query_grad.reshape(rows, heads, width),
        key_grad.reshape(rows, 1, width),
        value_grad.reshape(rows, 1, width),
    )


def solution(mesh):
    rows = P(("dp", "ctx"), "tp", None)
    return jax.shard_map(
        on_device,
        mesh=mesh,
        in_specs=(rows, rows, rows, rows, P("dp"), P("dp", None)),
        out_specs=(rows, rows, rows, rows),
        check_vma=False,
    )
```

```python
import functools
import jax
import jax.numpy as jnp
from jax import lax
from jax.experimental import pallas as pl
from jax.experimental.pallas import tpu as pltpu
from jax.sharding import PartitionSpec as P

MASKED = -1e30
LOG2_E = 1.4426950408889634
VMEM_LIMIT = 32 * 1024 * 1024


def dot(a, b, contract):
    return lax.dot_general(a, b, ((contract[0], contract[1]), ((), ())), preferred_element_type=jnp.float32)


def attend_block(first_row, skipped, ends, q, g, k, v, reach, heads, scale):
    cols = q.shape[0]
    key_rows = k.shape[0]
    token = lax.broadcasted_iota(jnp.int32, (1, cols), 1) // heads + skipped
    query_pos = first_row + token
    doc_start = jnp.zeros((1, cols), jnp.int32)
    for end in ends:
        doc_start = jnp.maximum(doc_start, jnp.where(end <= query_pos, end, 0))
    low = doc_start - (first_row - reach)
    raw = dot(k, q, ((1,), (1,)))
    index = lax.broadcasted_iota(jnp.int32, (key_rows, cols), 0)
    allowed = index >= low
    allowed_late = jnp.logical_and(allowed[reach:], index[reach:] - reach <= token)
    raw = jnp.concatenate(
        [jnp.where(allowed[:reach], raw[:reach], MASKED), jnp.where(allowed_late, raw[reach:], MASKED)], axis=0
    )
    row_max = jnp.max(raw, axis=0, keepdims=True)
    weights = jnp.exp2((raw - row_max) * (scale * LOG2_E))
    inverse = 1.0 / jnp.sum(weights, axis=0, keepdims=True)
    attended_t = (dot(v, weights.astype(jnp.bfloat16), ((0,), (0,))) * inverse).astype(jnp.bfloat16)
    attended = attended_t.T
    g_t = g.T.astype(jnp.float32)
    delta = jnp.sum(g_t * attended_t.astype(jnp.float32), axis=0, keepdims=True)
    probs = weights * inverse
    products = dot(v, g, ((1,), (1,)))
    slopes = (probs * (products - delta)).astype(jnp.bfloat16)
    value_part = dot(probs.astype(jnp.bfloat16), g, ((1,), (0,)))
    key_part = dot(slopes, q, ((1,), (0,))) * scale
    query_grad = (dot(k, slopes, ((0,), (0,))) * scale).astype(jnp.bfloat16).T
    return attended, query_grad, key_part, value_part


class Plan:
    def __init__(self, n, rows, heads, width, ndocs):
        self.n, self.rows, self.heads, self.width, self.ndocs = n, rows, heads, width, ndocs
        self.back = n // 2
        self.block = rows // n
        self.cols = self.block * heads
        self.reach = self.back * rows
        self.scale = width ** (-0.5)
        self.lower = self.back + 1
        self.half = self.cols // 2
        self.window_ranges = self.back + 3

    def is_middle(self, own):
        return jnp.logical_or(own == self.back - 1, own == self.back)

    def ends(self, meta):
        return [meta[1 + i] for i in range(self.ndocs)]

    def slot(self, meta, loader, owner):
        return meta[1 + self.ndocs + loader * self.n + owner]

    def cost(self, blocks):
        return pl.CostEstimate(
            flops=14 * blocks * self.cols * (self.reach + self.block) * self.width * 8,
            bytes_accessed=blocks * self.cols * self.width * 16,
            transcendentals=blocks * self.cols * (self.reach + self.block),
        )


def fill_window(plan, own, refs, k_win, v_win):
    rows, back = plan.rows, plan.back
    for win in (k_win, v_win):
        win[pl.ds(0, 2 * rows), :] = jnp.zeros((2 * rows, plan.width), win.dtype)
    k_win[pl.ds((back + 1) * rows, rows), :] = refs[0][pl.ds(0, rows), :]
    v_win[pl.ds((back + 1) * rows, rows), :] = refs[0][pl.ds(rows, rows), :]
    for i in range(1, back + 1):
        place = back + 1 - i if i < back else jnp.where(own == back - 1, back + 2, 1)
        to = pl.ds(pl.multiple_of(place * rows, rows), rows)
        k_win[to, :] = refs[2 * i - 1][...]
        v_win[to, :] = refs[2 * i][...]


def attend_at(plan, meta, loader, owner, q, g, k_win, v_win, skipped=0):
    slot = plan.slot(meta, loader, owner)
    start = (loader - meta[0] + 1) * plan.rows + slot * plan.block
    keys_here = pl.ds(pl.multiple_of(start, plan.block), plan.reach + plan.block)
    out = attend_block(
        loader * plan.rows + slot * plan.block, skipped, plan.ends(meta), q, g, k_win[keys_here, :],
        v_win[keys_here, :], plan.reach, plan.heads, plan.scale,
    )
    return keys_here, out


def pack_kernel(plan, ends_ref, owners_ref, q_ref, g_ref, k_ref, v_ref, *refs):
    n = plan.n
    blocks, (kv, meta, sems, kv_sems) = refs[: n + 1], refs[n + 1 :]
    own = lax.axis_index("ctx")
    copies = []
    for i, ref in enumerate((k_ref, v_ref)):
        to = kv.at[pl.ds(i * plan.rows, plan.rows), :]
        copies.append(pltpu.make_async_copy(ref, to, kv_sems.at[i]))
        copies[-1].start()

    def slots_of(loader):
        for slot in range(n):
            meta[1 + plan.ndocs + loader * n + owners_ref[loader, slot]] = slot

    slots_of(own)
    for i in range(n, -1, -1):
        apart, size = min(i, n - 1), blocks[i].shape[1]
        at = plan.slot(meta, own, own ^ apart) * plan.cols + (i - apart) * plan.half
        at = pl.ds(pl.multiple_of(at, plan.half), size)
        copies.append(pltpu.make_async_copy(q_ref.at[at, :], blocks[i].at[0], sems.at[i, 0]))
        copies.append(pltpu.make_async_copy(g_ref.at[at, :], blocks[i].at[1], sems.at[i, 1]))
        copies[-2].start()
        copies[-1].start()
    meta[0] = own
    end = jnp.int32(0)
    for i in range(plan.ndocs):
        end = end + ends_ref[i]
        meta[1 + i] = end
    for loader in range(n):
        slots_of(loader)
    for copy in copies:
        copy.wait()


def first_kernel(plan, apart, meta, qg, *refs):
    kv_refs, (pay_ref, grad_ref, k_win, v_win) = refs[:-4], refs[-4:]
    own = meta[0]
    fill_window(plan, own, kv_refs, k_win, v_win)
    _, (attended, query_grad, key_part, value_part) = attend_at(
        plan, meta, own, own ^ apart, qg[0], qg[1], k_win, v_win
    )
    pay_ref[0] = attended
    pay_ref[1] = query_grad
    grad_ref[:, : plan.width] = key_part
    grad_ref[:, plan.width :] = value_part


def add_parts(plan, acc, keys_here, key_part, value_part):
    acc[keys_here, : plan.width] = acc[keys_here, : plan.width] + key_part
    acc[keys_here, plan.width :] = acc[keys_here, plan.width :] + value_part


def put_rows(plan, pay_ref, attended, query_grad):
    pay_ref[0] = attended
    pay_ref[1] = query_grad


def next_kernel(plan, first, items, meta, *refs):
    n = plan.n
    qg_refs, first_grad, refs = refs[: len(items)], refs[len(items)], refs[len(items) + 1 :]
    outs = len(items) + 3
    kv_refs, pay_refs, (acc, k_win, v_win) = refs[:-outs], refs[-outs:-3], refs[-3:]
    step = pl.program_id(0)
    own = meta[0]

    @pl.when(step == 0)
    def _():
        fill_window(plan, own, kv_refs, k_win, v_win)
        acc[...] = jnp.zeros_like(acc)
        start = pl.multiple_of(plan.rows + plan.slot(meta, own, own ^ first) * plan.block, plan.block)
        acc[pl.ds(start, plan.reach + plan.block), :] = first_grad[...]

    for i, item in enumerate(items):

        @pl.when(step == i)
        def _():
            keys_here, (attended, query_grad, *parts) = attend_at(
                plan, meta, own, own ^ item, qg_refs[i][0], qg_refs[i][1], k_win, v_win,
                plan.block // 2 if item == n - 1 else 0,
            )
            add_parts(plan, acc, keys_here, *parts)
            put_rows(plan, pay_refs[i], attended, query_grad)


def last_kernel(plan, meta, own_ref, got_ref, acc_ref, *refs):
    n, block, rows = plan.n, plan.block, plan.rows
    kv_refs, (pay_ref, *grad_refs), (k_win, v_win, acc, qg) = refs[:-9], refs[-9:-4], refs[-4:]
    own = meta[0]
    middle = plan.is_middle(own)

    @pl.when(middle)
    def _():
        qg[...] = got_ref[...]

    @pl.when(jnp.logical_not(middle))
    def _():
        qg[...] = own_ref[...]

    acc[...] = acc_ref[...]
    fill_window(plan, own, kv_refs, k_win, v_win)
    other = own ^ (n - 1)
    keys_here, (attended, query_grad, *parts) = attend_at(
        plan, meta, jnp.where(middle, other, own), jnp.where(middle, own, other), qg[0], qg[1], k_win, v_win
    )
    add_parts(plan, acc, keys_here, *parts)
    put_rows(plan, pay_ref, attended, query_grad)

    def put_part(key_range, entry, part):
        @pl.when(key_range < plan.lower)
        def _():
            grad_refs[2][entry, key_range] = part.astype(jnp.bfloat16)

        @pl.when(key_range >= plan.lower)
        def _():
            grad_refs[3][entry, key_range - plan.lower] = part.astype(jnp.bfloat16)

    def of_range(key_range, carry):
        at = (lax.rem(key_range - own + plan.back + n, n) + 1) * rows
        for apart in range(n):
            slot = plan.slot(meta, key_range, own ^ apart)
            part = acc[pl.ds(pl.multiple_of(at + slot * block, block), block), :]
            if apart % 2 == 0:
                to = grad_refs[apart % 4 // 2]
                to[apart // 4, key_range] = part
            else:
                put_part(key_range, apart // 2, part)
        return carry

    lax.fori_loop(0, n, of_range, 0)


def spec_of(space):
    return pl.BlockSpec(memory_space=space)


def kernel_call(body, name, operands, spaces, out_shape, scratch, **more):
    return pl.pallas_call(
        body,
        out_shape=out_shape,
        in_specs=[spec_of(space) for space in spaces],
        compiler_params=pltpu.CompilerParams(vmem_limit_bytes=VMEM_LIMIT),
        scratch_shapes=scratch,
        name=name,
        **more,
    )(*operands)


def pack(plan, doc_lengths, block_owner, *operands):
    n = plan.n
    sizes = [plan.cols] * (n - 1) + [plan.half] * 2
    out_shape = [jax.ShapeDtypeStruct((2, size, plan.width), jnp.bfloat16) for size in sizes]
    out_shape.append(jax.ShapeDtypeStruct((2 * plan.rows, plan.width), jnp.bfloat16))
    out_shape.append(jax.ShapeDtypeStruct((1 + plan.ndocs + n * n,), jnp.int32))
    operands = [pltpu.with_memory_space_constraint(x, pltpu.HBM) for x in operands]
    return kernel_call(
        functools.partial(pack_kernel, plan), "pack", (doc_lengths, block_owner, *operands),
        [pltpu.SMEM] * 2 + [pl.ANY] * 4, out_shape,
        [pltpu.SemaphoreType.DMA((n + 1, 2)), pltpu.SemaphoreType.DMA((2,))],
        out_specs=[spec_of(pltpu.VMEM)] * (n + 2) + [spec_of(pltpu.SMEM)],
    )


def attend_first(plan, apart, meta, qg, kv_list):
    window = pltpu.VMEM((plan.window_ranges * plan.rows, plan.width), jnp.bfloat16)
    out_shape = [
        jax.ShapeDtypeStruct((2, plan.cols, plan.width), jnp.bfloat16),
        jax.ShapeDtypeStruct((plan.reach + plan.block, 2 * plan.width), jnp.float32),
    ]
    operands = (meta, qg, *kv_list)
    return kernel_call(
        functools.partial(first_kernel, plan, apart), "attend_first", operands,
        [pltpu.SMEM] + [pltpu.VMEM] * (len(operands) - 1), out_shape, [window, window],
        out_specs=[spec_of(pltpu.VMEM)] * 2, cost_estimate=plan.cost(1),
    )


def attend_next(plan, first, items, meta, qg_list, first_grad, kv_list):
    window = pltpu.VMEM((plan.window_ranges * plan.rows, plan.width), jnp.bfloat16)
    out_shape = [jax.ShapeDtypeStruct(qg.shape, jnp.bfloat16) for qg in qg_list]
    out_shape.append(jax.ShapeDtypeStruct(((plan.n + 1) * plan.rows, 2 * plan.width), jnp.float32))
    operands = (meta, *qg_list, first_grad, *kv_list)
    return kernel_call(
        functools.partial(next_kernel, plan, first, items), "attend_next", operands,
        [pltpu.SMEM] + [pltpu.VMEM] * (len(operands) - 1), out_shape, [window, window],
        out_specs=[spec_of(pltpu.VMEM)] * len(out_shape), cost_estimate=plan.cost(len(items)), grid=(len(items),),
    )


def attend_last(plan, meta, qg, got, sums, kv_list):
    n = plan.n
    window = pltpu.VMEM((plan.window_ranges * plan.rows, plan.width), jnp.bfloat16)
    part = (plan.block, 2 * plan.width)
    keep = jax.ShapeDtypeStruct((n // 4, n, *part), jnp.float32)
    lower = jax.ShapeDtypeStruct((n // 2, plan.lower, *part), jnp.bfloat16)
    upper = jax.ShapeDtypeStruct((n // 2, n - plan.lower, *part), jnp.bfloat16)
    out_shape = [jax.ShapeDtypeStruct(qg.shape, jnp.bfloat16), keep, keep, lower, upper]
    operands = (meta, qg, got, sums, *kv_list)
    return kernel_call(
        functools.partial(last_kernel, plan), "attend_last", operands,
        [pltpu.SMEM] + [pltpu.VMEM] * (len(operands) - 1), out_shape,
        [window, window, pltpu.VMEM(sums.shape, jnp.float32), pltpu.VMEM(qg.shape, jnp.bfloat16)],
        out_specs=[spec_of(pltpu.VMEM)] * len(out_shape), cost_estimate=plan.cost(1),
    )


def place_kernel(plan, items, final, *refs):
    n, cols, width = plan.n, plan.cols, plan.width
    own = lax.axis_index("ctx")
    pay_refs, refs = refs[: len(items)], refs[len(items) :]
    if final:
        grads, (_, _, attended, query_grad, key_grad, value_grad, sums, sems, sum_sems) = refs[:-9], refs[-9:]
    else:
        grads, (attended, query_grad, send, kept, sems) = refs[:-5], refs[-5:]
    middle = plan.is_middle(own)
    copies = []
    for i, (x, skipped, on_middle) in enumerate(items):
        here = None if on_middle is None else middle if on_middle else jnp.logical_not(middle)
        to = pl.ds(pl.multiple_of((own ^ x) * cols + skipped, plan.half), pay_refs[i].shape[1])
        copies.append((pltpu.make_async_copy(pay_refs[i].at[0], attended.at[to, :], sems.at[i, 0]), here))
        copies.append((pltpu.make_async_copy(pay_refs[i].at[1], query_grad.at[to, :], sems.at[i, 1]), here))

    def each(act):
        for copy, here in copies:
            if here is None:
                act(copy)
            else:
                pl.when(here)(functools.partial(act, copy))

    each(lambda copy: copy.start())
    if final:
        total = sum(grad[...].astype(jnp.float32) for grad in grads).astype(jnp.bfloat16)
        sums[0] = total[:, :width]
        sums[1] = total[:, width:]
        for i, ref in enumerate((key_grad, value_grad)):
            copies.append((pltpu.make_async_copy(sums.at[i], ref, sum_sems.at[i]), None))
            copies[-1][0].start()
    else:
        pass_on, keep, *arrived = grads
        for entry in range(n // 2):
            for half, ref in enumerate(arrived):
                ranges = pl.ds(plan.lower, n - plan.lower) if half else pl.ds(0, plan.lower)
                total = (keep, pass_on)[entry % 2][entry // 2, ranges] + ref[entry].astype(jnp.float32)
                if entry % 2:
                    send[entry // 2, ranges] = total.astype(jnp.bfloat16)
                else:
                    kept[entry // 2, ranges] = total
    each(lambda copy: copy.wait())


def place(plan, payloads, grads, filled=()):
    items = tuple(payloads)
    big = jax.ShapeDtypeStruct((plan.rows * plan.heads, plan.width), jnp.bfloat16)
    small = jax.ShapeDtypeStruct((plan.rows, plan.width), jnp.bfloat16)
    final = len(filled) > 0
    at = len(items) + len(grads)
    scratch = [pltpu.SemaphoreType.DMA((len(items), 2))]
    if final:
        scratch = [pltpu.VMEM((2, plan.rows, plan.width), jnp.bfloat16), *scratch, pltpu.SemaphoreType.DMA((2,))]
    return kernel_call(
        functools.partial(place_kernel, plan, items, final), "place_last" if final else "place_first",
        (*payloads.values(), *grads, *filled),
        [pl.ANY] * len(items) + [pltpu.VMEM] * len(grads) + [pl.ANY] * len(filled),
        [big, big] + ([small, small] if final else [jax.ShapeDtypeStruct(grads[0].shape, t) for t in (jnp.bfloat16, jnp.float32)]), scratch,
        out_specs=[spec_of(pl.ANY)] * 2 + [spec_of(pl.ANY if final else pltpu.VMEM)] * 2,
        input_output_aliases={at: 0, at + 1: 1} if final else {},
        cost_estimate=plan.cost(len(items)),
    )


def on_device(query, keys, values, output_gradient, doc_lengths, block_owner):
    n = lax.axis_size("ctx")
    own = lax.axis_index("ctx")
    rows, heads, width = query.shape
    plan = Plan(n, rows, heads, width, doc_lengths.shape[0])

    def permuted(array, pairs):
        return lax.ppermute(array, "ctx", pairs)

    def across(array, bits):
        return permuted(array, [(i, i ^ bits) for i in range(n)])

    k = keys.reshape(rows, width)
    v = values.reshape(rows, width)
    kv_list = []
    for by in range(1, plan.back + 1):
        pairs = [(i, (i + by) % n) for i in range(n)]
        if by == plan.back:
            pairs = [(i, i + by if i < by else (i - by - 1) % by) for i in range(n)]
        kv_list += [permuted(k, pairs), permuted(v, pairs)]

    q, g = (x.reshape(rows * heads, width) for x in (query, output_gradient))
    *blocks, kv, meta = pack(plan, doc_lengths, block_owner, q, g, k, v)
    kv_list = [kv, *kv_list]
    half = plan.half
    pairs = [(plan.back - 1, plan.back), (plan.back, plan.back - 1)]
    got = permuted(blocks[n - 1], pairs)
    first = n // 2
    first_pay, first_grad = attend_first(plan, first, meta, blocks[first], kv_list)
    first_pay = across(first_pay, first)
    items = tuple(x for x in range(n - 1, -1, -1) if x != first)
    qg_list = [blocks[n], *[blocks[x] for x in items[1:]]]
    *pays, sums = attend_next(plan, first, items, meta, qg_list, first_grad, kv_list)
    last_pay, *out = attend_last(plan, meta, blocks[n - 1], got, sums, kv_list)
    stay = {(first, 0, None): first_pay, (0, 0, None): pays[-1], (n - 1, 0, True): last_pay}
    late = {
        (n - 1, 0, False): permuted(last_pay, [(i, i ^ (n - 1)) for i in range(n) if (i, i ^ (n - 1)) not in pairs]),
        (n - 1, half, None): across(pays[0], n - 1),
    }
    late.update({(x, 0, None): across(pay, x) for x, pay in zip(items[1:-1], pays[1:-1])})
    keep, pass_on, lower, upper = out
    upper = permuted(upper, [(i, i ^ 1) for i in range(plan.back, n)])
    attended, query_grad, send, keep = place(plan, stay, (pass_on, keep, across(lower, 1), upper))
    terms = (keep, across(send, 2))
    bit = 4
    while bit < n:
        total = sum(term.astype(jnp.float32) for term in terms)
        terms = (total[0::2], across(total[1::2].astype(jnp.bfloat16), bit))
        bit *= 2
    terms = [term.reshape(rows, 2 * width) for term in terms]
    attended, query_grad, key_grad, value_grad = place(plan, late, terms, (attended, query_grad))
    return (
        attended.reshape(rows, heads, width),
        query_grad.reshape(rows, heads, width),
        key_grad.reshape(rows, 1, width),
        value_grad.reshape(rows, 1, width),
    )


def solution(mesh):
    rows = P(("dp", "ctx"), "tp", None)
    return jax.shard_map(
        on_device,
        mesh=mesh,
        in_specs=(rows, rows, rows, rows, P("dp"), P("dp", None)),
        out_specs=(rows, rows, rows, rows),
        check_vma=False,
    )
```

```python
import functools
import jax
import jax.numpy as jnp
from jax import lax
from jax.experimental import pallas as pl
from jax.experimental.pallas import tpu as pltpu
from jax.sharding import PartitionSpec as P

MASKED = -1e30
LOG2_E = 1.4426950408889634
VMEM_LIMIT = 32 * 1024 * 1024


def dot(a, b, contract):
    return lax.dot_general(a, b, ((contract[0], contract[1]), ((), ())), preferred_element_type=jnp.float32)


def attend_block(first_row, ends, q, g, k, v, reach, heads, scale):
    cols = q.shape[0]
    key_rows = k.shape[0]
    token = lax.broadcasted_iota(jnp.int32, (1, cols), 1) // heads
    query_pos = first_row + token
    doc_start = jnp.zeros((1, cols), jnp.int32)
    for end in ends:
        doc_start = jnp.maximum(doc_start, jnp.where(end <= query_pos, end, 0))
    low = doc_start - (first_row - reach)
    raw = dot(k, q, ((1,), (1,)))
    index = lax.broadcasted_iota(jnp.int32, (key_rows, cols), 0)
    allowed = index >= low
    allowed_late = jnp.logical_and(allowed[reach:], index[reach:] - reach <= token)
    raw = jnp.concatenate(
        [jnp.where(allowed[:reach], raw[:reach], MASKED), jnp.where(allowed_late, raw[reach:], MASKED)], axis=0
    )
    row_max = jnp.max(raw, axis=0, keepdims=True)
    weights = jnp.exp2((raw - row_max) * (scale * LOG2_E))
    inverse = 1.0 / jnp.sum(weights, axis=0, keepdims=True)
    attended_t = (dot(v, weights.astype(jnp.bfloat16), ((0,), (0,))) * inverse).astype(jnp.bfloat16)
    attended = attended_t.T
    g_t = g.T.astype(jnp.float32)
    delta = jnp.sum(g_t * attended_t.astype(jnp.float32), axis=0, keepdims=True)
    probs = weights * inverse
    products = dot(v, g, ((1,), (1,)))
    slopes = (probs * (products - delta)).astype(jnp.bfloat16)
    value_part = dot(probs.astype(jnp.bfloat16), g, ((1,), (0,)))
    key_part = dot(slopes, q, ((1,), (0,))) * scale
    query_grad = (dot(k, slopes, ((0,), (0,))) * scale).astype(jnp.bfloat16).T
    return attended, query_grad, key_part, value_part


class Plan:
    def __init__(self, n, rows, heads, width, ndocs):
        self.n, self.rows, self.heads, self.width, self.ndocs = n, rows, heads, width, ndocs
        self.back = n // 2
        self.block = rows // n
        self.cols = self.block * heads
        self.reach = self.back * rows
        self.scale = width ** (-0.5)
        self.window_ranges = self.back + 1

    def ends(self, meta):
        return [meta[1 + i] for i in range(self.ndocs)]

    def slot(self, meta, loader, owner):
        return meta[1 + self.ndocs + loader * self.n + owner]

    def cost(self, blocks):
        return pl.CostEstimate(
            flops=14 * blocks * self.cols * (self.reach + self.block) * self.width * 8,
            bytes_accessed=blocks * self.cols * self.width * 16,
            transcendentals=blocks * self.cols * (self.reach + self.block),
        )


def fill_window(plan, refs, k_win, v_win):
    rows = plan.rows
    k_win[pl.ds(plan.back * rows, rows), :] = refs[0][pl.ds(0, rows), :]
    v_win[pl.ds(plan.back * rows, rows), :] = refs[0][pl.ds(rows, rows), :]
    for i in range(1, plan.back + 1):
        to = pl.ds((plan.back - i) * rows, rows)
        k_win[to, :] = refs[2 * i - 1][...]
        v_win[to, :] = refs[2 * i][...]


def attend_at(plan, meta, loader, slot, q, g, k_win, v_win):
    start = (loader - meta[0]) * plan.rows + slot * plan.block
    keys_here = pl.ds(pl.multiple_of(start, plan.block), plan.reach + plan.block)
    out = attend_block(
        loader * plan.rows + slot * plan.block, plan.ends(meta), q, g, k_win[keys_here, :], v_win[keys_here, :],
        plan.reach, plan.heads, plan.scale,
    )
    return keys_here, out


def pack_kernel(plan, meta, q_ref, g_ref, k_ref, v_ref, *refs):
    blocks, (kv, sems, kv_sems) = refs[: plan.n], refs[plan.n :]
    own = meta[0]
    copies = []
    for apart, block in enumerate(blocks):
        slot = plan.slot(meta, own, own ^ apart)
        at = pl.ds(pl.multiple_of(slot * plan.cols, plan.cols), plan.cols)
        copies.append(pltpu.make_async_copy(q_ref.at[at, :], block.at[0], sems.at[apart, 0]))
        copies.append(pltpu.make_async_copy(g_ref.at[at, :], block.at[1], sems.at[apart, 1]))
    for i, ref in enumerate((k_ref, v_ref)):
        to = kv.at[pl.ds(i * plan.rows, plan.rows), :]
        copies.append(pltpu.make_async_copy(ref, to, kv_sems.at[i]))
    for copy in copies:
        copy.start()
    for copy in copies:
        copy.wait()


def first_kernel(plan, entries, meta, *refs):
    count = len(entries)
    qg_refs, kv_refs = refs[:count], refs[count : -2 * count - 2]
    pay_refs, grad_refs, (k_win, v_win) = refs[-2 * count - 2 : -count - 2], refs[-count - 2 : -2], refs[-2:]
    own = meta[0]
    fill_window(plan, kv_refs, k_win, v_win)
    for apart, qg, pay_ref, grad_ref in zip(entries, qg_refs, pay_refs, grad_refs):
        slot = plan.slot(meta, own, own ^ apart)
        _, (attended, query_grad, key_part, value_part) = attend_at(
            plan, meta, own, slot, qg[0], qg[1], k_win, v_win
        )
        pay_ref[0] = attended
        pay_ref[1] = query_grad
        grad_ref[:, : plan.width] = key_part
        grad_ref[:, plan.width :] = value_part


def last_kernel(plan, done, items, meta, *refs):
    n, width, rows, block = plan.n, plan.width, plan.rows, plan.block
    qg_refs, refs = refs[: len(items)], refs[len(items) :]
    done_refs, refs = refs[: len(done)], refs[len(done) :]
    kv_refs, refs = refs[: -(len(items) + 7)], refs[-(len(items) + 7) :]
    pay_refs, grad_refs, (k_win, v_win, acc) = refs[: len(items)], refs[len(items) : -3], refs[-3:]
    step = pl.program_id(0)
    own = meta[0]

    @pl.when(step == 0)
    def _():
        fill_window(plan, kv_refs, k_win, v_win)
        acc[...] = jnp.zeros_like(acc)
        for x, grad_ref in zip(done, done_refs):
            slot = plan.slot(meta, own, own ^ x)
            keys_here = pl.ds(pl.multiple_of(slot * block, block), plan.reach + block)
            acc[keys_here, :] = acc[keys_here, :] + grad_ref[...]

    for i, item in enumerate(items):

        @pl.when(step == i)
        def _():
            slot = plan.slot(meta, own, own ^ item)
            qg = qg_refs[i]
            keys_here, (attended, query_grad, key_part, value_part) = attend_at(
                plan, meta, own, slot, qg[0], qg[1], k_win, v_win
            )
            acc[keys_here, :width] = acc[keys_here, :width] + key_part
            acc[keys_here, width:] = acc[keys_here, width:] + value_part
            pay_refs[i][0] = attended
            pay_refs[i][1] = query_grad

    @pl.when(step == len(items) - 1)
    def _():
        def put_part(key_range, entry, part):
            @pl.when(key_range < n // 2)
            def _():
                grad_refs[2][entry, key_range] = part.astype(jnp.bfloat16)

            @pl.when(key_range >= n // 2)
            def _():
                grad_refs[3][entry, key_range - n // 2] = part.astype(jnp.bfloat16)

        def of_range(key_range, carry):
            at = lax.rem(key_range - own + plan.back + n, n) * rows
            for apart in range(n):
                slot = plan.slot(meta, key_range, own ^ apart)
                part = acc[pl.ds(pl.multiple_of(at + slot * block, block), block), :]
                if apart % 2 == 0:
                    to = grad_refs[apart % 4 // 2]
                    to[apart // 4, key_range] = part
                else:
                    put_part(key_range, apart // 2, part)
            return carry

        lax.fori_loop(0, n, of_range, 0)


def spec_of(space):
    return pl.BlockSpec(memory_space=space)


def kernel_call(body, name, operands, spaces, out_shape, scratch, **more):
    return pl.pallas_call(
        body,
        out_shape=out_shape,
        in_specs=[spec_of(space) for space in spaces],
        compiler_params=pltpu.CompilerParams(vmem_limit_bytes=VMEM_LIMIT),
        scratch_shapes=scratch,
        name=name,
        **more,
    )(*operands)


def pack(plan, meta, *operands):
    out_shape = [jax.ShapeDtypeStruct((2, plan.cols, plan.width), jnp.bfloat16)] * plan.n
    out_shape.append(jax.ShapeDtypeStruct((2 * plan.rows, plan.width), jnp.bfloat16))
    operands = [pltpu.with_memory_space_constraint(x, pltpu.HBM) for x in operands]
    return kernel_call(
        functools.partial(pack_kernel, plan), "pack", (meta, *operands), [pltpu.SMEM] + [pl.ANY] * 4, out_shape,
        [pltpu.SemaphoreType.DMA((plan.n, 2)), pltpu.SemaphoreType.DMA((2,))],
        out_specs=[spec_of(pltpu.VMEM)] * len(out_shape),
    )


def attend_first(plan, entries, meta, qg_list, kv_list):
    window = pltpu.VMEM((plan.window_ranges * plan.rows, plan.width), jnp.bfloat16)
    rows = jax.ShapeDtypeStruct((2, plan.cols, plan.width), jnp.bfloat16)
    grad = jax.ShapeDtypeStruct((plan.reach + plan.block, 2 * plan.width), jnp.float32)
    out_shape = [rows] * len(entries) + [grad] * len(entries)
    operands = (meta, *qg_list, *kv_list)
    return kernel_call(
        functools.partial(first_kernel, plan, entries), "attend_first", operands,
        [pltpu.SMEM] + [pltpu.VMEM] * (len(operands) - 1), out_shape, [window, window],
        out_specs=[spec_of(pltpu.VMEM)] * len(out_shape), cost_estimate=plan.cost(len(entries)),
    )


def attend_last(plan, done, items, meta, qg_list, done_grads, kv_list):
    n = plan.n
    window = pltpu.VMEM((plan.window_ranges * plan.rows, plan.width), jnp.bfloat16)
    keep = jax.ShapeDtypeStruct((n // 4, n, plan.block, 2 * plan.width), jnp.float32)
    send = jax.ShapeDtypeStruct((n // 2, n // 2, plan.block, 2 * plan.width), jnp.bfloat16)
    out_shape = [jax.ShapeDtypeStruct((2, plan.cols, plan.width), jnp.bfloat16)] * len(items)
    out_shape += [keep, keep, send, send]
    operands = (meta, *qg_list, *done_grads, *kv_list)
    return kernel_call(
        functools.partial(last_kernel, plan, done, items), "attend_last", operands,
        [pltpu.SMEM] + [pltpu.VMEM] * (len(operands) - 1), out_shape,
        [window, window, pltpu.VMEM((n * plan.rows, 2 * plan.width), jnp.float32)],
        out_specs=[spec_of(pltpu.VMEM)] * len(out_shape), cost_estimate=plan.cost(len(items)), grid=(len(items),),
    )


def place_kernel(plan, items, final, *refs):
    n, cols, width = plan.n, plan.cols, plan.width
    own = lax.axis_index("ctx")
    pay_refs, refs = refs[: len(items)], refs[len(items) :]
    if final:
        grads, (_, _, attended, query_grad, key_grad, value_grad, sums, sems, sum_sems) = refs[:-9], refs[-9:]
    else:
        grads, (attended, query_grad, send, kept, sems) = refs[:-5], refs[-5:]
    copies = []
    for i, item in enumerate(items):
        to = pl.ds(pl.multiple_of((own ^ item) * cols, cols), cols)
        copies.append(pltpu.make_async_copy(pay_refs[i].at[0], attended.at[to, :], sems.at[i, 0]))
        copies.append(pltpu.make_async_copy(pay_refs[i].at[1], query_grad.at[to, :], sems.at[i, 1]))
    for copy in copies:
        copy.start()
    if final:
        total = sum(grad[...].astype(jnp.float32) for grad in grads).astype(jnp.bfloat16)
        sums[0] = total[:, :width]
        sums[1] = total[:, width:]
        for i, ref in enumerate((key_grad, value_grad)):
            copies.append(pltpu.make_async_copy(sums.at[i], ref, sum_sems.at[i]))
            copies[-1].start()
    else:
        pass_on, keep, *arrived = grads
        for entry in range(n // 2):
            for half, ref in enumerate(arrived):
                ranges = pl.ds(half * (n // 2), n // 2)
                total = (keep, pass_on)[entry % 2][entry // 2, ranges] + ref[entry].astype(jnp.float32)
                if entry % 2:
                    send[entry // 2, ranges] = total.astype(jnp.bfloat16)
                else:
                    kept[entry // 2, ranges] = total
    for copy in copies:
        copy.wait()


def place(plan, payloads, grads, filled=(), final=False):
    items = tuple(payloads)
    out_shape = [jax.ShapeDtypeStruct((plan.rows * plan.heads, plan.width), jnp.bfloat16)] * 2
    out_specs = [spec_of(pl.ANY)] * 2
    scratch = [pltpu.SemaphoreType.DMA((len(items), 2))]
    if final:
        out_shape += [jax.ShapeDtypeStruct((plan.rows, plan.width), jnp.bfloat16)] * 2
        out_specs += [spec_of(pl.ANY)] * 2
        scratch = [pltpu.VMEM((2, plan.rows, plan.width), jnp.bfloat16), *scratch, pltpu.SemaphoreType.DMA((2,))]
    else:
        out_shape += [jax.ShapeDtypeStruct(grads[0].shape, kind) for kind in (jnp.bfloat16, jnp.float32)]
        out_specs += [spec_of(pltpu.VMEM)] * 2
    at = len(items) + len(grads)
    return kernel_call(
        functools.partial(place_kernel, plan, items, final), "place_" + "_".join(map(str, items)),
        (*payloads.values(), *grads, *filled),
        [pl.ANY] * len(items) + [pltpu.VMEM] * len(grads) + [pl.ANY] * len(filled),
        out_shape, scratch, out_specs=out_specs, input_output_aliases={at: 0, at + 1: 1} if filled else {},
        cost_estimate=plan.cost(len(items)),
    )


def on_device(query, keys, values, output_gradient, doc_lengths, block_owner):
    n = lax.axis_size("ctx")
    own = lax.axis_index("ctx")
    rows, heads, width = query.shape
    plan = Plan(n, rows, heads, width, doc_lengths.shape[0])

    def permuted(array, pairs):
        return lax.ppermute(array, "ctx", pairs)

    def across(array, bits):
        return permuted(array, [(i, i ^ bits) for i in range(n)])

    k = keys.reshape(rows, width)
    v = values.reshape(rows, width)
    kv_list = []
    for by in range(1, plan.back + 1):
        pairs = [(i, (i + by) % n) for i in range(n)]
        kv_list += [permuted(k, pairs), permuted(v, pairs)]

    owners = jnp.arange(n, dtype=jnp.int32)
    match = block_owner[:, None, :] == owners[None, :, None]
    table = jnp.sum(jnp.where(match, owners, 0), axis=2)
    meta = jnp.concatenate(
        [own.reshape(1).astype(jnp.int32), jnp.cumsum(doc_lengths).astype(jnp.int32), table.reshape(-1)]
    )

    q, g = (x.reshape(rows * heads, width) for x in (query, output_gradient))
    *blocks, kv = pack(plan, meta, q, g, k, v)
    kv_list = [kv, *kv_list]
    first = (n // 2, 1)
    first_pay, near_pay, *first_grads = attend_first(plan, first, meta, [blocks[x] for x in first], kv_list)
    stay = {x: across(pay, x) for x, pay in zip(first, (first_pay, near_pay))}
    sent = [x for x in range(1, n) if x not in first]
    items = (*sent, 0)
    out = attend_last(plan, first, items, meta, [blocks[x] for x in items], first_grads, kv_list)
    late = {x: across(pay, x) for x, pay in zip(sent, out)}
    stay[0] = out[len(sent)]
    keep, pass_on, lower, upper = out[len(items) :]
    upper = permuted(upper, [(i, i ^ 1) for i in range(n // 2, n)])
    *filled, send, keep = place(plan, stay, (pass_on, keep, across(lower, 1), upper))
    terms = (keep, across(send, 2))
    bit = 4
    while bit < n:
        total = sum(term.astype(jnp.float32) for term in terms)
        terms = (total[0::2], across(total[1::2].astype(jnp.bfloat16), bit))
        bit *= 2
    terms = [term.reshape(rows, 2 * width) for term in terms]
    attended, query_grad, key_grad, value_grad = place(plan, late, terms, filled, final=True)
    return (
        attended.reshape(rows, heads, width),
        query_grad.reshape(rows, heads, width),
        key_grad.reshape(rows, 1, width),
        value_grad.reshape(rows, 1, width),
    )


def solution(mesh):
    rows = P(("dp", "ctx"), "tp", None)
    return jax.shard_map(
        on_device,
        mesh=mesh,
        in_specs=(rows, rows, rows, rows, P("dp"), P("dp", None)),
        out_specs=(rows, rows, rows, rows),
        check_vma=False,
    )
```

```python
import functools
import jax
import jax.numpy as jnp
from jax import lax
from jax.experimental import pallas as pl
from jax.experimental.pallas import tpu as pltpu
from jax.sharding import PartitionSpec as P

MASKED = -1e30
LOG2_E = 1.4426950408889634
VMEM_LIMIT = 32 * 1024 * 1024


def dot(a, b, contract):
    return lax.dot_general(a, b, ((contract[0], contract[1]), ((), ())), preferred_element_type=jnp.float32)


def attend_block(first_row, ends, q, g, k, v, reach, heads, scale):
    cols = q.shape[0]
    key_rows = k.shape[0]
    token = lax.broadcasted_iota(jnp.int32, (1, cols), 1) // heads
    query_pos = first_row + token
    doc_start = jnp.zeros((1, cols), jnp.int32)
    for end in ends:
        doc_start = jnp.maximum(doc_start, jnp.where(end <= query_pos, end, 0))
    low = doc_start - (first_row - reach)
    raw = dot(k, q, ((1,), (1,)))
    index = lax.broadcasted_iota(jnp.int32, (key_rows, cols), 0)
    allowed = index >= low
    allowed_late = jnp.logical_and(allowed[reach:], index[reach:] - reach <= token)
    raw = jnp.concatenate(
        [jnp.where(allowed[:reach], raw[:reach], MASKED), jnp.where(allowed_late, raw[reach:], MASKED)], axis=0
    )
    row_max = jnp.max(raw, axis=0, keepdims=True)
    weights = jnp.exp2((raw - row_max) * (scale * LOG2_E))
    inverse = 1.0 / jnp.sum(weights, axis=0, keepdims=True)
    attended_t = (dot(v, weights.astype(jnp.bfloat16), ((0,), (0,))) * inverse).astype(jnp.bfloat16)
    attended = attended_t.T
    g_t = g.T.astype(jnp.float32)
    delta = jnp.sum(g_t * attended_t.astype(jnp.float32), axis=0, keepdims=True)
    probs = weights * inverse
    products = dot(v, g, ((1,), (1,)))
    slopes = (probs * (products - delta)).astype(jnp.bfloat16)
    value_part = dot(probs.astype(jnp.bfloat16), g, ((1,), (0,)))
    key_part = dot(slopes, q, ((1,), (0,))) * scale
    query_grad = (dot(k, slopes, ((0,), (0,))) * scale).astype(jnp.bfloat16).T
    return attended, query_grad, key_part, value_part


class Plan:
    def __init__(self, n, rows, heads, width, ndocs):
        self.n, self.rows, self.heads, self.width, self.ndocs = n, rows, heads, width, ndocs
        self.back = n // 2
        self.block = rows // n
        self.cols = self.block * heads
        self.reach = self.back * rows
        self.scale = width ** (-0.5)
        self.window_ranges = self.back + 1

    def pay_rows(self, x):
        return 2 * self.cols + (2 * (self.n // 4) * self.n * self.block if x == 1 else 0)

    def ends(self, meta):
        return [meta[1 + i] for i in range(self.ndocs)]

    def slot(self, meta, loader, owner):
        return meta[1 + self.ndocs + loader * self.n + owner]

    def cost(self, blocks):
        return pl.CostEstimate(
            flops=14 * blocks * self.cols * (self.reach + self.block) * self.width * 8,
            bytes_accessed=blocks * self.cols * self.width * 16,
            transcendentals=blocks * self.cols * (self.reach + self.block),
        )


def fill_window(plan, refs, k_win, v_win):
    rows = plan.rows
    k_win[pl.ds(plan.back * rows, rows), :] = refs[0][pl.ds(0, rows), :]
    v_win[pl.ds(plan.back * rows, rows), :] = refs[0][pl.ds(rows, rows), :]
    for i in range(1, plan.back + 1):
        to = pl.ds((plan.back - i) * rows, rows)
        k_win[to, :] = refs[2 * i - 1][...]
        v_win[to, :] = refs[2 * i][...]


def attend_at(plan, meta, loader, slot, q, g, k_win, v_win):
    start = (loader - meta[0]) * plan.rows + slot * plan.block
    keys_here = pl.ds(pl.multiple_of(start, plan.block), plan.reach + plan.block)
    out = attend_block(
        loader * plan.rows + slot * plan.block, plan.ends(meta), q, g, k_win[keys_here, :], v_win[keys_here, :],
        plan.reach, plan.heads, plan.scale,
    )
    return keys_here, out


def pack_kernel(plan, meta, q_ref, g_ref, k_ref, v_ref, *refs):
    blocks, (kv, sems, kv_sems) = refs[: plan.n], refs[plan.n :]
    own = meta[0]
    copies = []
    for apart, block in enumerate(blocks):
        slot = plan.slot(meta, own, own ^ apart)
        at = pl.ds(pl.multiple_of(slot * plan.cols, plan.cols), plan.cols)
        copies.append(pltpu.make_async_copy(q_ref.at[at, :], block.at[0], sems.at[apart, 0]))
        copies.append(pltpu.make_async_copy(g_ref.at[at, :], block.at[1], sems.at[apart, 1]))
    for i, ref in enumerate((k_ref, v_ref)):
        to = kv.at[pl.ds(i * plan.rows, plan.rows), :]
        copies.append(pltpu.make_async_copy(ref, to, kv_sems.at[i]))
    for copy in copies:
        copy.start()
    for copy in copies:
        copy.wait()


def first_kernel(plan, apart, meta, qg, *refs):
    kv_refs, (pay_ref, grad_ref, k_win, v_win) = refs[:-4], refs[-4:]
    own = meta[0]
    slot = plan.slot(meta, own, own ^ apart)
    fill_window(plan, kv_refs, k_win, v_win)
    _, (attended, query_grad, key_part, value_part) = attend_at(
        plan, meta, own, slot, qg[0], qg[1], k_win, v_win
    )
    pay_ref[pl.ds(0, plan.cols), :] = attended
    pay_ref[pl.ds(plan.cols, plan.cols), :] = query_grad
    grad_ref[:, : plan.width] = key_part
    grad_ref[:, plan.width :] = value_part


def last_kernel(plan, first, items, meta, *refs):
    n, width, rows, block = plan.n, plan.width, plan.rows, plan.block
    qg_refs, refs = refs[: len(items)], refs[len(items) :]
    first_grad, refs = refs[0], refs[1:]
    kv_refs, refs = refs[: -(len(items) + 7)], refs[-(len(items) + 7) :]
    pay_refs, grad_refs, (k_win, v_win, acc) = refs[: len(items)], refs[len(items) : -3], refs[-3:]
    step = pl.program_id(0)
    own = meta[0]

    @pl.when(step == 0)
    def _():
        fill_window(plan, kv_refs, k_win, v_win)
        acc[...] = jnp.zeros_like(acc)
        slot = plan.slot(meta, own, own ^ first)
        keys_here = pl.ds(pl.multiple_of(slot * block, block), plan.reach + block)
        acc[keys_here, :] = first_grad[...]

    for i, item in enumerate(items):

        @pl.when(step == i)
        def _():
            slot = plan.slot(meta, own, own ^ item)
            qg = qg_refs[i]
            keys_here, (attended, query_grad, key_part, value_part) = attend_at(
                plan, meta, own, slot, qg[0], qg[1], k_win, v_win
            )
            acc[keys_here, :width] = acc[keys_here, :width] + key_part
            acc[keys_here, width:] = acc[keys_here, width:] + value_part
            pay_refs[i][pl.ds(0, plan.cols), :] = attended
            pay_refs[i][pl.ds(plan.cols, plan.cols), :] = query_grad

    @pl.when(step == len(items) - 1)
    def _():
        near_ref = pay_refs[items.index(1)]

        def of_range(key_range, carry):
            at = lax.rem(key_range - own + plan.back + n, n) * rows
            for apart in range(n):
                slot = plan.slot(meta, key_range, own ^ apart)
                part = acc[pl.ds(pl.multiple_of(at + slot * block, block), block), :]
                entry = apart // 4
                if apart % 2 == 0:
                    grad_refs[apart % 4 // 2][entry, key_range] = part
                elif apart % 4 == 1:
                    for half in range(2):
                        to = 2 * plan.cols + ((half * (n // 4) + entry) * n + key_range) * block
                        value = part[:, half * width : (half + 1) * width].astype(jnp.bfloat16)
                        near_ref[pl.ds(pl.multiple_of(to, block), block), :] = value
                else:

                    @pl.when(key_range < n // 2)
                    def _():
                        grad_refs[2][entry, key_range] = part.astype(jnp.bfloat16)

                    @pl.when(key_range >= n // 2)
                    def _():
                        grad_refs[3][entry, key_range - n // 2] = part.astype(jnp.bfloat16)

            return carry

        lax.fori_loop(0, n, of_range, 0)


def spec_of(space):
    return pl.BlockSpec(memory_space=space)


def kernel_call(body, name, operands, spaces, out_shape, scratch, **more):
    return pl.pallas_call(
        body,
        out_shape=out_shape,
        in_specs=[spec_of(space) for space in spaces],
        compiler_params=pltpu.CompilerParams(vmem_limit_bytes=VMEM_LIMIT),
        scratch_shapes=scratch,
        name=name,
        **more,
    )(*operands)


def pack(plan, meta, *operands):
    out_shape = [jax.ShapeDtypeStruct((2, plan.cols, plan.width), jnp.bfloat16)] * plan.n
    out_shape.append(jax.ShapeDtypeStruct((2 * plan.rows, plan.width), jnp.bfloat16))
    operands = [pltpu.with_memory_space_constraint(x, pltpu.HBM) for x in operands]
    return kernel_call(
        functools.partial(pack_kernel, plan), "pack", (meta, *operands), [pltpu.SMEM] + [pl.ANY] * 4, out_shape,
        [pltpu.SemaphoreType.DMA((plan.n, 2)), pltpu.SemaphoreType.DMA((2,))],
        out_specs=[spec_of(pltpu.VMEM)] * len(out_shape),
    )


def attend_first(plan, apart, meta, qg, kv_list):
    window = pltpu.VMEM((plan.window_ranges * plan.rows, plan.width), jnp.bfloat16)
    out_shape = [
        jax.ShapeDtypeStruct((plan.pay_rows(apart), plan.width), jnp.bfloat16),
        jax.ShapeDtypeStruct((plan.reach + plan.block, 2 * plan.width), jnp.float32),
    ]
    operands = (meta, qg, *kv_list)
    return kernel_call(
        functools.partial(first_kernel, plan, apart), "attend_first", operands,
        [pltpu.SMEM] + [pltpu.VMEM] * (len(operands) - 1), out_shape, [window, window],
        out_specs=[spec_of(pltpu.VMEM)] * 2, cost_estimate=plan.cost(1),
    )


def attend_last(plan, first, items, meta, qg_list, first_grad, kv_list):
    n = plan.n
    window = pltpu.VMEM((plan.window_ranges * plan.rows, plan.width), jnp.bfloat16)
    keep = jax.ShapeDtypeStruct((n // 4, n, plan.block, 2 * plan.width), jnp.float32)
    send = jax.ShapeDtypeStruct((n // 4, n // 2, plan.block, 2 * plan.width), jnp.bfloat16)
    out_shape = [jax.ShapeDtypeStruct((plan.pay_rows(x), plan.width), jnp.bfloat16) for x in items]
    out_shape += [keep, keep, send, send]
    operands = (meta, *qg_list, first_grad, *kv_list)
    return kernel_call(
        functools.partial(last_kernel, plan, first, items), "attend_last", operands,
        [pltpu.SMEM] + [pltpu.VMEM] * (len(operands) - 1), out_shape,
        [window, window, pltpu.VMEM((n * plan.rows, 2 * plan.width), jnp.float32)],
        out_specs=[spec_of(pltpu.VMEM)] * len(out_shape), cost_estimate=plan.cost(len(items)), grid=(len(items),),
    )


def place_kernel(plan, items, final, *refs):
    n, cols, width, rows = plan.n, plan.cols, plan.width, plan.rows
    own = lax.axis_index("ctx")
    pay_refs, refs = refs[: len(items)], refs[len(items) :]
    if final:
        grads, (_, _, attended, query_grad, key_grad, value_grad, sums, sems, sum_sems) = refs[:-9], refs[-9:]
    else:
        (pass_on, *arrived), (attended, query_grad, send, sems) = refs[:-4], refs[-4:]
    copies = []
    for i, item in enumerate(items):
        to = pl.ds(pl.multiple_of((own ^ item) * cols, cols), cols)
        for part, ref in enumerate((attended, query_grad)):
            source = pay_refs[i].at[pl.ds(part * cols, cols), :]
            copies.append(pltpu.make_async_copy(source, ref.at[to, :], sems.at[i, part]))
    for copy in copies:
        copy.start()
    if final:
        for i, ref in enumerate((key_grad, value_grad)):
            total = sum(grad[:, i * width : (i + 1) * width].astype(jnp.float32) for grad in grads)
            if n == 4:
                total = total + pay_refs[items.index(1)][pl.ds(2 * cols + i * rows, rows), :].astype(jnp.float32)
            sums[i] = total.astype(jnp.bfloat16)
            copies.append(pltpu.make_async_copy(sums.at[i], ref, sum_sems.at[i]))
            copies[-1].start()
    else:
        for half, ref in enumerate(arrived):
            ranges = pl.ds(half * (n // 2), n // 2)
            send[:, ranges] = (pass_on[:, ranges] + ref[...].astype(jnp.float32)).astype(jnp.bfloat16)
    for copy in copies:
        copy.wait()


def place(plan, payloads, grads, filled=()):
    items = tuple(payloads)
    final = len(filled) > 0
    out_shape = [jax.ShapeDtypeStruct((plan.rows * plan.heads, plan.width), jnp.bfloat16)] * 2
    scratch = [pltpu.SemaphoreType.DMA((len(items), 2))]
    if final:
        out_shape += [jax.ShapeDtypeStruct((plan.rows, plan.width), jnp.bfloat16)] * 2
        scratch = [pltpu.VMEM((2, plan.rows, plan.width), jnp.bfloat16), *scratch, pltpu.SemaphoreType.DMA((2,))]
    else:
        out_shape.append(jax.ShapeDtypeStruct(grads[0].shape, jnp.bfloat16))
    at = len(items) + len(grads)
    return kernel_call(
        functools.partial(place_kernel, plan, items, final), "place_last" if final else "place_first",
        (*payloads.values(), *grads, *filled),
        [pltpu.VMEM if x == 1 else pl.ANY for x in items] + [pltpu.VMEM] * len(grads) + [pl.ANY] * len(filled),
        out_shape, scratch,
        out_specs=[spec_of(pl.ANY)] * 2 + ([spec_of(pl.ANY)] * 2 if final else [spec_of(pltpu.VMEM)]),
        input_output_aliases={at: 0, at + 1: 1} if final else {},
        cost_estimate=plan.cost(len(items)),
    )


def on_device(query, keys, values, output_gradient, doc_lengths, block_owner):
    n = lax.axis_size("ctx")
    own = lax.axis_index("ctx")
    rows, heads, width = query.shape
    plan = Plan(n, rows, heads, width, doc_lengths.shape[0])

    def permuted(array, pairs):
        return lax.ppermute(array, "ctx", pairs)

    def across(array, bits):
        return permuted(array, [(i, i ^ bits) for i in range(n)])

    k = keys.reshape(rows, width)
    v = values.reshape(rows, width)
    kv_list = []
    for by in range(1, plan.back + 1):
        pairs = [(i, (i + by) % n) for i in range(n)]
        kv_list += [permuted(k, pairs), permuted(v, pairs)]

    owners = jnp.arange(n, dtype=jnp.int32)
    match = block_owner[:, None, :] == owners[None, :, None]
    table = jnp.sum(jnp.where(match, owners, 0), axis=2)
    meta = jnp.concatenate(
        [own.reshape(1).astype(jnp.int32), jnp.cumsum(doc_lengths).astype(jnp.int32), table.reshape(-1)]
    )

    q, g = (x.reshape(rows * heads, width) for x in (query, output_gradient))
    *blocks, kv = pack(plan, meta, q, g, k, v)
    kv_list = [kv, *kv_list]
    first = n // 2
    first_pay, first_grad = attend_first(plan, first, meta, blocks[first], kv_list)
    stay = {first: across(first_pay, first)}
    sent = [x for x in range(n - 1, 0, -1) if x != first]
    items = (*sent, 0)
    out = attend_last(plan, first, items, meta, [blocks[x] for x in items], first_grad, kv_list)
    late = {x: across(pay, x) for x, pay in zip(sent, out)}
    stay[0] = out[len(sent)]
    keep, pass_on, lower, upper = out[len(items) :]
    upper = permuted(upper, [(i, i ^ 1) for i in range(n // 2, n)])
    *filled, send = place(plan, stay, (pass_on, across(lower, 1), upper))
    terms = [keep, across(send, 2)]
    bit = 4
    while bit < n:
        total = sum(term.astype(jnp.float32) for term in terms)
        if bit == 4:
            near = late[1][2 * plan.cols :].reshape(2, n // 4, n, plan.block, width)
            total = total + jnp.concatenate([near[0], near[1]], axis=-1).astype(jnp.float32)
        terms = [total[0::2], across(total[1::2].astype(jnp.bfloat16), bit)]
        bit *= 2
    terms = [term.reshape(rows, 2 * width) for term in terms]
    attended, query_grad, key_grad, value_grad = place(plan, late, terms, filled)
    return (
        attended.reshape(rows, heads, width),
        query_grad.reshape(rows, heads, width),
        key_grad.reshape(rows, 1, width),
        value_grad.reshape(rows, 1, width),
    )


def solution(mesh):
    rows = P(("dp", "ctx"), "tp", None)
    return jax.shard_map(
        on_device,
        mesh=mesh,
        in_specs=(rows, rows, rows, rows, P("dp"), P("dp", None)),
        out_specs=(rows, rows, rows, rows),
        check_vma=False,
    )
```

```python
import functools
import jax
import jax.numpy as jnp
from jax import lax
from jax.experimental import pallas as pl
from jax.experimental.pallas import tpu as pltpu
from jax.sharding import PartitionSpec as P

MASKED = -1e30
LOG2_E = 1.4426950408889634
VMEM_LIMIT = 32 * 1024 * 1024


def dot(a, b, contract):
    return lax.dot_general(a, b, ((contract[0], contract[1]), ((), ())), preferred_element_type=jnp.float32)


def attend_block(first_row, ends, q, g, k, v, reach, heads, scale):
    cols = q.shape[0]
    key_rows = k.shape[0]
    token = lax.broadcasted_iota(jnp.int32, (1, cols), 1) // heads
    query_pos = first_row + token
    doc_start = jnp.zeros((1, cols), jnp.int32)
    for end in ends:
        doc_start = jnp.maximum(doc_start, jnp.where(end <= query_pos, end, 0))
    low = doc_start - (first_row - reach)
    raw = dot(k, q, ((1,), (1,)))
    index = lax.broadcasted_iota(jnp.int32, (key_rows, cols), 0)
    allowed = index >= low
    allowed_late = jnp.logical_and(allowed[reach:], index[reach:] - reach <= token)
    raw = jnp.concatenate(
        [jnp.where(allowed[:reach], raw[:reach], MASKED), jnp.where(allowed_late, raw[reach:], MASKED)], axis=0
    )
    row_max = jnp.max(raw, axis=0, keepdims=True)
    weights = jnp.exp2((raw - row_max) * (scale * LOG2_E))
    inverse = 1.0 / jnp.sum(weights, axis=0, keepdims=True)
    attended_t = (dot(v, weights.astype(jnp.bfloat16), ((0,), (0,))) * inverse).astype(jnp.bfloat16)
    attended = attended_t.T
    g_t = g.T.astype(jnp.float32)
    delta = jnp.sum(g_t * attended_t.astype(jnp.float32), axis=0, keepdims=True)
    probs = weights * inverse
    products = dot(v, g, ((1,), (1,)))
    slopes = (probs * (products - delta)).astype(jnp.bfloat16)
    value_part = dot(probs.astype(jnp.bfloat16), g, ((1,), (0,)))
    key_part = dot(slopes, q, ((1,), (0,))) * scale
    query_grad = (dot(k, slopes, ((0,), (0,))) * scale).astype(jnp.bfloat16).T
    return attended, query_grad, key_part, value_part


class Plan:
    def __init__(self, n, rows, heads, width, ndocs):
        self.n, self.rows, self.heads, self.width, self.ndocs = n, rows, heads, width, ndocs
        self.back = n // 2
        self.block = rows // n
        self.cols = self.block * heads
        self.reach = self.back * rows
        self.scale = width ** (-0.5)
        self.lower = self.back + 1
        self.window_ranges = self.back + 2

    def ends(self, meta):
        return [meta[1 + i] for i in range(self.ndocs)]

    def slot(self, meta, loader, owner):
        return meta[1 + self.ndocs + loader * self.n + owner]

    def cost(self, blocks):
        return pl.CostEstimate(
            flops=14 * blocks * self.cols * (self.reach + self.block) * self.width * 8,
            bytes_accessed=blocks * self.cols * self.width * 16,
            transcendentals=blocks * self.cols * (self.reach + self.block),
        )


def fill_window(plan, own, refs, k_win, v_win):
    rows = plan.rows
    k_win[pl.ds(0, rows), :] = jnp.zeros((rows, plan.width), k_win.dtype)
    v_win[pl.ds(0, rows), :] = jnp.zeros((rows, plan.width), v_win.dtype)
    k_win[pl.ds(plan.back * rows, rows), :] = refs[0][pl.ds(0, rows), :]
    v_win[pl.ds(plan.back * rows, rows), :] = refs[0][pl.ds(rows, rows), :]
    for i in range(1, plan.back + 1):
        place = plan.back - i if i < plan.back else jnp.where(own == plan.back - 1, plan.back + 1, 0)
        to = pl.ds(pl.multiple_of(place * rows, rows), rows)
        k_win[to, :] = refs[2 * i - 1][...]
        v_win[to, :] = refs[2 * i][...]


def attend_at(plan, meta, loader, slot, q, g, k_win, v_win):
    start = (loader - meta[0]) * plan.rows + slot * plan.block
    keys_here = pl.ds(pl.multiple_of(start, plan.block), plan.reach + plan.block)
    out = attend_block(
        loader * plan.rows + slot * plan.block, plan.ends(meta), q, g, k_win[keys_here, :], v_win[keys_here, :],
        plan.reach, plan.heads, plan.scale,
    )
    return keys_here, out


def early_kernel(plan, owners_ref, q_ref, g_ref, block, sems):
    own = lax.axis_index("ctx")
    owner, slot = own ^ (plan.n - 1), jnp.int32(0)
    for i in range(1, plan.n):
        slot = jnp.where(owners_ref[own, i] == owner, i, slot)
    at = pl.ds(pl.multiple_of(slot * plan.cols, plan.cols), plan.cols)
    copies = [pltpu.make_async_copy(ref.at[at, :], block.at[i], sems.at[i]) for i, ref in enumerate((q_ref, g_ref))]
    for copy in copies:
        copy.start()
    for copy in copies:
        copy.wait()


def pack_kernel(plan, ends_ref, owners_ref, q_ref, g_ref, k_ref, v_ref, *refs):
    n = plan.n
    blocks, (kv, meta, sems, kv_sems) = refs[: n - 1], refs[n - 1 :]
    own = lax.axis_index("ctx")
    copies = []
    for i, ref in enumerate((k_ref, v_ref)):
        to = kv.at[pl.ds(i * plan.rows, plan.rows), :]
        copies.append(pltpu.make_async_copy(ref, to, kv_sems.at[i]))
        copies[-1].start()

    def slots_of(loader):
        for slot in range(n):
            meta[1 + plan.ndocs + loader * n + owners_ref[loader, slot]] = slot

    slots_of(own)
    for apart in range(n - 2, -1, -1):
        slot = plan.slot(meta, own, own ^ apart)
        at = pl.ds(pl.multiple_of(slot * plan.cols, plan.cols), plan.cols)
        copies.append(pltpu.make_async_copy(q_ref.at[at, :], blocks[apart].at[0], sems.at[apart, 0]))
        copies.append(pltpu.make_async_copy(g_ref.at[at, :], blocks[apart].at[1], sems.at[apart, 1]))
        copies[-2].start()
        copies[-1].start()
    meta[0] = own
    end = jnp.int32(0)
    for i in range(plan.ndocs):
        end = end + ends_ref[i]
        meta[1 + i] = end
    for loader in range(n):
        slots_of(loader)
    for copy in copies:
        copy.wait()


def first_kernel(plan, apart, meta, qg, *refs):
    kv_refs, (pay_ref, grad_ref, k_win, v_win) = refs[:-4], refs[-4:]
    own = meta[0]
    slot = plan.slot(meta, own, own ^ apart)
    fill_window(plan, own, kv_refs, k_win, v_win)
    _, (attended, query_grad, key_part, value_part) = attend_at(
        plan, meta, own, slot, qg[0], qg[1], k_win, v_win
    )
    pay_ref[0] = attended
    pay_ref[1] = query_grad
    grad_ref[:, : plan.width] = key_part
    grad_ref[:, plan.width :] = value_part


def add_parts(plan, acc, keys_here, key_part, value_part):
    acc[keys_here, : plan.width] = acc[keys_here, : plan.width] + key_part
    acc[keys_here, plan.width :] = acc[keys_here, plan.width :] + value_part


def put_rows(plan, pay_ref, attended, query_grad):
    pay_ref[0] = attended
    pay_ref[1] = query_grad


def next_kernel(plan, first, items, meta, *refs):
    n = plan.n
    qg_refs, first_grad, refs = refs[: len(items)], refs[len(items)], refs[len(items) + 1 :]
    outs = len(items) + 3
    kv_refs, pay_refs, (acc, k_win, v_win) = refs[:-outs], refs[-outs:-3], refs[-3:]
    step = pl.program_id(0)
    own = meta[0]

    @pl.when(step == 0)
    def _():
        fill_window(plan, own, kv_refs, k_win, v_win)
        acc[...] = jnp.zeros_like(acc)
        slot = plan.slot(meta, own, own ^ first)
        start = pl.multiple_of(slot * plan.block, plan.block)
        acc[pl.ds(start, plan.reach + plan.block), :] = first_grad[...]

    for i, item in enumerate(items):
        here = step == i
        if item == n - 1:
            here = jnp.logical_and(here, own != plan.back)

        @pl.when(here)
        def _():
            slot = plan.slot(meta, own, own ^ item)
            keys_here, (attended, query_grad, *parts) = attend_at(
                plan, meta, own, slot, qg_refs[i][0], qg_refs[i][1], k_win, v_win
            )
            add_parts(plan, acc, keys_here, *parts)
            put_rows(plan, pay_refs[i], attended, query_grad)


def last_kernel(plan, meta, got_ref, acc_ref, *refs):
    n, block, rows = plan.n, plan.block, plan.rows
    kv_refs, (pay_ref, *grad_refs), (k_win, v_win, acc) = refs[:-8], refs[-8:-3], refs[-3:]
    own = meta[0]
    acc[...] = acc_ref[...]

    @pl.when(own == plan.back - 1)
    def _():
        fill_window(plan, own, kv_refs, k_win, v_win)
        keys_here, (attended, query_grad, *parts) = attend_at(
            plan, meta, own + 1, plan.slot(meta, own + 1, own), got_ref[0], got_ref[1], k_win, v_win
        )
        add_parts(plan, acc, keys_here, *parts)
        put_rows(plan, pay_ref, attended, query_grad)

    def put_part(key_range, entry, part):
        @pl.when(key_range < plan.lower)
        def _():
            grad_refs[2][entry, key_range] = part.astype(jnp.bfloat16)

        @pl.when(key_range >= plan.lower)
        def _():
            grad_refs[3][entry, key_range - plan.lower] = part.astype(jnp.bfloat16)

    def of_range(key_range, carry):
        at = lax.rem(key_range - own + plan.back + n, n) * rows
        for apart in range(n):
            slot = plan.slot(meta, key_range, own ^ apart)
            part = acc[pl.ds(pl.multiple_of(at + slot * block, block), block), :]
            if apart % 2 == 0:
                to = grad_refs[apart % 4 // 2]
                to[apart // 4, key_range] = part
            else:
                put_part(key_range, apart // 2, part)
        return carry

    lax.fori_loop(0, n, of_range, 0)


def spec_of(space):
    return pl.BlockSpec(memory_space=space)


def kernel_call(body, name, operands, spaces, out_shape, scratch, **more):
    return pl.pallas_call(
        body,
        out_shape=out_shape,
        in_specs=[spec_of(space) for space in spaces],
        compiler_params=pltpu.CompilerParams(vmem_limit_bytes=VMEM_LIMIT),
        scratch_shapes=scratch,
        name=name,
        **more,
    )(*operands)


def in_hbm(*operands):
    return [pltpu.with_memory_space_constraint(x, pltpu.HBM) for x in operands]


def pack_early(plan, block_owner, q, g):
    return kernel_call(
        functools.partial(early_kernel, plan), "pack_early", (block_owner, *in_hbm(q, g)),
        [pltpu.SMEM] + [pl.ANY] * 2, jax.ShapeDtypeStruct((2, plan.cols, plan.width), jnp.bfloat16),
        [pltpu.SemaphoreType.DMA((2,))], out_specs=spec_of(pltpu.VMEM),
    )


def pack(plan, doc_lengths, block_owner, *operands):
    n = plan.n
    out_shape = [jax.ShapeDtypeStruct((2, plan.cols, plan.width), jnp.bfloat16)] * (n - 1)
    out_shape.append(jax.ShapeDtypeStruct((2 * plan.rows, plan.width), jnp.bfloat16))
    out_shape.append(jax.ShapeDtypeStruct((1 + plan.ndocs + n * n,), jnp.int32))
    return kernel_call(
        functools.partial(pack_kernel, plan), "pack", (doc_lengths, block_owner, *in_hbm(*operands)),
        [pltpu.SMEM] * 2 + [pl.ANY] * 4, out_shape,
        [pltpu.SemaphoreType.DMA((n, 2)), pltpu.SemaphoreType.DMA((2,))],
        out_specs=[spec_of(pltpu.VMEM)] * n + [spec_of(pltpu.SMEM)],
    )


def attend_first(plan, apart, meta, qg, kv_list):
    window = pltpu.VMEM((plan.window_ranges * plan.rows, plan.width), jnp.bfloat16)
    out_shape = [
        jax.ShapeDtypeStruct((2, plan.cols, plan.width), jnp.bfloat16),
        jax.ShapeDtypeStruct((plan.reach + plan.block, 2 * plan.width), jnp.float32),
    ]
    operands = (meta, qg, *kv_list)
    return kernel_call(
        functools.partial(first_kernel, plan, apart), "attend_first", operands,
        [pltpu.SMEM] + [pltpu.VMEM] * (len(operands) - 1), out_shape, [window, window],
        out_specs=[spec_of(pltpu.VMEM)] * 2, cost_estimate=plan.cost(1),
    )


def attend_next(plan, first, items, meta, qg_list, first_grad, kv_list):
    window = pltpu.VMEM((plan.window_ranges * plan.rows, plan.width), jnp.bfloat16)
    out_shape = [jax.ShapeDtypeStruct((2, plan.cols, plan.width), jnp.bfloat16)] * len(items)
    out_shape.append(jax.ShapeDtypeStruct((plan.n * plan.rows, 2 * plan.width), jnp.float32))
    operands = (meta, *qg_list, first_grad, *kv_list)
    return kernel_call(
        functools.partial(next_kernel, plan, first, items), "attend_next", operands,
        [pltpu.SMEM] + [pltpu.VMEM] * (len(operands) - 1), out_shape, [window, window],
        out_specs=[spec_of(pltpu.VMEM)] * len(out_shape), cost_estimate=plan.cost(len(items)), grid=(len(items),),
    )


def attend_last(plan, meta, got, sums, kv_list):
    n = plan.n
    window = pltpu.VMEM((plan.window_ranges * plan.rows, plan.width), jnp.bfloat16)
    part = (plan.block, 2 * plan.width)
    keep = jax.ShapeDtypeStruct((n // 4, n, *part), jnp.float32)
    lower = jax.ShapeDtypeStruct((n // 2, plan.lower, *part), jnp.bfloat16)
    upper = jax.ShapeDtypeStruct((n // 2, n - plan.lower, *part), jnp.bfloat16)
    out_shape = [jax.ShapeDtypeStruct((2, plan.cols, plan.width), jnp.bfloat16), keep, keep, lower, upper]
    operands = (meta, got, sums, *kv_list)
    return kernel_call(
        functools.partial(last_kernel, plan), "attend_last", operands,
        [pltpu.SMEM] + [pltpu.VMEM] * (len(operands) - 1), out_shape,
        [window, window, pltpu.VMEM(sums.shape, jnp.float32)],
        out_specs=[spec_of(pltpu.VMEM)] * len(out_shape), cost_estimate=plan.cost(1),
    )


def place_kernel(plan, items, final, *refs):
    n, cols, width = plan.n, plan.cols, plan.width
    own = lax.axis_index("ctx")
    pay_refs, refs = refs[: len(items)], refs[len(items) :]
    if final:
        grads, (_, _, attended, query_grad, key_grad, value_grad, sums, sems, sum_sems) = refs[:-9], refs[-9:]
    else:
        grads, (attended, query_grad, send, kept, sems) = refs[:-5], refs[-5:]
    copies = []
    for i, item in enumerate(items):
        to = pl.ds(pl.multiple_of((own ^ (n - 1 if item == "got" else item)) * cols, cols), cols)
        pair = [
            pltpu.make_async_copy(pay_refs[i].at[0], attended.at[to, :], sems.at[i, 0]),
            pltpu.make_async_copy(pay_refs[i].at[1], query_grad.at[to, :], sems.at[i, 1]),
        ]
        if item in ("got", n - 1):
            copies += [(copy, (own == plan.back - 1) == (item == "got")) for copy in pair]
        else:
            copies += [(copy, None) for copy in pair]

    def each(act):
        for copy, here in copies:
            if here is None:
                act(copy)
            else:
                pl.when(here)(functools.partial(act, copy))

    each(lambda copy: copy.start())
    if final:
        total = sum(grad[...].astype(jnp.float32) for grad in grads).astype(jnp.bfloat16)
        sums[0] = total[:, :width]
        sums[1] = total[:, width:]
        for i, ref in enumerate((key_grad, value_grad)):
            copies.append((pltpu.make_async_copy(sums.at[i], ref, sum_sems.at[i]), None))
            copies[-1][0].start()
    else:
        pass_on, keep, *arrived = grads
        for entry in range(n // 2):
            for half, ref in enumerate(arrived):
                ranges = pl.ds(plan.lower, n - plan.lower) if half else pl.ds(0, plan.lower)
                total = (keep, pass_on)[entry % 2][entry // 2, ranges] + ref[entry].astype(jnp.float32)
                if entry % 2:
                    send[entry // 2, ranges] = total.astype(jnp.bfloat16)
                else:
                    kept[entry // 2, ranges] = total
    each(lambda copy: copy.wait())


def place(plan, payloads, grads, filled=()):
    items = tuple(payloads)
    big = jax.ShapeDtypeStruct((plan.rows * plan.heads, plan.width), jnp.bfloat16)
    small = jax.ShapeDtypeStruct((plan.rows, plan.width), jnp.bfloat16)
    final = len(filled) > 0
    at = len(items) + len(grads)
    scratch = [pltpu.SemaphoreType.DMA((len(items), 2))]
    if final:
        scratch = [pltpu.VMEM((2, plan.rows, plan.width), jnp.bfloat16), *scratch, pltpu.SemaphoreType.DMA((2,))]
    return kernel_call(
        functools.partial(place_kernel, plan, items, final), "place_last" if final else "place_first",
        (*payloads.values(), *grads, *filled),
        [pl.ANY] * len(items) + [pltpu.VMEM] * len(grads) + [pl.ANY] * len(filled),
        [big, big] + ([small, small] if final else [jax.ShapeDtypeStruct(grads[0].shape, t) for t in (jnp.bfloat16, jnp.float32)]), scratch,
        out_specs=[spec_of(pl.ANY)] * 2 + [spec_of(pl.ANY if final else pltpu.VMEM)] * 2,
        input_output_aliases={at: 0, at + 1: 1} if final else {},
        cost_estimate=plan.cost(len(items)),
    )


def on_device(query, keys, values, output_gradient, doc_lengths, block_owner):
    n = lax.axis_size("ctx")
    own = lax.axis_index("ctx")
    rows, heads, width = query.shape
    plan = Plan(n, rows, heads, width, doc_lengths.shape[0])

    def permuted(array, pairs):
        return lax.ppermute(array, "ctx", pairs)

    def across(array, bits):
        return permuted(array, [(i, i ^ bits) for i in range(n)])

    k = keys.reshape(rows, width)
    v = values.reshape(rows, width)
    kv_list = []
    for by in range(1, plan.back + 1):
        pairs = [(i, (i + by) % n) for i in range(n)]
        if by == plan.back:
            pairs = [(i, i + by if i < by else (i - by - 1) % by) for i in range(n)]
        kv_list += [permuted(k, pairs), permuted(v, pairs)]

    q, g = (x.reshape(rows * heads, width) for x in (query, output_gradient))
    last_block = pack_early(plan, block_owner, q, g)
    got = permuted(last_block, [(plan.back, plan.back - 1)])
    *blocks, kv, meta = pack(plan, doc_lengths, block_owner, q, g, k, v)
    blocks.append(last_block)
    kv_list = [kv, *kv_list]
    first = n // 2
    first_pay, first_grad = attend_first(plan, first, meta, blocks[first], kv_list)
    stay = {first: across(first_pay, first)}
    items = (*[x for x in range(1, n) if x != first], 0)
    *pays, sums = attend_next(plan, first, items, meta, [blocks[x] for x in items], first_grad, kv_list)
    stay["got"], *out = attend_last(plan, meta, got, sums, kv_list)
    stay[0] = pays[-1]
    late = {x: across(pay, x) for x, pay in zip(items[:-2], pays[:-2])}
    late[n - 1] = permuted(pays[-2], [(i, i ^ (n - 1)) for i in range(n) if i != plan.back])
    keep, pass_on, lower, upper = out
    upper = permuted(upper, [(i, i ^ 1) for i in range(plan.back, n)])
    attended, query_grad, send, keep = place(plan, stay, (pass_on, keep, across(lower, 1), upper))
    terms = (keep, across(send, 2))
    bit = 4
    while bit < n:
        total = sum(term.astype(jnp.float32) for term in terms)
        terms = (total[0::2], across(total[1::2].astype(jnp.bfloat16), bit))
        bit *= 2
    terms = [term.reshape(rows, 2 * width) for term in terms]
    attended, query_grad, key_grad, value_grad = place(plan, late, terms, (attended, query_grad))
    return (
        attended.reshape(rows, heads, width),
        query_grad.reshape(rows, heads, width),
        key_grad.reshape(rows, 1, width),
        value_grad.reshape(rows, 1, width),
    )


def solution(mesh):
    rows = P(("dp", "ctx"), "tp", None)
    return jax.shard_map(
        on_device,
        mesh=mesh,
        in_specs=(rows, rows, rows, rows, P("dp"), P("dp", None)),
        out_specs=(rows, rows, rows, rows),
        check_vma=False,
    )
```

```python
import functools
import jax
import jax.numpy as jnp
from jax import lax
from jax.experimental import pallas as pl
from jax.experimental.pallas import tpu as pltpu
from jax.sharding import PartitionSpec as P

MASKED = -1e30
LOG2_E = 1.4426950408889634
VMEM_LIMIT = 32 * 1024 * 1024


def dot(a, b, contract):
    return lax.dot_general(a, b, ((contract[0], contract[1]), ((), ())), preferred_element_type=jnp.float32)


def attend_block(first_row, ends, q, g, k, v, reach, heads, scale):
    cols = q.shape[0]
    key_rows = k.shape[0]
    token = lax.broadcasted_iota(jnp.int32, (1, cols), 1) // heads
    query_pos = first_row + token
    doc_start = jnp.zeros((1, cols), jnp.int32)
    for end in ends:
        doc_start = jnp.maximum(doc_start, jnp.where(end <= query_pos, end, 0))
    low = doc_start - (first_row - reach)
    raw = dot(k, q, ((1,), (1,)))
    index = lax.broadcasted_iota(jnp.int32, (key_rows, cols), 0)
    allowed = index >= low
    allowed_late = jnp.logical_and(allowed[reach:], index[reach:] - reach <= token)
    raw = jnp.concatenate(
        [jnp.where(allowed[:reach], raw[:reach], MASKED), jnp.where(allowed_late, raw[reach:], MASKED)], axis=0
    )
    row_max = jnp.max(raw, axis=0, keepdims=True)
    weights = jnp.exp2((raw - row_max) * (scale * LOG2_E))
    inverse = 1.0 / jnp.sum(weights, axis=0, keepdims=True)
    attended_t = (dot(v, weights.astype(jnp.bfloat16), ((0,), (0,))) * inverse).astype(jnp.bfloat16)
    attended = attended_t.T
    g_t = g.T.astype(jnp.float32)
    delta = jnp.sum(g_t * attended_t.astype(jnp.float32), axis=0, keepdims=True)
    probs = weights * inverse
    products = dot(v, g, ((1,), (1,)))
    slopes = (probs * (products - delta)).astype(jnp.bfloat16)
    value_part = dot(probs.astype(jnp.bfloat16), g, ((1,), (0,)))
    key_part = dot(slopes, q, ((1,), (0,))) * scale
    query_grad = (dot(k, slopes, ((0,), (0,))) * scale).astype(jnp.bfloat16).T
    return attended, query_grad, key_part, value_part


class Plan:
    def __init__(self, n, rows, heads, width, ndocs):
        self.n, self.rows, self.heads, self.width, self.ndocs = n, rows, heads, width, ndocs
        self.back = n // 2
        self.block = rows // n
        self.cols = self.block * heads
        self.reach = self.back * rows
        self.scale = width ** (-0.5)
        self.window_ranges = self.back + 1

    def ends(self, meta):
        return [meta[1 + i] for i in range(self.ndocs)]

    def slot(self, meta, loader, owner):
        return meta[1 + self.ndocs + loader * self.n + owner]

    def cost(self, blocks):
        return pl.CostEstimate(
            flops=14 * blocks * self.cols * (self.reach + self.block) * self.width * 8,
            bytes_accessed=blocks * self.cols * self.width * 16,
            transcendentals=blocks * self.cols * (self.reach + self.block),
        )


def fill_window(plan, refs, k_win, v_win):
    rows = plan.rows
    k_win[pl.ds(plan.back * rows, rows), :] = refs[0][pl.ds(0, rows), :]
    v_win[pl.ds(plan.back * rows, rows), :] = refs[0][pl.ds(rows, rows), :]
    for i in range(1, plan.back + 1):
        to = pl.ds((plan.back - i) * rows, rows)
        k_win[to, :] = refs[2 * i - 1][...]
        v_win[to, :] = refs[2 * i][...]


def attend_at(plan, meta, loader, slot, q, g, k_win, v_win):
    start = (loader - meta[0]) * plan.rows + slot * plan.block
    keys_here = pl.ds(pl.multiple_of(start, plan.block), plan.reach + plan.block)
    out = attend_block(
        loader * plan.rows + slot * plan.block, plan.ends(meta), q, g, k_win[keys_here, :], v_win[keys_here, :],
        plan.reach, plan.heads, plan.scale,
    )
    return keys_here, out


def pack_kernel(plan, meta, q_ref, g_ref, k_ref, v_ref, *refs):
    blocks, (kv, sems, kv_sems) = refs[: plan.n], refs[plan.n :]
    own = meta[0]
    copies = []
    for apart, block in enumerate(blocks):
        slot = plan.slot(meta, own, own ^ apart)
        at = pl.ds(pl.multiple_of(slot * plan.cols, plan.cols), plan.cols)
        copies.append(pltpu.make_async_copy(q_ref.at[at, :], block.at[0], sems.at[apart, 0]))
        copies.append(pltpu.make_async_copy(g_ref.at[at, :], block.at[1], sems.at[apart, 1]))
    for i, ref in enumerate((k_ref, v_ref)):
        to = kv.at[pl.ds(i * plan.rows, plan.rows), :]
        copies.append(pltpu.make_async_copy(ref, to, kv_sems.at[i]))
    for copy in copies:
        copy.start()
    for copy in copies:
        copy.wait()


def first_kernel(plan, entries, meta, *refs):
    count = len(entries)
    qg_refs, kv_refs = refs[:count], refs[count : -2 * count - 2]
    pay_refs, grad_refs, (k_win, v_win) = refs[-2 * count - 2 : -count - 2], refs[-count - 2 : -2], refs[-2:]
    own = meta[0]
    fill_window(plan, kv_refs, k_win, v_win)
    for apart, qg, pay_ref, grad_ref in zip(entries, qg_refs, pay_refs, grad_refs):
        slot = plan.slot(meta, own, own ^ apart)
        _, (attended, query_grad, key_part, value_part) = attend_at(
            plan, meta, own, slot, qg[0], qg[1], k_win, v_win
        )
        pay_ref[0] = attended
        pay_ref[1] = query_grad
        grad_ref[:, : plan.width] = key_part
        grad_ref[:, plan.width :] = value_part


def last_kernel(plan, done, items, meta, *refs):
    n, width, rows, block = plan.n, plan.width, plan.rows, plan.block
    qg_refs, refs = refs[: len(items)], refs[len(items) :]
    done_refs, refs = refs[: len(done)], refs[len(done) :]
    kv_refs, refs = refs[: -(len(items) + 8)], refs[-(len(items) + 8) :]
    pay_refs, grad_refs, (k_win, v_win, acc) = refs[: len(items)], refs[len(items) : -3], refs[-3:]
    step = pl.program_id(0)
    own = meta[0]

    @pl.when(step == 0)
    def _():
        fill_window(plan, kv_refs, k_win, v_win)
        acc[...] = jnp.zeros_like(acc)
        for x, grad_ref in zip(done, done_refs):
            slot = plan.slot(meta, own, own ^ x)
            keys_here = pl.ds(pl.multiple_of(slot * block, block), plan.reach + block)
            acc[keys_here, :] = acc[keys_here, :] + grad_ref[...]

    for i, item in enumerate(items):

        @pl.when(step == i)
        def _():
            slot = plan.slot(meta, own, own ^ item)
            qg = qg_refs[i]
            keys_here, (attended, query_grad, key_part, value_part) = attend_at(
                plan, meta, own, slot, qg[0], qg[1], k_win, v_win
            )
            acc[keys_here, :width] = acc[keys_here, :width] + key_part
            acc[keys_here, width:] = acc[keys_here, width:] + value_part
            pay_refs[i][0] = attended
            pay_refs[i][1] = query_grad

    @pl.when(step == len(items) - 1)
    def _():
        def of_range(key_range, carry):
            at = lax.rem(key_range - own + plan.back + n, n) * rows
            for apart in range(n):
                slot = plan.slot(meta, key_range, own ^ apart)
                part = acc[pl.ds(pl.multiple_of(at + slot * block, block), block), :]
                entry = apart // 4
                if apart % 4 == 3:

                    @pl.when(key_range < n // 2)
                    def _():
                        grad_refs[2][entry, key_range] = part.astype(jnp.bfloat16)

                    @pl.when(key_range >= n // 2)
                    def _():
                        grad_refs[3][entry, key_range - n // 2] = part.astype(jnp.bfloat16)
                else:
                    to = grad_refs[(0, 4, 1)[apart % 4]]
                    to[entry, key_range] = part.astype(to.dtype)
            return carry

        lax.fori_loop(0, n, of_range, 0)


def spec_of(space):
    return pl.BlockSpec(memory_space=space)


def kernel_call(body, name, operands, spaces, out_shape, scratch, **more):
    return pl.pallas_call(
        body,
        out_shape=out_shape,
        in_specs=[spec_of(space) for space in spaces],
        compiler_params=pltpu.CompilerParams(vmem_limit_bytes=VMEM_LIMIT),
        scratch_shapes=scratch,
        name=name,
        **more,
    )(*operands)


def pack(plan, meta, *operands):
    out_shape = [jax.ShapeDtypeStruct((2, plan.cols, plan.width), jnp.bfloat16)] * plan.n
    out_shape.append(jax.ShapeDtypeStruct((2 * plan.rows, plan.width), jnp.bfloat16))
    operands = [pltpu.with_memory_space_constraint(x, pltpu.HBM) for x in operands]
    return kernel_call(
        functools.partial(pack_kernel, plan), "pack", (meta, *operands), [pltpu.SMEM] + [pl.ANY] * 4, out_shape,
        [pltpu.SemaphoreType.DMA((plan.n, 2)), pltpu.SemaphoreType.DMA((2,))],
        out_specs=[spec_of(pltpu.VMEM)] * len(out_shape),
    )


def attend_first(plan, entries, meta, qg_list, kv_list):
    window = pltpu.VMEM((plan.window_ranges * plan.rows, plan.width), jnp.bfloat16)
    rows = jax.ShapeDtypeStruct((2, plan.cols, plan.width), jnp.bfloat16)
    grad = jax.ShapeDtypeStruct((plan.reach + plan.block, 2 * plan.width), jnp.float32)
    out_shape = [rows] * len(entries) + [grad] * len(entries)
    operands = (meta, *qg_list, *kv_list)
    return kernel_call(
        functools.partial(first_kernel, plan, entries), "attend_first", operands,
        [pltpu.SMEM] + [pltpu.VMEM] * (len(operands) - 1), out_shape, [window, window],
        out_specs=[spec_of(pltpu.VMEM)] * len(out_shape), cost_estimate=plan.cost(len(entries)),
    )


def attend_last(plan, done, items, meta, qg_list, done_grads, kv_list):
    n = plan.n
    window = pltpu.VMEM((plan.window_ranges * plan.rows, plan.width), jnp.bfloat16)
    keep = jax.ShapeDtypeStruct((n // 4, n, plan.block, 2 * plan.width), jnp.float32)
    send = jax.ShapeDtypeStruct((n // 4, n // 2, plan.block, 2 * plan.width), jnp.bfloat16)
    near = jax.ShapeDtypeStruct(keep.shape, jnp.bfloat16)
    out_shape = [jax.ShapeDtypeStruct((2, plan.cols, plan.width), jnp.bfloat16)] * len(items)
    out_shape += [keep, keep, send, send, near]
    operands = (meta, *qg_list, *done_grads, *kv_list)
    return kernel_call(
        functools.partial(last_kernel, plan, done, items), "attend_last", operands,
        [pltpu.SMEM] + [pltpu.VMEM] * (len(operands) - 1), out_shape,
        [window, window, pltpu.VMEM((n * plan.rows, 2 * plan.width), jnp.float32)],
        out_specs=[spec_of(pltpu.VMEM)] * len(out_shape), cost_estimate=plan.cost(len(items)), grid=(len(items),),
    )


def place_kernel(plan, items, final, *refs):
    n, cols, width = plan.n, plan.cols, plan.width
    own = lax.axis_index("ctx")
    pay_refs, refs = refs[: len(items)], refs[len(items) :]
    if final:
        grads, (_, _, attended, query_grad, key_grad, value_grad, sums, sems, sum_sems) = refs[:-9], refs[-9:]
    else:
        (pass_on, to_near, *arrived), (attended, query_grad, send, near, sems) = refs[:-5], refs[-5:]
    copies = []
    for i, item in enumerate(items):
        to = pl.ds(pl.multiple_of((own ^ item) * cols, cols), cols)
        copies.append(pltpu.make_async_copy(pay_refs[i].at[0], attended.at[to, :], sems.at[i, 0]))
        copies.append(pltpu.make_async_copy(pay_refs[i].at[1], query_grad.at[to, :], sems.at[i, 1]))
    for copy in copies:
        copy.start()
    if final:
        total = sum(grad[...].astype(jnp.float32) for grad in grads).astype(jnp.bfloat16)
        sums[0] = total[:, :width]
        sums[1] = total[:, width:]
        for i, ref in enumerate((key_grad, value_grad)):
            copies.append(pltpu.make_async_copy(sums.at[i], ref, sum_sems.at[i]))
            copies[-1].start()
    else:
        near[...] = to_near[...]
        for half, ref in enumerate(arrived):
            ranges = pl.ds(half * (n // 2), n // 2)
            send[:, ranges] = (pass_on[:, ranges] + ref[...].astype(jnp.float32)).astype(jnp.bfloat16)
    for copy in copies:
        copy.wait()


def place(plan, payloads, grads, filled=(), final=False):
    items = tuple(payloads)
    out_shape = [jax.ShapeDtypeStruct((plan.rows * plan.heads, plan.width), jnp.bfloat16)] * 2
    out_specs = [spec_of(pl.ANY)] * 2
    scratch = [pltpu.SemaphoreType.DMA((len(items), 2))]
    if final:
        out_shape += [jax.ShapeDtypeStruct((plan.rows, plan.width), jnp.bfloat16)] * 2
        out_specs += [spec_of(pl.ANY)] * 2
        scratch = [pltpu.VMEM((2, plan.rows, plan.width), jnp.bfloat16), *scratch, pltpu.SemaphoreType.DMA((2,))]
    else:
        out_shape += [jax.ShapeDtypeStruct(grads[0].shape, jnp.bfloat16)] * 2
        out_specs += [spec_of(pltpu.VMEM)] * 2
    at = len(items) + len(grads)
    return kernel_call(
        functools.partial(place_kernel, plan, items, final), "place_" + "_".join(map(str, items)),
        (*payloads.values(), *grads, *filled),
        [pl.ANY] * len(items) + [pltpu.VMEM] * len(grads) + [pl.ANY] * len(filled),
        out_shape, scratch, out_specs=out_specs, input_output_aliases={at: 0, at + 1: 1} if filled else {},
        cost_estimate=plan.cost(len(items)),
    )


def on_device(query, keys, values, output_gradient, doc_lengths, block_owner):
    n = lax.axis_size("ctx")
    own = lax.axis_index("ctx")
    rows, heads, width = query.shape
    plan = Plan(n, rows, heads, width, doc_lengths.shape[0])

    def permuted(array, pairs):
        return lax.ppermute(array, "ctx", pairs)

    def across(array, bits):
        return permuted(array, [(i, i ^ bits) for i in range(n)])

    k = keys.reshape(rows, width)
    v = values.reshape(rows, width)
    kv_list = []
    for by in range(1, plan.back + 1):
        pairs = [(i, (i + by) % n) for i in range(n)]
        kv_list += [permuted(k, pairs), permuted(v, pairs)]

    owners = jnp.arange(n, dtype=jnp.int32)
    match = block_owner[:, None, :] == owners[None, :, None]
    table = jnp.sum(jnp.where(match, owners, 0), axis=2)
    meta = jnp.concatenate(
        [own.reshape(1).astype(jnp.int32), jnp.cumsum(doc_lengths).astype(jnp.int32), table.reshape(-1)]
    )

    q, g = (x.reshape(rows * heads, width) for x in (query, output_gradient))
    *blocks, kv = pack(plan, meta, q, g, k, v)
    kv_list = [kv, *kv_list]
    first = (n // 2, 1)
    first_pay, near_pay, *first_grads = attend_first(plan, first, meta, [blocks[x] for x in first], kv_list)
    stay = {x: across(pay, x) for x, pay in zip(first, (first_pay, near_pay))}
    sent = [x for x in range(1, n) if x not in first]
    items = (*sent, 0)
    out = attend_last(plan, first, items, meta, [blocks[x] for x in items], first_grads, kv_list)
    late = {x: across(pay, x) for x, pay in zip(sent, out)}
    stay[0] = out[len(sent)]
    keep, pass_on, lower, upper, to_near = out[len(items) :]
    upper = permuted(upper, [(i, i ^ 1) for i in range(n // 2, n)])
    *filled, send, to_near = place(plan, stay, (pass_on, to_near, across(lower, 1), upper))
    terms = (keep, across(send, 2), across(to_near, 1))
    bit = 4
    while bit < n:
        total = sum(term.astype(jnp.float32) for term in terms)
        terms = (total[0::2], across(total[1::2].astype(jnp.bfloat16), bit))
        bit *= 2
    terms = [term.reshape(rows, 2 * width) for term in terms]
    attended, query_grad, key_grad, value_grad = place(plan, late, terms, filled, final=True)
    return (
        attended.reshape(rows, heads, width),
        query_grad.reshape(rows, heads, width),
        key_grad.reshape(rows, 1, width),
        value_grad.reshape(rows, 1, width),
    )


def solution(mesh):
    rows = P(("dp", "ctx"), "tp", None)
    return jax.shard_map(
        on_device,
        mesh=mesh,
        in_specs=(rows, rows, rows, rows, P("dp"), P("dp", None)),
        out_specs=(rows, rows, rows, rows),
        check_vma=False,
    )
```

```python
import functools
import jax
import jax.numpy as jnp
from jax import lax
from jax.experimental import pallas as pl
from jax.experimental.pallas import tpu as pltpu
from jax.sharding import PartitionSpec as P

MASKED = -1e30
LOG2_E = 1.4426950408889634
VMEM_LIMIT = 32 * 1024 * 1024


def dot(a, b, contract):
    return lax.dot_general(a, b, ((contract[0], contract[1]), ((), ())), preferred_element_type=jnp.float32)


def attend_block(first_row, ends, q, g, k, v, reach, heads, scale):
    cols = q.shape[0]
    key_rows = k.shape[0]
    token = lax.broadcasted_iota(jnp.int32, (1, cols), 1) // heads
    query_pos = first_row + token
    doc_start = jnp.zeros((1, cols), jnp.int32)
    for end in ends:
        doc_start = jnp.maximum(doc_start, jnp.where(end <= query_pos, end, 0))
    low = doc_start - (first_row - reach)
    raw = dot(k, q, ((1,), (1,)))
    index = lax.broadcasted_iota(jnp.int32, (key_rows, cols), 0)
    allowed = index >= low
    allowed_late = jnp.logical_and(allowed[reach:], index[reach:] - reach <= token)
    raw = jnp.concatenate(
        [jnp.where(allowed[:reach], raw[:reach], MASKED), jnp.where(allowed_late, raw[reach:], MASKED)], axis=0
    )
    row_max = jnp.max(raw, axis=0, keepdims=True)
    weights = jnp.exp2((raw - row_max) * (scale * LOG2_E))
    inverse = 1.0 / jnp.sum(weights, axis=0, keepdims=True)
    attended_t = (dot(v, weights.astype(jnp.bfloat16), ((0,), (0,))) * inverse).astype(jnp.bfloat16)
    attended = attended_t.T
    g_t = g.T.astype(jnp.float32)
    delta = jnp.sum(g_t * attended_t.astype(jnp.float32), axis=0, keepdims=True)
    probs = weights * inverse
    products = dot(v, g, ((1,), (1,)))
    slopes = (probs * (products - delta)).astype(jnp.bfloat16)
    value_part = dot(probs.astype(jnp.bfloat16), g, ((1,), (0,)))
    key_part = dot(slopes, q, ((1,), (0,))) * scale
    query_grad = (dot(k, slopes, ((0,), (0,))) * scale).astype(jnp.bfloat16).T
    return attended, query_grad, key_part, value_part


class Plan:
    def __init__(self, n, rows, heads, width, ndocs):
        self.n, self.rows, self.heads, self.width, self.ndocs = n, rows, heads, width, ndocs
        self.back = n // 2
        self.block = rows // n
        self.cols = self.block * heads
        self.reach = self.back * rows
        self.scale = width ** (-0.5)
        self.window_ranges = self.back + 1

    def ends(self, meta):
        return [meta[1 + i] for i in range(self.ndocs)]

    def slot(self, meta, loader, owner):
        return meta[1 + self.ndocs + loader * self.n + owner]

    def cost(self, blocks):
        return pl.CostEstimate(
            flops=14 * blocks * self.cols * (self.reach + self.block) * self.width * 8,
            bytes_accessed=blocks * self.cols * self.width * 16,
            transcendentals=blocks * self.cols * (self.reach + self.block),
        )


def fill_window(plan, refs, k_win, v_win):
    rows = plan.rows
    k_win[pl.ds(plan.back * rows, rows), :] = refs[0][pl.ds(0, rows), :]
    v_win[pl.ds(plan.back * rows, rows), :] = refs[0][pl.ds(rows, rows), :]
    for i in range(1, plan.back + 1):
        to = pl.ds((plan.back - i) * rows, rows)
        k_win[to, :] = refs[2 * i - 1][...]
        v_win[to, :] = refs[2 * i][...]


def attend_at(plan, meta, loader, slot, q, g, k_win, v_win):
    start = (loader - meta[0]) * plan.rows + slot * plan.block
    keys_here = pl.ds(pl.multiple_of(start, plan.block), plan.reach + plan.block)
    out = attend_block(
        loader * plan.rows + slot * plan.block, plan.ends(meta), q, g, k_win[keys_here, :], v_win[keys_here, :],
        plan.reach, plan.heads, plan.scale,
    )
    return keys_here, out


def pack_kernel(plan, meta, q_ref, g_ref, k_ref, v_ref, *refs):
    blocks, (kv, sems, kv_sems) = refs[: plan.n], refs[plan.n :]
    own = meta[0]
    copies = []
    for apart, block in enumerate(blocks):
        slot = plan.slot(meta, own, own ^ apart)
        at = pl.ds(pl.multiple_of(slot * plan.cols, plan.cols), plan.cols)
        copies.append(pltpu.make_async_copy(q_ref.at[at, :], block.at[0], sems.at[apart, 0]))
        copies.append(pltpu.make_async_copy(g_ref.at[at, :], block.at[1], sems.at[apart, 1]))
    for i, ref in enumerate((k_ref, v_ref)):
        to = kv.at[pl.ds(i * plan.rows, plan.rows), :]
        copies.append(pltpu.make_async_copy(ref, to, kv_sems.at[i]))
    for copy in copies:
        copy.start()
    for copy in copies:
        copy.wait()


def first_kernel(plan, entries, meta, *refs):
    count = len(entries)
    qg_refs, kv_refs = refs[:count], refs[count : -2 * count - 2]
    pay_refs, grad_refs, (k_win, v_win) = refs[-2 * count - 2 : -count - 2], refs[-count - 2 : -2], refs[-2:]
    own = meta[0]
    fill_window(plan, kv_refs, k_win, v_win)
    for apart, qg, pay_ref, grad_ref in zip(entries, qg_refs, pay_refs, grad_refs):
        slot = plan.slot(meta, own, own ^ apart)
        _, (attended, query_grad, key_part, value_part) = attend_at(
            plan, meta, own, slot, qg[0], qg[1], k_win, v_win
        )
        pay_ref[0] = attended
        pay_ref[1] = query_grad
        grad_ref[:, : plan.width] = key_part
        grad_ref[:, plan.width :] = value_part


def last_kernel(plan, done, items, meta, *refs):
    n, width, rows, block = plan.n, plan.width, plan.rows, plan.block
    qg_refs, refs = refs[: len(items)], refs[len(items) :]
    done_refs, refs = refs[: len(done)], refs[len(done) :]
    kv_refs, refs = refs[: -(len(items) + 8)], refs[-(len(items) + 8) :]
    pay_refs, grad_refs, (k_win, v_win, acc) = refs[: len(items)], refs[len(items) : -3], refs[-3:]
    step = pl.program_id(0)
    own = meta[0]

    @pl.when(step == 0)
    def _():
        fill_window(plan, kv_refs, k_win, v_win)
        acc[...] = jnp.zeros_like(acc)
        for x, grad_ref in zip(done, done_refs):
            slot = plan.slot(meta, own, own ^ x)
            keys_here = pl.ds(pl.multiple_of(slot * block, block), plan.reach + block)
            acc[keys_here, :] = acc[keys_here, :] + grad_ref[...]

    for i, item in enumerate(items):

        @pl.when(step == i)
        def _():
            slot = plan.slot(meta, own, own ^ item)
            qg = qg_refs[i]
            keys_here, (attended, query_grad, key_part, value_part) = attend_at(
                plan, meta, own, slot, qg[0], qg[1], k_win, v_win
            )
            acc[keys_here, :width] = acc[keys_here, :width] + key_part
            acc[keys_here, width:] = acc[keys_here, width:] + value_part
            pay_refs[i][0] = attended
            pay_refs[i][1] = query_grad

    @pl.when(step == len(items) - 1)
    def _():
        def of_range(key_range, carry):
            at = lax.rem(key_range - own + plan.back + n, n) * rows
            for apart in range(n):
                slot = plan.slot(meta, key_range, own ^ apart)
                part = acc[pl.ds(pl.multiple_of(at + slot * block, block), block), :]
                entry = apart // 4
                if apart % 4 == 3:

                    @pl.when(key_range < n // 2)
                    def _():
                        grad_refs[2][entry, key_range] = part.astype(jnp.bfloat16)

                    @pl.when(key_range >= n // 2)
                    def _():
                        grad_refs[3][entry, key_range - n // 2] = part.astype(jnp.bfloat16)
                else:
                    to = grad_refs[(0, 4, 1)[apart % 4]]
                    to[entry, key_range] = part.astype(to.dtype)
            return carry

        lax.fori_loop(0, n, of_range, 0)


def spec_of(space):
    return pl.BlockSpec(memory_space=space)


def kernel_call(body, name, operands, spaces, out_shape, scratch, **more):
    return pl.pallas_call(
        body,
        out_shape=out_shape,
        in_specs=[spec_of(space) for space in spaces],
        compiler_params=pltpu.CompilerParams(vmem_limit_bytes=VMEM_LIMIT),
        scratch_shapes=scratch,
        name=name,
        **more,
    )(*operands)


def pack(plan, meta, *operands):
    out_shape = [jax.ShapeDtypeStruct((2, plan.cols, plan.width), jnp.bfloat16)] * plan.n
    out_shape.append(jax.ShapeDtypeStruct((2 * plan.rows, plan.width), jnp.bfloat16))
    operands = [pltpu.with_memory_space_constraint(x, pltpu.HBM) for x in operands]
    return kernel_call(
        functools.partial(pack_kernel, plan), "pack", (meta, *operands), [pltpu.SMEM] + [pl.ANY] * 4, out_shape,
        [pltpu.SemaphoreType.DMA((plan.n, 2)), pltpu.SemaphoreType.DMA((2,))],
        out_specs=[spec_of(pltpu.VMEM)] * len(out_shape),
    )


def attend_first(plan, entries, meta, qg_list, kv_list):
    window = pltpu.VMEM((plan.window_ranges * plan.rows, plan.width), jnp.bfloat16)
    rows = jax.ShapeDtypeStruct((2, plan.cols, plan.width), jnp.bfloat16)
    grad = jax.ShapeDtypeStruct((plan.reach + plan.block, 2 * plan.width), jnp.float32)
    out_shape = [rows] * len(entries) + [grad] * len(entries)
    operands = (meta, *qg_list, *kv_list)
    return kernel_call(
        functools.partial(first_kernel, plan, entries), f"attend_{entries[0]}", operands,
        [pltpu.SMEM] + [pltpu.VMEM] * (len(operands) - 1), out_shape, [window, window],
        out_specs=[spec_of(pltpu.VMEM)] * len(out_shape), cost_estimate=plan.cost(len(entries)),
    )


def attend_last(plan, done, items, meta, qg_list, done_grads, kv_list):
    n = plan.n
    window = pltpu.VMEM((plan.window_ranges * plan.rows, plan.width), jnp.bfloat16)
    keep = jax.ShapeDtypeStruct((n // 4, n, plan.block, 2 * plan.width), jnp.float32)
    send = jax.ShapeDtypeStruct((n // 4, n // 2, plan.block, 2 * plan.width), jnp.bfloat16)
    near = jax.ShapeDtypeStruct(keep.shape, jnp.bfloat16)
    out_shape = [jax.ShapeDtypeStruct((2, plan.cols, plan.width), jnp.bfloat16)] * len(items)
    out_shape += [keep, keep, send, send, near]
    operands = (meta, *qg_list, *done_grads, *kv_list)
    return kernel_call(
        functools.partial(last_kernel, plan, done, items), "attend_last", operands,
        [pltpu.SMEM] + [pltpu.VMEM] * (len(operands) - 1), out_shape,
        [window, window, pltpu.VMEM((n * plan.rows, 2 * plan.width), jnp.float32)],
        out_specs=[spec_of(pltpu.VMEM)] * len(out_shape), cost_estimate=plan.cost(len(items)), grid=(len(items),),
    )


def place_kernel(plan, items, ngrads, final, *refs):
    n, cols, width = plan.n, plan.cols, plan.width
    own = lax.axis_index("ctx")
    pay_refs, refs = refs[: len(items)], refs[len(items) :]
    if final:
        grads, (_, _, attended, query_grad, key_grad, value_grad, sums, sems, sum_sems) = refs[:-9], refs[-9:]
    elif ngrads:
        (pass_on, to_near, *arrived), (_, _, attended, query_grad, send, near, sems) = refs[:-7], refs[-7:]
    else:
        attended, query_grad, sems = refs
    copies = []
    for i, item in enumerate(items):
        to = pl.ds(pl.multiple_of((own ^ item) * cols, cols), cols)
        copies.append(pltpu.make_async_copy(pay_refs[i].at[0], attended.at[to, :], sems.at[i, 0]))
        copies.append(pltpu.make_async_copy(pay_refs[i].at[1], query_grad.at[to, :], sems.at[i, 1]))
    for copy in copies:
        copy.start()
    if final:
        total = sum(grad[...].astype(jnp.float32) for grad in grads).astype(jnp.bfloat16)
        sums[0] = total[:, :width]
        sums[1] = total[:, width:]
        for i, ref in enumerate((key_grad, value_grad)):
            copies.append(pltpu.make_async_copy(sums.at[i], ref, sum_sems.at[i]))
            copies[-1].start()
    elif ngrads:
        near[...] = to_near[...]
        for half, ref in enumerate(arrived):
            ranges = pl.ds(half * (n // 2), n // 2)
            send[:, ranges] = (pass_on[:, ranges] + ref[...].astype(jnp.float32)).astype(jnp.bfloat16)
    for copy in copies:
        copy.wait()


def place(plan, payloads, grads, filled=(), final=False):
    items = tuple(payloads)
    out_shape = [jax.ShapeDtypeStruct((plan.rows * plan.heads, plan.width), jnp.bfloat16)] * 2
    out_specs = [spec_of(pl.ANY)] * 2
    scratch = [pltpu.SemaphoreType.DMA((len(items), 2))]
    if final:
        out_shape += [jax.ShapeDtypeStruct((plan.rows, plan.width), jnp.bfloat16)] * 2
        out_specs += [spec_of(pl.ANY)] * 2
        scratch = [pltpu.VMEM((2, plan.rows, plan.width), jnp.bfloat16), *scratch, pltpu.SemaphoreType.DMA((2,))]
    elif grads:
        out_shape += [jax.ShapeDtypeStruct(grads[0].shape, jnp.bfloat16)] * 2
        out_specs += [spec_of(pltpu.VMEM)] * 2
    at = len(items) + len(grads)
    return kernel_call(
        functools.partial(place_kernel, plan, items, len(grads), final), "place_" + "_".join(map(str, items)),
        (*payloads.values(), *grads, *filled),
        [pl.ANY] * len(items) + [pltpu.VMEM] * len(grads) + [pl.ANY] * len(filled),
        out_shape, scratch, out_specs=out_specs, input_output_aliases={at: 0, at + 1: 1} if filled else {},
        cost_estimate=plan.cost(len(items)),
    )


def on_device(query, keys, values, output_gradient, doc_lengths, block_owner):
    n = lax.axis_size("ctx")
    own = lax.axis_index("ctx")
    rows, heads, width = query.shape
    plan = Plan(n, rows, heads, width, doc_lengths.shape[0])

    def permuted(array, pairs):
        return lax.ppermute(array, "ctx", pairs)

    def across(array, bits):
        return permuted(array, [(i, i ^ bits) for i in range(n)])

    k = keys.reshape(rows, width)
    v = values.reshape(rows, width)
    kv_list = []
    for by in range(1, plan.back + 1):
        pairs = [(i, (i + by) % n) for i in range(n)]
        kv_list += [permuted(k, pairs), permuted(v, pairs)]

    owners = jnp.arange(n, dtype=jnp.int32)
    match = block_owner[:, None, :] == owners[None, :, None]
    table = jnp.sum(jnp.where(match, owners, 0), axis=2)
    meta = jnp.concatenate(
        [own.reshape(1).astype(jnp.int32), jnp.cumsum(doc_lengths).astype(jnp.int32), table.reshape(-1)]
    )

    q, g = (x.reshape(rows * heads, width) for x in (query, output_gradient))
    *blocks, kv = pack(plan, meta, q, g, k, v)
    kv_list = [kv, *kv_list]
    first = (n // 2, 1)
    pays, grads = {}, []
    for x in first:
        pay, grad = attend_first(plan, (x,), meta, [blocks[x]], kv_list)
        pays[x] = across(pay, x)
        grads.append(grad)
    sent = [x for x in range(1, n) if x not in first]
    items = (*sent, 0)
    out = attend_last(plan, first, items, meta, [blocks[x] for x in items], grads, kv_list)
    late = {x: across(pay, x) for x, pay in zip(sent, out)}
    stay = {0: out[len(sent)]}
    keep, pass_on, lower, upper, to_near = out[len(items) :]
    upper = permuted(upper, [(i, i ^ 1) for i in range(n // 2, n)])
    filled = place(plan, pays, ())
    *filled, send, to_near = place(plan, stay, (pass_on, to_near, across(lower, 1), upper), filled)
    terms = (keep, across(send, 2), across(to_near, 1))
    bit = 4
    while bit < n:
        total = sum(term.astype(jnp.float32) for term in terms)
        terms = (total[0::2], across(total[1::2].astype(jnp.bfloat16), bit))
        bit *= 2
    terms = [term.reshape(rows, 2 * width) for term in terms]
    attended, query_grad, key_grad, value_grad = place(plan, late, terms, filled, final=True)
    return (
        attended.reshape(rows, heads, width),
        query_grad.reshape(rows, heads, width),
        key_grad.reshape(rows, 1, width),
        value_grad.reshape(rows, 1, width),
    )


def solution(mesh):
    rows = P(("dp", "ctx"), "tp", None)
    return jax.shard_map(
        on_device,
        mesh=mesh,
        in_specs=(rows, rows, rows, rows, P("dp"), P("dp", None)),
        out_specs=(rows, rows, rows, rows),
        check_vma=False,
    )
```

```python
import functools
import jax
import jax.numpy as jnp
from jax import lax
from jax.experimental import pallas as pl
from jax.experimental.pallas import tpu as pltpu
from jax.sharding import PartitionSpec as P

MASKED = -1e30
LOG2_E = 1.4426950408889634
VMEM_LIMIT = 32 * 1024 * 1024


def dot(a, b, contract):
    return lax.dot_general(a, b, ((contract[0], contract[1]), ((), ())), preferred_element_type=jnp.float32)


def attend_block(first_row, ends, q, g, k, v, reach, heads, scale):
    cols = q.shape[0]
    key_rows = k.shape[0]
    token = lax.broadcasted_iota(jnp.int32, (1, cols), 1) // heads
    query_pos = first_row + token
    doc_start = jnp.zeros((1, cols), jnp.int32)
    for end in ends:
        doc_start = jnp.maximum(doc_start, jnp.where(end <= query_pos, end, 0))
    low = doc_start - (first_row - reach)
    raw = dot(k, q, ((1,), (1,)))
    index = lax.broadcasted_iota(jnp.int32, (key_rows, cols), 0)
    allowed = index >= low
    allowed_late = jnp.logical_and(allowed[reach:], index[reach:] - reach <= token)
    raw = jnp.concatenate(
        [jnp.where(allowed[:reach], raw[:reach], MASKED), jnp.where(allowed_late, raw[reach:], MASKED)], axis=0
    )
    row_max = jnp.max(raw, axis=0, keepdims=True)
    weights = jnp.exp2((raw - row_max) * (scale * LOG2_E))
    inverse = 1.0 / jnp.sum(weights, axis=0, keepdims=True)
    attended_t = (dot(v, weights.astype(jnp.bfloat16), ((0,), (0,))) * inverse).astype(jnp.bfloat16)
    attended = attended_t.T
    g_t = g.T.astype(jnp.float32)
    delta = jnp.sum(g_t * attended_t.astype(jnp.float32), axis=0, keepdims=True)
    probs = weights * inverse
    products = dot(v, g, ((1,), (1,)))
    slopes = (probs * (products - delta)).astype(jnp.bfloat16)
    value_part = dot(probs.astype(jnp.bfloat16), g, ((1,), (0,)))
    key_part = dot(slopes, q, ((1,), (0,))) * scale
    query_grad = (dot(k, slopes, ((0,), (0,))) * scale).astype(jnp.bfloat16).T
    return attended, query_grad, key_part, value_part


class Plan:
    def __init__(self, n, rows, heads, width, ndocs):
        self.n, self.rows, self.heads, self.width, self.ndocs = n, rows, heads, width, ndocs
        self.back = n // 2
        self.block = rows // n
        self.cols = self.block * heads
        self.reach = self.back * rows
        self.scale = width ** (-0.5)
        self.window_ranges = self.back + 1

    def ends(self, meta):
        return [meta[1 + i] for i in range(self.ndocs)]

    def slot(self, meta, loader, owner):
        return meta[1 + self.ndocs + loader * self.n + owner]

    def cost(self, blocks):
        return pl.CostEstimate(
            flops=14 * blocks * self.cols * (self.reach + self.block) * self.width * 8,
            bytes_accessed=blocks * self.cols * self.width * 16,
            transcendentals=blocks * self.cols * (self.reach + self.block),
        )


def fill_window(plan, refs, k_win, v_win):
    rows = plan.rows
    k_win[pl.ds(plan.back * rows, rows), :] = refs[0][pl.ds(0, rows), :]
    v_win[pl.ds(plan.back * rows, rows), :] = refs[0][pl.ds(rows, rows), :]
    for i in range(1, plan.back + 1):
        to = pl.ds((plan.back - i) * rows, rows)
        k_win[to, :] = refs[2 * i - 1][...]
        v_win[to, :] = refs[2 * i][...]


def attend_at(plan, meta, loader, slot, q, g, k_win, v_win):
    start = (loader - meta[0]) * plan.rows + slot * plan.block
    keys_here = pl.ds(pl.multiple_of(start, plan.block), plan.reach + plan.block)
    out = attend_block(
        loader * plan.rows + slot * plan.block, plan.ends(meta), q, g, k_win[keys_here, :], v_win[keys_here, :],
        plan.reach, plan.heads, plan.scale,
    )
    return keys_here, out


def pack_kernel(plan, meta, q_ref, g_ref, k_ref, v_ref, *refs):
    blocks, (kv, sems, kv_sems) = refs[: plan.n], refs[plan.n :]
    own = meta[0]
    copies = []
    for apart, block in enumerate(blocks):
        slot = plan.slot(meta, own, own ^ apart)
        at = pl.ds(pl.multiple_of(slot * plan.cols, plan.cols), plan.cols)
        copies.append(pltpu.make_async_copy(q_ref.at[at, :], block.at[0], sems.at[apart, 0]))
        copies.append(pltpu.make_async_copy(g_ref.at[at, :], block.at[1], sems.at[apart, 1]))
    for i, ref in enumerate((k_ref, v_ref)):
        to = kv.at[pl.ds(i * plan.rows, plan.rows), :]
        copies.append(pltpu.make_async_copy(ref, to, kv_sems.at[i]))
    for copy in copies:
        copy.start()
    for copy in copies:
        copy.wait()


def first_kernel(plan, entries, meta, *refs):
    count = len(entries)
    qg_refs, kv_refs = refs[:count], refs[count : -2 * count - 2]
    pay_refs, grad_refs, (k_win, v_win) = refs[-2 * count - 2 : -count - 2], refs[-count - 2 : -2], refs[-2:]
    own = meta[0]
    fill_window(plan, kv_refs, k_win, v_win)
    for apart, qg, pay_ref, grad_ref in zip(entries, qg_refs, pay_refs, grad_refs):
        slot = plan.slot(meta, own, own ^ apart)
        _, (attended, query_grad, key_part, value_part) = attend_at(
            plan, meta, own, slot, qg[0], qg[1], k_win, v_win
        )
        pay_ref[0] = attended
        pay_ref[1] = query_grad
        grad_ref[:, : plan.width] = key_part
        grad_ref[:, plan.width :] = value_part


def last_kernel(plan, done, items, meta, *refs):
    n, width, rows, block = plan.n, plan.width, plan.rows, plan.block
    qg_refs, refs = refs[: len(items)], refs[len(items) :]
    done_refs, refs = refs[: len(done)], refs[len(done) :]
    kv_refs, refs = refs[: -(len(items) + 8)], refs[-(len(items) + 8) :]
    pay_refs, grad_refs, (k_win, v_win, acc) = refs[: len(items)], refs[len(items) : -3], refs[-3:]
    step = pl.program_id(0)
    own = meta[0]

    @pl.when(step == 0)
    def _():
        fill_window(plan, kv_refs, k_win, v_win)
        acc[...] = jnp.zeros_like(acc)
        for x, grad_ref in zip(done, done_refs):
            slot = plan.slot(meta, own, own ^ x)
            keys_here = pl.ds(pl.multiple_of(slot * block, block), plan.reach + block)
            acc[keys_here, :] = acc[keys_here, :] + grad_ref[...]

    for i, item in enumerate(items):

        @pl.when(step == i)
        def _():
            slot = plan.slot(meta, own, own ^ item)
            qg = qg_refs[i]
            keys_here, (attended, query_grad, key_part, value_part) = attend_at(
                plan, meta, own, slot, qg[0], qg[1], k_win, v_win
            )
            acc[keys_here, :width] = acc[keys_here, :width] + key_part
            acc[keys_here, width:] = acc[keys_here, width:] + value_part
            pay_refs[i][0] = attended
            pay_refs[i][1] = query_grad

    @pl.when(step == len(items) - 1)
    def _():
        def of_range(key_range, carry):
            at = lax.rem(key_range - own + plan.back + n, n) * rows
            for apart in range(n):
                slot = plan.slot(meta, key_range, own ^ apart)
                part = acc[pl.ds(pl.multiple_of(at + slot * block, block), block), :]
                entry = apart // 4
                if apart % 4 == 3:

                    @pl.when(key_range < n // 2)
                    def _():
                        grad_refs[2][entry, key_range] = part.astype(jnp.bfloat16)

                    @pl.when(key_range >= n // 2)
                    def _():
                        grad_refs[3][entry, key_range - n // 2] = part.astype(jnp.bfloat16)
                else:
                    to = grad_refs[(0, 4, 1)[apart % 4]]
                    to[entry, key_range] = part.astype(to.dtype)
            return carry

        lax.fori_loop(0, n, of_range, 0)


def spec_of(space):
    return pl.BlockSpec(memory_space=space)


def kernel_call(body, name, operands, spaces, out_shape, scratch, **more):
    return pl.pallas_call(
        body,
        out_shape=out_shape,
        in_specs=[spec_of(space) for space in spaces],
        compiler_params=pltpu.CompilerParams(vmem_limit_bytes=VMEM_LIMIT),
        scratch_shapes=scratch,
        name=name,
        **more,
    )(*operands)


def pack(plan, meta, *operands):
    out_shape = [jax.ShapeDtypeStruct((2, plan.cols, plan.width), jnp.bfloat16)] * plan.n
    out_shape.append(jax.ShapeDtypeStruct((2 * plan.rows, plan.width), jnp.bfloat16))
    operands = [pltpu.with_memory_space_constraint(x, pltpu.HBM) for x in operands]
    return kernel_call(
        functools.partial(pack_kernel, plan), "pack", (meta, *operands), [pltpu.SMEM] + [pl.ANY] * 4, out_shape,
        [pltpu.SemaphoreType.DMA((plan.n, 2)), pltpu.SemaphoreType.DMA((2,))],
        out_specs=[spec_of(pltpu.VMEM)] * len(out_shape),
    )


def attend_first(plan, entries, meta, qg_list, kv_list):
    window = pltpu.VMEM((plan.window_ranges * plan.rows, plan.width), jnp.bfloat16)
    rows = jax.ShapeDtypeStruct((2, plan.cols, plan.width), jnp.bfloat16)
    grad = jax.ShapeDtypeStruct((plan.reach + plan.block, 2 * plan.width), jnp.float32)
    out_shape = [rows] * len(entries) + [grad] * len(entries)
    operands = (meta, *qg_list, *kv_list)
    return kernel_call(
        functools.partial(first_kernel, plan, entries), f"attend_{entries[0]}", operands,
        [pltpu.SMEM] + [pltpu.VMEM] * (len(operands) - 1), out_shape, [window, window],
        out_specs=[spec_of(pltpu.VMEM)] * len(out_shape), cost_estimate=plan.cost(len(entries)),
    )


def attend_last(plan, done, items, meta, qg_list, done_grads, kv_list):
    n = plan.n
    window = pltpu.VMEM((plan.window_ranges * plan.rows, plan.width), jnp.bfloat16)
    keep = jax.ShapeDtypeStruct((n // 4, n, plan.block, 2 * plan.width), jnp.float32)
    send = jax.ShapeDtypeStruct((n // 4, n // 2, plan.block, 2 * plan.width), jnp.bfloat16)
    near = jax.ShapeDtypeStruct(keep.shape, jnp.bfloat16)
    out_shape = [jax.ShapeDtypeStruct((2, plan.cols, plan.width), jnp.bfloat16)] * len(items)
    out_shape += [keep, keep, send, send, near]
    operands = (meta, *qg_list, *done_grads, *kv_list)
    return kernel_call(
        functools.partial(last_kernel, plan, done, items), "attend_last", operands,
        [pltpu.SMEM] + [pltpu.VMEM] * (len(operands) - 1), out_shape,
        [window, window, pltpu.VMEM((n * plan.rows, 2 * plan.width), jnp.float32)],
        out_specs=[spec_of(pltpu.VMEM)] * len(out_shape), cost_estimate=plan.cost(4 * len(items)), grid=(len(items),),
    )


def fold_kernel(plan, pass_on, to_near, lower, upper, send, near):
    near[...] = to_near[...]
    for half, ref in enumerate((lower, upper)):
        ranges = pl.ds(half * (plan.n // 2), plan.n // 2)
        send[:, ranges] = (pass_on[:, ranges] + ref[...].astype(jnp.float32)).astype(jnp.bfloat16)


def fold(plan, *operands):
    out_shape = [jax.ShapeDtypeStruct(operands[1].shape, jnp.bfloat16)] * 2
    return kernel_call(
        functools.partial(fold_kernel, plan), "fold", operands, [pltpu.VMEM] * 4, out_shape, [],
        out_specs=[spec_of(pltpu.VMEM)] * 2,
        cost_estimate=pl.CostEstimate(flops=0, bytes_accessed=1024, transcendentals=0),
    )


def place_kernel(plan, items, final, *refs):
    n, cols, width = plan.n, plan.cols, plan.width
    own = lax.axis_index("ctx")
    pay_refs, refs = refs[: len(items)], refs[len(items) :]
    if final:
        grads, (_, _, attended, query_grad, key_grad, value_grad, sums, sems, sum_sems) = refs[:-9], refs[-9:]
    else:
        attended, query_grad, sems = refs
    copies = []
    for i, item in enumerate(items):
        to = pl.ds(pl.multiple_of((own ^ item) * cols, cols), cols)
        copies.append(pltpu.make_async_copy(pay_refs[i].at[0], attended.at[to, :], sems.at[i, 0]))
        copies.append(pltpu.make_async_copy(pay_refs[i].at[1], query_grad.at[to, :], sems.at[i, 1]))
    for copy in copies:
        copy.start()
    if final:
        total = sum(grad[...].astype(jnp.float32) for grad in grads).astype(jnp.bfloat16)
        sums[0] = total[:, :width]
        sums[1] = total[:, width:]
        for i, ref in enumerate((key_grad, value_grad)):
            copies.append(pltpu.make_async_copy(sums.at[i], ref, sum_sems.at[i]))
            copies[-1].start()
    for copy in copies:
        copy.wait()


def place(plan, payloads, grads, filled=(), final=False):
    items = tuple(payloads)
    out_shape = [jax.ShapeDtypeStruct((plan.rows * plan.heads, plan.width), jnp.bfloat16)] * 2
    out_specs = [spec_of(pl.ANY)] * 2
    scratch = [pltpu.SemaphoreType.DMA((len(items), 2))]
    if final:
        out_shape += [jax.ShapeDtypeStruct((plan.rows, plan.width), jnp.bfloat16)] * 2
        out_specs += [spec_of(pl.ANY)] * 2
        scratch = [pltpu.VMEM((2, plan.rows, plan.width), jnp.bfloat16), *scratch, pltpu.SemaphoreType.DMA((2,))]
    at = len(items) + len(grads)
    return kernel_call(
        functools.partial(place_kernel, plan, items, final), "place_" + "_".join(map(str, items)),
        (*payloads.values(), *grads, *filled),
        [pl.ANY] * len(items) + [pltpu.VMEM] * len(grads) + [pl.ANY] * len(filled),
        out_shape, scratch, out_specs=out_specs, input_output_aliases={at: 0, at + 1: 1} if filled else {},
        cost_estimate=plan.cost(4 * len(items)),
    )


def on_device(query, keys, values, output_gradient, doc_lengths, block_owner):
    n = lax.axis_size("ctx")
    own = lax.axis_index("ctx")
    rows, heads, width = query.shape
    plan = Plan(n, rows, heads, width, doc_lengths.shape[0])

    def permuted(array, pairs):
        return lax.ppermute(array, "ctx", pairs)

    def across(array, bits):
        return permuted(array, [(i, i ^ bits) for i in range(n)])

    k = keys.reshape(rows, width)
    v = values.reshape(rows, width)
    kv_list = []
    for by in range(1, plan.back + 1):
        pairs = [(i, (i + by) % n) for i in range(n)]
        kv_list += [permuted(k, pairs), permuted(v, pairs)]

    owners = jnp.arange(n, dtype=jnp.int32)
    match = block_owner[:, None, :] == owners[None, :, None]
    table = jnp.sum(jnp.where(match, owners, 0), axis=2)
    meta = jnp.concatenate(
        [own.reshape(1).astype(jnp.int32), jnp.cumsum(doc_lengths).astype(jnp.int32), table.reshape(-1)]
    )

    q, g = (x.reshape(rows * heads, width) for x in (query, output_gradient))
    *blocks, kv = pack(plan, meta, q, g, k, v)
    kv_list = [kv, *kv_list]
    first = (n // 2, 1)
    pays, grads = {}, []
    for x in first:
        pay, grad = attend_first(plan, (x,), meta, [blocks[x]], kv_list)
        pays[x] = across(pay, x)
        grads.append(grad)
    sent = [x for x in range(1, n) if x not in first]
    items = (*sent, 0)
    out = attend_last(plan, first, items, meta, [blocks[x] for x in items], grads, kv_list)
    late = {x: across(pay, x) for x, pay in zip(sent, out)}
    pays[0] = out[len(sent)]
    keep, pass_on, lower, upper, to_near = out[len(items) :]
    upper = permuted(upper, [(i, i ^ 1) for i in range(n // 2, n)])
    send, to_near = fold(plan, pass_on, to_near, across(lower, 1), upper)
    filled = place(plan, pays, ())
    terms = (keep, across(send, 2), across(to_near, 1))
    bit = 4
    while bit < n:
        total = sum(term.astype(jnp.float32) for term in terms)
        terms = (total[0::2], across(total[1::2].astype(jnp.bfloat16), bit))
        bit *= 2
    terms = [term.reshape(rows, 2 * width) for term in terms]
    attended, query_grad, key_grad, value_grad = place(plan, late, terms, filled, final=True)
    return (
        attended.reshape(rows, heads, width),
        query_grad.reshape(rows, heads, width),
        key_grad.reshape(rows, 1, width),
        value_grad.reshape(rows, 1, width),
    )


def solution(mesh):
    rows = P(("dp", "ctx"), "tp", None)
    return jax.shard_map(
        on_device,
        mesh=mesh,
        in_specs=(rows, rows, rows, rows, P("dp"), P("dp", None)),
        out_specs=(rows, rows, rows, rows),
        check_vma=False,
    )
```

```python
import functools
import jax
import jax.numpy as jnp
from jax import lax
from jax.experimental import pallas as pl
from jax.experimental.pallas import tpu as pltpu
from jax.sharding import PartitionSpec as P

MASKED = -1e30
LOG2_E = 1.4426950408889634
VMEM_LIMIT = 32 * 1024 * 1024


def dot(a, b, contract):
    return lax.dot_general(a, b, ((contract[0], contract[1]), ((), ())), preferred_element_type=jnp.float32)


def attend_block(first_row, ends, q, g, k, v, reach, heads, scale):
    cols = q.shape[0]
    key_rows = k.shape[0]
    token = lax.broadcasted_iota(jnp.int32, (1, cols), 1) // heads
    query_pos = first_row + token
    doc_start = jnp.zeros((1, cols), jnp.int32)
    for end in ends:
        doc_start = jnp.maximum(doc_start, jnp.where(end <= query_pos, end, 0))
    low = doc_start - (first_row - reach)
    raw = dot(k, q, ((1,), (1,)))
    index = lax.broadcasted_iota(jnp.int32, (key_rows, cols), 0)
    allowed = index >= low
    allowed_late = jnp.logical_and(allowed[reach:], index[reach:] - reach <= token)
    raw = jnp.concatenate(
        [jnp.where(allowed[:reach], raw[:reach], MASKED), jnp.where(allowed_late, raw[reach:], MASKED)], axis=0
    )
    row_max = jnp.max(raw, axis=0, keepdims=True)
    weights = jnp.exp2((raw - row_max) * (scale * LOG2_E))
    inverse = 1.0 / jnp.sum(weights, axis=0, keepdims=True)
    attended_t = (dot(v, weights.astype(jnp.bfloat16), ((0,), (0,))) * inverse).astype(jnp.bfloat16)
    attended = attended_t.T
    g_t = g.T.astype(jnp.float32)
    delta = jnp.sum(g_t * attended_t.astype(jnp.float32), axis=0, keepdims=True)
    probs = weights * inverse
    products = dot(v, g, ((1,), (1,)))
    slopes = (probs * (products - delta)).astype(jnp.bfloat16)
    value_part = dot(probs.astype(jnp.bfloat16), g, ((1,), (0,)))
    key_part = dot(slopes, q, ((1,), (0,))) * scale
    query_grad = (dot(k, slopes, ((0,), (0,))) * scale).astype(jnp.bfloat16).T
    return attended, query_grad, key_part, value_part


class Plan:
    def __init__(self, n, rows, heads, width, ndocs):
        self.n, self.rows, self.heads, self.width, self.ndocs = n, rows, heads, width, ndocs
        self.back = n // 2
        self.block = rows // n
        self.cols = self.block * heads
        self.reach = self.back * rows
        self.scale = width ** (-0.5)
        self.window_ranges = self.back + 1

    def ends(self, meta):
        return [meta[1 + i] for i in range(self.ndocs)]

    def slot(self, meta, loader, owner):
        return meta[1 + self.ndocs + loader * self.n + owner]

    def cost(self, blocks):
        return pl.CostEstimate(
            flops=14 * blocks * self.cols * (self.reach + self.block) * self.width * 8,
            bytes_accessed=blocks * self.cols * self.width * 16,
            transcendentals=blocks * self.cols * (self.reach + self.block),
        )


def fill_window(plan, refs, k_win, v_win):
    rows = plan.rows
    k_win[pl.ds(plan.back * rows, rows), :] = refs[0][pl.ds(0, rows), :]
    v_win[pl.ds(plan.back * rows, rows), :] = refs[0][pl.ds(rows, rows), :]
    for i in range(1, plan.back + 1):
        to = pl.ds((plan.back - i) * rows, rows)
        k_win[to, :] = refs[2 * i - 1][...]
        v_win[to, :] = refs[2 * i][...]


def attend_at(plan, meta, loader, slot, q, g, k_win, v_win):
    start = (loader - meta[0]) * plan.rows + slot * plan.block
    keys_here = pl.ds(pl.multiple_of(start, plan.block), plan.reach + plan.block)
    out = attend_block(
        loader * plan.rows + slot * plan.block, plan.ends(meta), q, g, k_win[keys_here, :], v_win[keys_here, :],
        plan.reach, plan.heads, plan.scale,
    )
    return keys_here, out


def pack_kernel(plan, meta, q_ref, g_ref, k_ref, v_ref, *refs):
    blocks, (kv, sems, kv_sems) = refs[: plan.n], refs[plan.n :]
    own = meta[0]
    copies = []
    for apart, block in enumerate(blocks):
        slot = plan.slot(meta, own, own ^ apart)
        at = pl.ds(pl.multiple_of(slot * plan.cols, plan.cols), plan.cols)
        copies.append(pltpu.make_async_copy(q_ref.at[at, :], block.at[0], sems.at[apart, 0]))
        copies.append(pltpu.make_async_copy(g_ref.at[at, :], block.at[1], sems.at[apart, 1]))
    for i, ref in enumerate((k_ref, v_ref)):
        to = kv.at[pl.ds(i * plan.rows, plan.rows), :]
        copies.append(pltpu.make_async_copy(ref, to, kv_sems.at[i]))
    for copy in copies:
        copy.start()
    for copy in copies:
        copy.wait()


def first_kernel(plan, entries, meta, *refs):
    count = len(entries)
    qg_refs, kv_refs = refs[:count], refs[count : -2 * count - 2]
    pay_refs, grad_refs, (k_win, v_win) = refs[-2 * count - 2 : -count - 2], refs[-count - 2 : -2], refs[-2:]
    own = meta[0]
    fill_window(plan, kv_refs, k_win, v_win)
    for apart, qg, pay_ref, grad_ref in zip(entries, qg_refs, pay_refs, grad_refs):
        slot = plan.slot(meta, own, own ^ apart)
        _, (attended, query_grad, key_part, value_part) = attend_at(
            plan, meta, own, slot, qg[0], qg[1], k_win, v_win
        )
        pay_ref[0] = attended
        pay_ref[1] = query_grad
        grad_ref[:, : plan.width] = key_part
        grad_ref[:, plan.width :] = value_part


def last_kernel(plan, done, items, meta, *refs):
    n, width, rows, block = plan.n, plan.width, plan.rows, plan.block
    qg_refs, refs = refs[: len(items)], refs[len(items) :]
    done_refs, refs = refs[: len(done)], refs[len(done) :]
    kv_refs, refs = refs[: -(len(items) + 8)], refs[-(len(items) + 8) :]
    pay_refs, grad_refs, (k_win, v_win, acc) = refs[: len(items)], refs[len(items) : -3], refs[-3:]
    step = pl.program_id(0)
    own = meta[0]

    @pl.when(step == 0)
    def _():
        fill_window(plan, kv_refs, k_win, v_win)
        acc[...] = jnp.zeros_like(acc)
        for x, grad_ref in zip(done, done_refs):
            slot = plan.slot(meta, own, own ^ x)
            keys_here = pl.ds(pl.multiple_of(slot * block, block), plan.reach + block)
            acc[keys_here, :] = acc[keys_here, :] + grad_ref[...]

    for i, item in enumerate(items):

        @pl.when(step == i)
        def _():
            slot = plan.slot(meta, own, own ^ item)
            qg = qg_refs[i]
            keys_here, (attended, query_grad, key_part, value_part) = attend_at(
                plan, meta, own, slot, qg[0], qg[1], k_win, v_win
            )
            acc[keys_here, :width] = acc[keys_here, :width] + key_part
            acc[keys_here, width:] = acc[keys_here, width:] + value_part
            pay_refs[i][0] = attended
            pay_refs[i][1] = query_grad

    @pl.when(step == len(items) - 1)
    def _():
        def of_range(key_range, carry):
            at = lax.rem(key_range - own + plan.back + n, n) * rows
            for apart in range(n):
                slot = plan.slot(meta, key_range, own ^ apart)
                part = acc[pl.ds(pl.multiple_of(at + slot * block, block), block), :]
                entry = apart // 4
                if apart % 4 == 3:

                    @pl.when(key_range < n // 2)
                    def _():
                        grad_refs[2][entry, key_range] = part.astype(jnp.bfloat16)

                    @pl.when(key_range >= n // 2)
                    def _():
                        grad_refs[3][entry, key_range - n // 2] = part.astype(jnp.bfloat16)
                else:
                    to = grad_refs[(0, 4, 1)[apart % 4]]
                    to[entry, key_range] = part.astype(to.dtype)
            return carry

        lax.fori_loop(0, n, of_range, 0)


def spec_of(space):
    return pl.BlockSpec(memory_space=space)


def kernel_call(body, name, operands, spaces, out_shape, scratch, **more):
    return pl.pallas_call(
        body,
        out_shape=out_shape,
        in_specs=[spec_of(space) for space in spaces],
        compiler_params=pltpu.CompilerParams(vmem_limit_bytes=VMEM_LIMIT),
        scratch_shapes=scratch,
        name=name,
        **more,
    )(*operands)


def pack(plan, meta, *operands):
    out_shape = [jax.ShapeDtypeStruct((2, plan.cols, plan.width), jnp.bfloat16)] * plan.n
    out_shape.append(jax.ShapeDtypeStruct((2 * plan.rows, plan.width), jnp.bfloat16))
    operands = [pltpu.with_memory_space_constraint(x, pltpu.HBM) for x in operands]
    return kernel_call(
        functools.partial(pack_kernel, plan), "pack", (meta, *operands), [pltpu.SMEM] + [pl.ANY] * 4, out_shape,
        [pltpu.SemaphoreType.DMA((plan.n, 2)), pltpu.SemaphoreType.DMA((2,))],
        out_specs=[spec_of(pltpu.VMEM)] * len(out_shape),
    )


def attend_first(plan, entries, meta, qg_list, kv_list):
    window = pltpu.VMEM((plan.window_ranges * plan.rows, plan.width), jnp.bfloat16)
    rows = jax.ShapeDtypeStruct((2, plan.cols, plan.width), jnp.bfloat16)
    grad = jax.ShapeDtypeStruct((plan.reach + plan.block, 2 * plan.width), jnp.float32)
    out_shape = [rows] * len(entries) + [grad] * len(entries)
    operands = (meta, *qg_list, *kv_list)
    return kernel_call(
        functools.partial(first_kernel, plan, entries), f"attend_{entries[0]}", operands,
        [pltpu.SMEM] + [pltpu.VMEM] * (len(operands) - 1), out_shape, [window, window],
        out_specs=[spec_of(pltpu.VMEM)] * len(out_shape), cost_estimate=plan.cost(len(entries)),
    )


def attend_last(plan, done, items, meta, qg_list, done_grads, kv_list):
    n = plan.n
    window = pltpu.VMEM((plan.window_ranges * plan.rows, plan.width), jnp.bfloat16)
    keep = jax.ShapeDtypeStruct((n // 4, n, plan.block, 2 * plan.width), jnp.float32)
    send = jax.ShapeDtypeStruct((n // 4, n // 2, plan.block, 2 * plan.width), jnp.bfloat16)
    near = jax.ShapeDtypeStruct(keep.shape, jnp.bfloat16)
    out_shape = [jax.ShapeDtypeStruct((2, plan.cols, plan.width), jnp.bfloat16)] * len(items)
    out_shape += [keep, keep, send, send, near]
    operands = (meta, *qg_list, *done_grads, *kv_list)
    return kernel_call(
        functools.partial(last_kernel, plan, done, items), "attend_last", operands,
        [pltpu.SMEM] + [pltpu.VMEM] * (len(operands) - 1), out_shape,
        [window, window, pltpu.VMEM((n * plan.rows, 2 * plan.width), jnp.float32)],
        out_specs=[spec_of(pltpu.VMEM)] * len(out_shape), cost_estimate=plan.cost(4 * len(items)), grid=(len(items),),
    )


def fold_kernel(plan, pass_on, to_near, lower, upper, send, near):
    near[...] = to_near[...]
    for half, ref in enumerate((lower, upper)):
        ranges = pl.ds(half * (plan.n // 2), plan.n // 2)
        send[:, ranges] = (pass_on[:, ranges] + ref[...].astype(jnp.float32)).astype(jnp.bfloat16)


def fold(plan, *operands):
    out_shape = [jax.ShapeDtypeStruct(operands[1].shape, jnp.bfloat16)] * 2
    return kernel_call(
        functools.partial(fold_kernel, plan), "fold", operands, [pltpu.VMEM] * 4, out_shape, [],
        out_specs=[spec_of(pltpu.VMEM)] * 2,
        cost_estimate=pl.CostEstimate(flops=0, bytes_accessed=1024, transcendentals=0),
    )


def place_kernel(plan, items, final, *refs):
    n, cols, width = plan.n, plan.cols, plan.width
    own = lax.axis_index("ctx")
    pay_refs, refs = refs[: len(items)], refs[len(items) :]
    if final:
        grads, (_, _, attended, query_grad, key_grad, value_grad, sums, sems, sum_sems) = refs[:-9], refs[-9:]
    else:
        attended, query_grad, sems = refs
    copies = []
    for i, item in enumerate(items):
        to = pl.ds(pl.multiple_of((own ^ item) * cols, cols), cols)
        copies.append(pltpu.make_async_copy(pay_refs[i].at[0], attended.at[to, :], sems.at[i, 0]))
        copies.append(pltpu.make_async_copy(pay_refs[i].at[1], query_grad.at[to, :], sems.at[i, 1]))
    for copy in copies:
        copy.start()
    if final:
        total = sum(grad[...].astype(jnp.float32) for grad in grads).astype(jnp.bfloat16)
        sums[0] = total[:, :width]
        sums[1] = total[:, width:]
        for i, ref in enumerate((key_grad, value_grad)):
            copies.append(pltpu.make_async_copy(sums.at[i], ref, sum_sems.at[i]))
            copies[-1].start()
    for copy in copies:
        copy.wait()


def place(plan, payloads, grads, filled=(), final=False):
    items = tuple(payloads)
    out_shape = [jax.ShapeDtypeStruct((plan.rows * plan.heads, plan.width), jnp.bfloat16)] * 2
    out_specs = [spec_of(pl.ANY)] * 2
    scratch = [pltpu.SemaphoreType.DMA((len(items), 2))]
    if final:
        out_shape += [jax.ShapeDtypeStruct((plan.rows, plan.width), jnp.bfloat16)] * 2
        out_specs += [spec_of(pl.ANY)] * 2
        scratch = [pltpu.VMEM((2, plan.rows, plan.width), jnp.bfloat16), *scratch, pltpu.SemaphoreType.DMA((2,))]
    at = len(items) + len(grads)
    return kernel_call(
        functools.partial(place_kernel, plan, items, final), "place_" + "_".join(map(str, items)),
        (*payloads.values(), *grads, *filled),
        [pl.ANY] * len(items) + [pltpu.VMEM] * len(grads) + [pl.ANY] * len(filled),
        out_shape, scratch, out_specs=out_specs, input_output_aliases={at: 0, at + 1: 1} if filled else {},
        cost_estimate=plan.cost(4 * len(items)),
    )


def on_device(query, keys, values, output_gradient, doc_lengths, block_owner):
    n = lax.axis_size("ctx")
    own = lax.axis_index("ctx")
    rows, heads, width = query.shape
    plan = Plan(n, rows, heads, width, doc_lengths.shape[0])

    def permuted(array, pairs):
        return lax.ppermute(array, "ctx", pairs)

    def across(array, bits):
        return permuted(array, [(i, i ^ bits) for i in range(n)])

    k = keys.reshape(rows, width)
    v = values.reshape(rows, width)
    kv_list = []
    for by in range(1, plan.back + 1):
        pairs = [(i, (i + by) % n) for i in range(n)]
        kv_list += [permuted(k, pairs), permuted(v, pairs)]

    owners = jnp.arange(n, dtype=jnp.int32)
    match = block_owner[:, None, :] == owners[None, :, None]
    table = jnp.sum(jnp.where(match, owners, 0), axis=2)
    meta = jnp.concatenate(
        [own.reshape(1).astype(jnp.int32), jnp.cumsum(doc_lengths).astype(jnp.int32), table.reshape(-1)]
    )

    q, g = (x.reshape(rows * heads, width) for x in (query, output_gradient))
    *blocks, kv = pack(plan, meta, q, g, k, v)
    kv_list = [kv, *kv_list]
    first = (n // 2,)
    pays, grads = {}, []
    for x in first:
        pay, grad = attend_first(plan, (x,), meta, [blocks[x]], kv_list)
        pays[x] = across(pay, x)
        grads.append(grad)
    sent = [x for x in range(1, n) if x not in first]
    items = (*sent, 0)
    out = attend_last(plan, first, items, meta, [blocks[x] for x in items], grads, kv_list)
    late = {x: across(pay, x) for x, pay in zip(sent, out)}
    pays[0] = out[len(sent)]
    keep, pass_on, lower, upper, to_near = out[len(items) :]
    upper = permuted(upper, [(i, i ^ 1) for i in range(n // 2, n)])
    send, to_near = fold(plan, pass_on, to_near, across(lower, 1), upper)
    filled = place(plan, pays, ())
    terms = (keep, across(send, 2), across(to_near, 1))
    bit = 4
    while bit < n:
        total = sum(term.astype(jnp.float32) for term in terms)
        terms = (total[0::2], across(total[1::2].astype(jnp.bfloat16), bit))
        bit *= 2
    terms = [term.reshape(rows, 2 * width) for term in terms]
    attended, query_grad, key_grad, value_grad = place(plan, late, terms, filled, final=True)
    return (
        attended.reshape(rows, heads, width),
        query_grad.reshape(rows, heads, width),
        key_grad.reshape(rows, 1, width),
        value_grad.reshape(rows, 1, width),
    )


def solution(mesh):
    rows = P(("dp", "ctx"), "tp", None)
    return jax.shard_map(
        on_device,
        mesh=mesh,
        in_specs=(rows, rows, rows, rows, P("dp"), P("dp", None)),
        out_specs=(rows, rows, rows, rows),
        check_vma=False,
    )
```
